128 devices in a mesh: tensor: 8 (over z_hi, y), seq: 16 (over x, z_lo, core).
Axes of the slice: x: 4, y: 4, z: 4 (z_hi: 2, z_lo: 2; z = z_hi * 2 + z_lo), core: 2. Of those that a mesh axis runs over, the one named last changes fastest.
Arguments:
- inputs: bfloat16 [4096, 4096], P('seq', 'tensor'), may hold values from -60 to 60
- gain: bfloat16 [4096], P('tensor'), may hold values from 0.099609375 to 1.8984375
- weights: bfloat16 [4096, 3, 6144], P(None, None, 'tensor'), may hold values from -0.09375 to 0.09375
- d_out: bfloat16 [4096, 4096], P('seq', 'tensor'), may hold values from -18 to 18
Outputs:
- output: bfloat16 [4096, 4096], P('seq', 'tensor')
- d_input: bfloat16 [4096, 4096], P('seq', 'tensor')
- d_gain: float32 [4096], P('tensor')
- d_weights: bfloat16 [4096, 3, 6144], P('seq', None, 'tensor')
The draws below stay inside these ranges and needn't reach their ends.
All inputs are finite; a program needn't handle non-finite values.
Results may differ from the reference program's by a relative error of at most 0.018.
Values may be sent and summed in bfloat16 or wider, within the bound.
No kernel may reach another device: no remote copies, remote signals or barrier semaphores. Data moves between devices by JAX's collectives and lax.ppermute only.
A program may use at most 128 MiB of HBM per device.

```python
import math
import jax
import jax.numpy as jnp
from jax import lax

D = 4096
FF = 6144
TOK_DEV = 256
TOKENS = 4096
N_TENSOR = 8
N_SEQ = 16


def draw_inputs(key, part):
    key = jax.random.fold_in(key, 11)
    key_rows, key_cols, key_base = jax.random.split(key, 3)
    row_scale = jnp.exp(jax.random.uniform(key_rows, (TOKENS, 1), jnp.float32, 0.0, math.log(10.0)))
    col_scale = jnp.exp(jax.random.uniform(key_cols, (1, D), jnp.float32, 0.0, math.log(10.0)))
    base = jnp.clip(jax.random.normal(key_base, (TOKENS, D), jnp.float32), -6.0, 6.0)
    return (0.1 * base * row_scale * col_scale).astype(jnp.bfloat16)


def draw_d_out(key, part):
    key = jax.random.fold_in(key, 23)
    key_base = jax.random.fold_in(key, 0)
    position = jnp.arange(TOKENS, dtype=jnp.float32)[:, None] / (TOKENS - 1)
    rising = jnp.exp(position * math.log(3.0))
    base = jnp.clip(jax.random.normal(key_base, (TOKENS, D), jnp.float32), -6.0, 6.0)
    return (base * rising).astype(jnp.bfloat16)


def levels(key, shape, cuts, low, high):
    def one(axis_at, shards_of):
        heights = jax.random.uniform(jax.random.fold_in(jax.random.fold_in(key, 6), axis_at), (shards_of,), jnp.float32, low / len(cuts), high / len(cuts))
        return jnp.repeat(jnp.exp(heights), shape[axis_at] // shards_of).reshape((-1,) + (1,) * (len(shape) - axis_at - 1))

    loudness = one(*cuts[0])
    for cut in cuts[1:]:
        loudness = loudness * one(*cut)
    return loudness


def bell_draw(stream_key, extent, scale, limit, cuts=(), kind=jnp.bfloat16):
    factor_of = levels(stream_key, extent, cuts, -0.22, 0.18) if cuts else 1.0
    values = jax.random.normal(stream_key, extent, jnp.float32) * scale * factor_of
    return jnp.minimum(jnp.maximum(values, -limit), limit).astype(kind)


def setup_inputs(seed: int = 0) -> dict:
    keys = jax.random.split(jax.random.key(seed), 5)
    return {
        "inputs": draw_inputs(jax.random.fold_in(keys[4], 71), 0),
        "gain": jnp.clip(1.0 + 0.18 * jax.random.normal(keys[1], (D,), jnp.float32), 0.099609375, 1.8984375).astype(jnp.bfloat16),
        "weights": bell_draw(keys[2], (D, 3, FF), D ** -0.5, 0.09375, ((2, 8),)),
        "d_out": draw_d_out(jax.random.fold_in(keys[4], 71), 0),
    }


norm_eps = 1e-05

def reference(inputs, gain, weights, d_out):
    x_vals = inputs.astype(jnp.float32)
    inv_rms = lax.rsqrt(lax.optimization_barrier(jnp.mean(x_vals * x_vals, axis=1, keepdims=True)) + norm_eps)
    gain_vals = gain.astype(jnp.float32)
    normed = (x_vals * inv_rms * gain_vals).astype(jnp.bfloat16)
    gate = jnp.dot(normed, weights[:, 0, :], preferred_element_type=jnp.float32)
    up_val = jnp.dot(normed, weights[:, 1, :], preferred_element_type=jnp.float32)
    sigma = jax.nn.sigmoid(gate)
    hidden = (gate * sigma * up_val).astype(jnp.bfloat16)
    block = FF // N_TENSOR
    branch = jnp.zeros((TOKENS, D), jnp.float32)
    for index in range(N_TENSOR):
        part = lax.dot_general(hidden[:, index * block:(index + 1) * block], weights[:, 2, index * block:(index + 1) * block], (((1,), (1,)), ((), ())), preferred_element_type=jnp.float32)
        part = lax.optimization_barrier(part.astype(jnp.bfloat16))
        branch = branch + part.astype(jnp.float32)
    output = branch.astype(jnp.bfloat16)
    d_hidden = jnp.dot(d_out, weights[:, 2, :], preferred_element_type=jnp.float32)
    d_gate = (d_hidden * up_val * sigma * (1.0 + gate * (1.0 - sigma))).astype(jnp.bfloat16)
    d_up = (d_hidden * gate * sigma).astype(jnp.bfloat16)
    d_normed = jnp.dot(d_gate, weights[:, 0, :].T, preferred_element_type=jnp.float32) + jnp.dot(d_up, weights[:, 1, :].T, preferred_element_type=jnp.float32)
    products = lax.optimization_barrier(jnp.mean(d_normed * gain_vals * x_vals, axis=1, keepdims=True))
    d_input = (inv_rms * d_normed * gain_vals - inv_rms ** 3 * products * x_vals).astype(jnp.bfloat16)
    d_gain = lax.optimization_barrier(jnp.sum(d_normed * x_vals * inv_rms, axis=0))
    total = jnp.zeros((D, 3, FF), jnp.float32)
    for index in range(N_SEQ):
        lower = index * TOK_DEV
        upper = lower + TOK_DEV
        normed_b = normed[lower:upper]
        term_gate = jnp.dot(normed_b.T, d_gate[lower:upper], preferred_element_type=jnp.float32)
        term_up = jnp.dot(normed_b.T, d_up[lower:upper], preferred_element_type=jnp.float32)
        term_down = jnp.dot(d_out[lower:upper].T, hidden[lower:upper], preferred_element_type=jnp.float32)
        term = jnp.stack([term_gate, term_up, term_down], axis=1)
        term = lax.optimization_barrier(term.astype(jnp.bfloat16))
        total = total + term.astype(jnp.float32)
    d_weights = total.astype(jnp.bfloat16)
    return (output, d_input, d_gain, d_weights)
```

```python
import jax
import jax.numpy as jnp
from jax import lax
from jax.experimental import pallas as pl
from jax.experimental.pallas import tpu as pltpu
from jax.sharding import PartitionSpec as P

norm_eps = 1e-05
AXES = ("tensor", "seq")
f32 = jnp.float32
bf16 = jnp.bfloat16


def flat(x, y, z, c):
    x, y, z = x % 4, y % 4, z % 4
    return ((z // 2) * 4 + y) * 16 + (x * 2 + z % 2) * 2 + c


def pairs(move):
    places = [(x, y, z, c) for x in range(4) for y in range(4) for z in range(4) for c in range(2)]
    return [(flat(*place), flat(*move(*place))) for place in places]


moves = {
    "x^1": lambda x, y, z, c: (x ^ 1, y, z, c),
    "x^3": lambda x, y, z, c: (x ^ 3, y, z, c),
    "x+2": lambda x, y, z, c: (x + 2, y, z, c),
    "y+": lambda x, y, z, c: (x, y + 1, z, c),
    "y-": lambda x, y, z, c: (x, y - 1, z, c),
    "y^1": lambda x, y, z, c: (x, y ^ 1, z, c),
    "y^3": lambda x, y, z, c: (x, y ^ 3, z, c),
    "z^3": lambda x, y, z, c: (x, y, z ^ 3, c),
    "z+2": lambda x, y, z, c: (x, y, z + 2, c),
    "z^1": lambda x, y, z, c: (x, y, z ^ 1, c),
    "c": lambda x, y, z, c: (x, y, z, 1 - c),
}


def send(value, move):
    return lax.ppermute(value, AXES, pairs(moves[move]))


def rows_cat(*parts):
    return jnp.concatenate(parts, axis=0)


def dot(a, b):
    return jnp.dot(a, b, preferred_element_type=f32)


def dot_nt(a, b):
    return lax.dot_general(a, b, (((1,), (1,)), ((), ())), preferred_element_type=f32)


def dot_tn(a, b):
    return lax.dot_general(a, b, (((0,), (0,)), ((), ())), preferred_element_type=f32)


def lanes(value, start, size):
    return lax.dynamic_slice_in_dim(value, start, size, axis=1)


def assemble(pieces, rows, y, z_hi):
    buf = jnp.zeros((rows, 4096), bf16)
    for dz, dy, row, piece in pieces:
        at = ((z_hi + dz) % 2 * 4 + (y + dy) % 4) * 512
        buf = lax.dynamic_update_slice(buf, piece, (row, at))
    return buf


def after(value, *done):
    return lax.optimization_barrier((value, *done))[0]


def gather_inputs(own, y, z_hi):
    below, above, other = send(own, "y+"), send(own, "y-"), send(own, "z+2")
    up2 = send(rows_cat(below[:128], other), "y+")
    dn2 = send(rows_cat(above[128:], other), "y-")
    up3 = send(up2[128:256], "y+")
    dn3 = send(dn2[272:], "y-")
    pieces = [
        (0, 0, 0, own), (0, 3, 0, below), (0, 1, 0, above), (1, 0, 0, other),
        (0, 2, 0, up2[:128]), (1, 3, 0, up2[128:]), (0, 2, 128, dn2[:144]), (1, 1, 0, dn2[144:]),
        (1, 2, 0, up3), (1, 2, 128, dn3),
    ]
    return assemble(pieces, 272, y, z_hi), (below, above), (up2, dn2)


def gather_cot(own, y, z_hi, first, second):
    own = after(own, *first)
    other = send(own, "z+2")
    both = after(rows_cat(own, other), *second)
    below, above = send(both, "y+"), send(both, "y-")
    low = send(rows_cat(below[:128], below[256:384]), "y+")
    high = send(rows_cat(above[128:256], above[384:]), "y-")
    pieces = []
    for dz in (0, 1):
        at = dz * 256
        pieces += [
            (dz, 0, 0, both[at:at + 256]), (dz, 3, 0, below[at:at + 256]), (dz, 1, 0, above[at:at + 256]),
            (dz, 2, 0, low[at // 2:at // 2 + 128]), (dz, 2, 128, high[at // 2:at // 2 + 128]),
        ]
    return assemble(pieces, 256, y, z_hi)


def pick_body(parity, a_ref, b_ref, keep_ref, away_ref):
    keep_ref[...] = a_ref[...]
    away_ref[...] = b_ref[...]


def pick(full, z_lo):
    block = (256, 512)
    return pl.pallas_call(
        pick_body,
        grid_spec=pltpu.PrefetchScalarGridSpec(
            num_scalar_prefetch=1,
            grid=(4,),
            in_specs=[
                pl.BlockSpec(block, lambda i, p: (0, 2 * i + p[0])),
                pl.BlockSpec(block, lambda i, p: (0, 2 * i + 1 - p[0])),
            ],
            out_specs=[pl.BlockSpec(block, lambda i, p: (0, i)), pl.BlockSpec(block, lambda i, p: (0, i))],
        ),
        out_shape=[jax.ShapeDtypeStruct((256, 2048), bf16)] * 2,
        name="pick",
    )(z_lo.astype(jnp.int32).reshape(1), full, full)


def gather_rows(full, z_lo):
    keep, away = pick(full, z_lo)
    both = rows_cat(keep, send(away, "z^3"))
    return rows_cat(both, send(both, "c"))


def gather_tokens(block):
    both = rows_cat(block, send(block, "z^1"))
    return rows_cat(both, send(both, "c")), both


def halve(term, at, first, second, done=()):
    near, far = (at ^ 1, at ^ 3) if first.endswith("1") else (at ^ 3, at ^ 1)
    out = rows_cat(term(near).astype(bf16), term(near ^ far ^ at).astype(bf16))
    got = send(out, first)
    rows = got.shape[0] // 2
    later = after(got[rows:], *done)
    last = send((term(far) + later.astype(f32)).astype(bf16), second)
    return term(at) + got[:rows].astype(f32) + last.astype(f32), got


def local(inputs, gain, weights, d_out):
    width = weights.shape[0]
    t, s = lax.axis_index("tensor"), lax.axis_index("seq")
    z_hi, y = t // 4, t % 4
    x, z_lo, core = s // 4, s // 2 % 2, s % 2
    w_gate, w_up, w_down = weights[:, 0, :], weights[:, 1, :], weights[:, 2, :]

    def weight_rows(which, block):
        return lax.dynamic_slice(weights, (block * 512, which, 0), (512, 1, 768)).reshape(512, 768)

    own = rows_cat(inputs, jnp.broadcast_to(gain.reshape(1, 512), (16, 512)))
    full, first, second = gather_inputs(own, y, z_hi)
    x_raw = full[:256]
    x_rows = gather_rows(x_raw, z_lo)
    x_full = x_raw.astype(f32)
    gain_row = full[256:257].astype(f32)
    inv_rms = lax.rsqrt(jnp.mean(x_full * x_full, axis=1, keepdims=True) + norm_eps)
    scaled = (x_full * gain_row).astype(bf16)
    gate = dot(scaled, w_gate) * inv_rms
    up_val = dot(scaled, w_up) * inv_rms
    sigma = jax.nn.sigmoid(gate)
    hidden = (gate * sigma * up_val).astype(bf16)

    cot_full = gather_cot(d_out, y, z_hi, first, second)
    d_hidden = dot(cot_full, w_down) * inv_rms
    d_gate = (d_hidden * up_val * sigma * (1.0 + gate * (1.0 - sigma))).astype(bf16)
    d_up = (d_hidden * gate * sigma).astype(bf16)
    d_pair_all, d_pair_half = gather_tokens(jnp.concatenate([d_gate, d_up], axis=1))

    hidden_two = rows_cat(hidden, send(hidden, "c"))
    cot_two = rows_cat(cot_full, send(cot_full, "c"))

    def down_term(columns):
        def term(block):
            at = block * 1024 + core * 256
            return rows_cat(dot_tn(lanes(cot_two, at, 256), columns), dot_tn(lanes(cot_two, at + 512, 256), columns))
        return term

    d_w_low, down_one = halve(down_term(hidden_two[:, :384]), x, "x^1", "x^3")
    d_w_high, down_two = halve(down_term(hidden_two[:, 384:]), x, "x^3", "x^1")
    d_w_down = jnp.concatenate([d_w_low, d_w_high], axis=1)
    lower = z_lo == 0
    theirs = jnp.where(lower, d_w_down[256:], d_w_down[:256]).astype(bf16)
    d_w_down = jnp.where(lower, d_w_down[:256], d_w_down[256:]) + send(theirs, "z^1").astype(f32)

    products = jnp.sum(d_gate.astype(f32) * gate + d_up.astype(f32) * up_val, axis=1, keepdims=True)

    def out_term(z, tied):
        def term(block):
            return dot_nt(tied, weight_rows(2, z * 4 + block))
        return term

    def d_term(z, tied_gate, tied_up):
        def term(block):
            at = z * 4 + block
            value = dot_nt(tied_gate, weight_rows(0, at)) + dot_nt(tied_up, weight_rows(1, at))
            if z == 0:
                value = jnp.concatenate([value, jnp.broadcast_to(products, (256, 128))], axis=1)
            return value
        return term

    tied = after(hidden, cot_full)
    low, _ = halve(out_term(0, tied), y, "y^1", "y^3")
    high, _ = halve(out_term(1, tied), y, "y^3", "y^1")
    upper = z_hi == 1
    theirs = jnp.where(upper, low, high).astype(bf16)
    branch = (jnp.where(upper, high, low) + send(theirs, "z+2").astype(f32)).astype(bf16)

    def pair_term(columns):
        return lambda block: dot_tn(lanes(x_rows, block * 512 + core * 256, 256), columns)

    d_w_gate, pair_one = halve(pair_term(d_pair_all[:, :768]), x, "x^1", "x^3")
    d_w_up, pair_two = halve(pair_term(d_pair_all[:, 768:]), x, "x^3", "x^1")

    tied_gate, tied_up, _ = lax.optimization_barrier((d_gate, d_up, d_pair_half))
    down_done = (down_one, down_two)
    d_low, _ = halve(d_term(0, tied_gate, tied_up), y, "y^1", "y^3", down_done)
    d_high, _ = halve(d_term(1, tied_gate, tied_up), y, "y^3", "y^1", down_done)
    prod = d_low[:, 512:]
    d_low = d_low[:, :512]
    mine = jnp.concatenate([jnp.where(upper, d_high, d_low), prod], axis=1)
    theirs = jnp.concatenate([jnp.where(upper, d_low, d_high), prod], axis=1)
    theirs = after(theirs.astype(bf16), pair_one, pair_two)
    mine = mine + send(theirs, "z+2").astype(f32)
    d_normed, products = mine[:, :512], mine[:, 512:513] / width

    x_own = inputs.astype(f32)
    d_input = (d_normed * gain.astype(f32) - inv_rms * products * x_own).astype(bf16)
    d_gain = jnp.sum(d_normed * x_own, axis=0, keepdims=True)
    for move in ("c", "z^1", "x^1", "x+2"):
        d_gain = d_gain + send(d_gain, move)

    gain_rows = lanes(gain_row, s * 256, 256).reshape(256, 1)
    d_weights = jnp.stack(
        [(d_w_gate * gain_rows).astype(bf16), (d_w_up * gain_rows).astype(bf16), d_w_down.astype(bf16)], axis=1
    )
    return (branch, d_input, d_gain.reshape(512), d_weights)


def solution(mesh):
    in_specs = (P("seq", "tensor"), P("tensor"), P(None, None, "tensor"), P("seq", "tensor"))
    out_specs = (P("seq", "tensor"), P("seq", "tensor"), P("tensor"), P("seq", None, "tensor"))
    return jax.shard_map(local, mesh=mesh, in_specs=in_specs, out_specs=out_specs, check_vma=False)
```

```python
import functools
import jax
import jax.numpy as jnp
from jax import lax
from jax.experimental import pallas as pl
from jax.experimental.pallas import tpu as pltpu
from jax.sharding import PartitionSpec as P

norm_eps = 1e-05
AXES = ("tensor", "seq")
f32 = jnp.float32
bf16 = jnp.bfloat16
MiB = 1 << 20


def flat(x, y, z, c):
    x, y, z = x % 4, y % 4, z % 4
    return ((z // 2) * 4 + y) * 16 + (x * 2 + z % 2) * 2 + c


def pairs(move):
    places = [(x, y, z, c) for x in range(4) for y in range(4) for z in range(4) for c in range(2)]
    return [(flat(*place), flat(*move(*place))) for place in places]


moves = {
    "x^1": lambda x, y, z, c: (x ^ 1, y, z, c),
    "x^3": lambda x, y, z, c: (x ^ 3, y, z, c),
    "x+2": lambda x, y, z, c: (x + 2, y, z, c),
    "y+": lambda x, y, z, c: (x, y + 1, z, c),
    "y-": lambda x, y, z, c: (x, y - 1, z, c),
    "y^1": lambda x, y, z, c: (x, y ^ 1, z, c),
    "y^3": lambda x, y, z, c: (x, y ^ 3, z, c),
    "z+2": lambda x, y, z, c: (x, y, z + 2, c),
    "z^1": lambda x, y, z, c: (x, y, z ^ 1, c),
    "z^3": lambda x, y, z, c: (x, y, z ^ 3, c),
    "z^3c": lambda x, y, z, c: (x, y, z ^ 3, 1 - c),
    "c": lambda x, y, z, c: (x, y, z, 1 - c),
}


def send(value, move):
    return lax.ppermute(value, AXES, pairs(moves[move]))


def after(value, *done):
    return lax.optimization_barrier((value, *done))[0]


def rows_cat(*parts):
    return jnp.concatenate(parts, axis=0)


def dot(a, b):
    return jnp.dot(a, b, preferred_element_type=f32)


def dot_nt(a, b):
    return lax.dot_general(a, b, (((1,), (1,)), ((), ())), preferred_element_type=f32)


def dot_tn(a, b):
    return lax.dot_general(a, b, (((0,), (0,)), ((), ())), preferred_element_type=f32)


def call(body, name, shapes, scratch, limit, flops, size, args, hbm=()):
    spaces = [pltpu.SMEM] + [pltpu.HBM if i in hbm else pltpu.VMEM for i in range(1, len(args))]
    return pl.pallas_call(
        body,
        in_specs=[pl.BlockSpec(memory_space=space) for space in spaces],
        out_specs=[pl.BlockSpec(memory_space=pltpu.VMEM) for _ in shapes],
        out_shape=[jax.ShapeDtypeStruct(shape, dtype) for shape, dtype in shapes],
        scratch_shapes=scratch,
        compiler_params=pltpu.CompilerParams(vmem_limit_bytes=limit * MiB),
        cost_estimate=pl.CostEstimate(flops=flops, bytes_accessed=size, transcendentals=0),
        name=name,
    )(*args)


def lane(at, size, unit):
    return pl.ds(pl.multiple_of(at, unit), size)


def put(buf, spot, pieces):
    for dz, dy, row, ref, first, rows in pieces:
        buf[row:row + rows, lane(spot[dz * 4 + dy] * 512, 512, 512)] = ref[first:first + rows, :]


def fetch(w, held, sems, first, count, block_of):
    copies = []
    for k in range(8):
        rows = pl.ds(pl.multiple_of(block_of(k) * 512, 512), 512)
        copies.append(pltpu.make_async_copy(w.at[pl.ds(first, count), rows, :], held.at[k], sems.at[k]))
        copies[-1].start()
    return copies


def forward_body(spot, own, below, above, other, up2, dn2, up3, dn3, w, gate, up, hidden, inv, gains, keep, core_out,
                 z_out, cross_out, buf, held, sems):
    copies = fetch(w, held, sems, 0, 2, lambda k: k)
    put(buf, spot, [
        (0, 0, 0, own, 0, 272), (0, 3, 0, below, 0, 272), (0, 1, 0, above, 0, 272), (1, 0, 0, other, 0, 272),
        (0, 2, 0, up2, 0, 128), (1, 3, 0, up2, 128, 272), (0, 2, 128, dn2, 0, 144), (1, 1, 0, dn2, 144, 272),
        (1, 2, 0, up3, 0, 128), (1, 2, 128, dn3, 0, 144),
    ])
    z_lo, core = spot[8], spot[9]
    for i in range(4):
        for ref, zl, c in ((keep, z_lo, core), (core_out, z_lo, 1 - core), (z_out, 1 - z_lo, core),
                           (cross_out, 1 - z_lo, 1 - core)):
            ref[:, i * 256:(i + 1) * 256] = buf[0:256, lane((2 * i + zl) * 512 + c * 256, 256, 256)]
    gains[...] = buf[256:272, :]
    squares = jnp.zeros((256, 1), f32)
    for k in range(8):
        copies[k].wait()
        cols = slice(k * 512, (k + 1) * 512)
        x = buf[0:256, cols].astype(f32)
        squares = squares + jnp.sum(x * x, axis=1, keepdims=True)
        scaled = (x * buf[256:272, cols][0:1].astype(f32)).astype(bf16)
        for ref, j in ((gate, 0), (up, 1)):
            value = dot(scaled, held[k, j])
            ref[...] = value if k == 0 else ref[...] + value
    inv_rms = lax.rsqrt(squares / 4096 + norm_eps)
    g = gate[...] * inv_rms
    u = up[...] * inv_rms
    gate[...] = g
    up[...] = u
    hidden[...] = (g * jax.nn.sigmoid(g) * u).astype(bf16)
    inv[...] = jnp.broadcast_to(inv_rms, (256, 128))


def forward(spot, pieces, w3):
    shapes = [((256, 768), f32), ((256, 768), f32), ((256, 768), bf16), ((256, 128), f32), ((16, 4096), bf16)]
    shapes += [((256, 1024), bf16)] * 4
    scratch = [pltpu.VMEM((272, 4096), bf16), pltpu.VMEM((8, 2, 512, 768), bf16), pltpu.SemaphoreType.DMA((8,))]
    return call(forward_body, "forward", shapes, scratch, 46, 2 * 256 * 4096 * 1536, 16 * MiB,
                (spot, *pieces, w3), hbm=(len(pieces) + 1,))


def backward_body(spot, both, below, above, low, high, w, gate, up, inv, pair, products, mine, core_out, buf, acc,
                  held, sems):
    copies = fetch(w, held, sems, 2, 1, lambda k: k)
    put(buf, spot, [
        (0, 0, 0, both, 0, 256), (1, 0, 0, both, 256, 256), (0, 3, 0, below, 0, 256), (1, 3, 0, below, 256, 256),
        (0, 1, 0, above, 0, 256), (1, 1, 0, above, 256, 256), (0, 2, 0, low, 0, 128), (1, 2, 0, low, 128, 128),
        (0, 2, 128, high, 0, 128), (1, 2, 128, high, 128, 128),
    ])
    core = spot[9]
    for i in range(8):
        for ref, c in ((mine, core), (core_out, 1 - core)):
            ref[:, i * 256:(i + 1) * 256] = buf[:, lane(i * 512 + c * 256, 256, 256)]
    for k in range(8):
        copies[k].wait()
        value = dot(buf[:, k * 512:(k + 1) * 512], held[k, 0])
        acc[...] = value if k == 0 else acc[...] + value
    d_hidden = acc[...] * inv[:, 0:1]
    g, u = gate[...], up[...]
    sigma = jax.nn.sigmoid(g)
    d_gate = (d_hidden * u * sigma * (1.0 + g * (1.0 - sigma))).astype(bf16)
    d_up = (d_hidden * g * sigma).astype(bf16)
    pair[:, 0:768] = d_gate
    pair[:, 768:1536] = d_up
    total = jnp.sum(d_gate.astype(f32) * g + d_up.astype(f32) * u, axis=1, keepdims=True)
    products[...] = jnp.broadcast_to(total, (256, 128)).astype(bf16)


def backward(spot, pieces, w3, gate, up, inv):
    shapes = [((256, 1536), bf16), ((256, 128), bf16), ((256, 2048), bf16), ((256, 2048), bf16)]
    scratch = [pltpu.VMEM((256, 4096), bf16), pltpu.VMEM((256, 768), f32), pltpu.VMEM((8, 1, 512, 768), bf16),
               pltpu.SemaphoreType.DMA((8,))]
    return call(backward_body, "backward", shapes, scratch, 46, 2 * 256 * 4096 * 768, 8 * MiB,
                (spot, *pieces, w3, gate, up, inv), hbm=(len(pieces) + 1,))


def outer_body(count, rows, cols, order, *refs):
    a_refs, b_refs, out = refs[:count], refs[count:2 * count], refs[2 * count]

    def step(i, carry):
        at = lane(order[i] * rows, rows, rows)
        columns = lane(i // 4 * cols, cols, cols)
        total = dot_tn(a_refs[0][:, at], b_refs[0][:, columns])
        for a, b in zip(a_refs[1:], b_refs[1:]):
            total = total + dot_tn(a[:, at], b[:, columns])
        out[i] = total.astype(bf16)
        return carry

    lax.fori_loop(0, 8, step, 0)


def outer(name, order, a_list, b_list, rows):
    n = len(a_list)
    cols = b_list[0].shape[1] // 2
    return call(functools.partial(outer_body, n, rows, cols), name, [((8, rows, cols), bf16)], [], 24,
                2 * 256 * n * rows * 8 * cols, 8 * MiB, (order, *a_list, *b_list))[0]


def branch_rows_body(order, hidden, w, out, held, sems):
    copies = fetch(w, held, sems, 2, 1, lambda k: k // 4 * 4 + order[k])
    for k in range(8):
        copies[k].wait()
        out[k] = dot_nt(hidden[...], held[k, 0]).astype(bf16)


def branch_rows(order, hidden, w3):
    scratch = [pltpu.VMEM((8, 1, 512, 768), bf16), pltpu.SemaphoreType.DMA((8,))]
    return call(branch_rows_body, "branch_rows", [((8, 256, 512), bf16)], scratch, 46, 2 * 256 * 768 * 4096, 8 * MiB,
                (order, hidden, w3), hbm=(2,))[0]


def pair_rows_body(order, pair, products, w, out, held, sems):
    copies = fetch(w, held, sems, 0, 2, lambda k: k // 4 * 4 + order[k])
    for k in range(8):
        copies[k].wait()
        value = dot_nt(pair[:, 0:768], held[k, 0]) + dot_nt(pair[:, 768:1536], held[k, 1])
        out[k, :, 0:512] = value.astype(bf16)
        out[k, :, 512:640] = products[...]


def pair_rows(order, pair, products, w3):
    scratch = [pltpu.VMEM((8, 2, 512, 768), bf16), pltpu.SemaphoreType.DMA((8,))]
    return call(pair_rows_body, "pair_rows", [((8, 256, 640), bf16)], scratch, 46, 2 * 256 * 1536 * 4096, 16 * MiB,
                (order, pair, products, w3), hbm=(3,))[0]


def halve(terms, first, second, done=()):
    rows, cols = terms.shape[1:]
    got = send(terms[0:2].reshape(2 * rows, cols), first)
    later = after(got[rows:], *done)
    out = (terms[2].astype(f32) + later.astype(f32)).astype(bf16)
    last = send(out, second)
    return terms[3].astype(f32) + got[:rows].astype(f32) + last.astype(f32), got, out


def gather_inputs(own):
    below, above, other = send(own, "y+"), send(own, "y-"), send(own, "z+2")
    up2 = send(rows_cat(below[:128], other), "y+")
    dn2 = send(rows_cat(above[128:], other), "y-")
    up3 = send(up2[128:256], "y+")
    dn3 = send(dn2[272:], "y-")
    return (own, below, above, other, up2, dn2, up3, dn3)


def gather_cot(own, first, second):
    own = after(own, *first)
    other = send(own, "z+2")
    both = after(rows_cat(own, other), *second)
    below, above = send(both, "y+"), send(both, "y-")
    low = send(rows_cat(below[:128], below[256:384]), "y+")
    high = send(rows_cat(above[128:256], above[384:]), "y-")
    return (both, below, above, low, high)


def local(inputs, gain, weights, d_out):
    width = weights.shape[0]
    t, s = lax.axis_index("tensor"), lax.axis_index("seq")
    z_hi, y = t // 4, t % 4
    x, z_lo, core = s // 4, s // 2 % 2, s % 2
    w3 = jnp.transpose(weights, (1, 0, 2))
    spot = jnp.stack(
        [(z_hi + dz) % 2 * 4 + (y + dy) % 4 for dz in (0, 1) for dy in range(4)] + [z_lo, core]
    ).astype(jnp.int32)

    def order(at):
        return jnp.stack([at ^ 1, at ^ 2, at ^ 3, at, at ^ 3, at ^ 2, at ^ 1, at]).astype(jnp.int32)

    x_pieces = gather_inputs(rows_cat(inputs, jnp.broadcast_to(gain.reshape(1, 512), (16, 512))))
    cot_pieces = gather_cot(d_out, x_pieces[1:3], x_pieces[4:6])
    gate, up_val, hidden, inv, gains, x_keep, x_core, x_z, x_cross = forward(spot, x_pieces, w3)
    x_all = [x_keep, send(x_z, "z^3"), send(x_core, "c"), send(x_cross, "z^3c")]
    hidden_core = send(hidden, "c")

    d_pair, products, cot_mine, cot_core = backward(spot, cot_pieces, w3, gate, up_val, inv)
    cot_core = send(cot_core, "c")
    pair_z = send(d_pair, "z^1")
    pair_core = send(d_pair, "c")
    pair_cross = send(pair_z, "c")

    down_terms = outer("down_terms", order(x), [cot_mine, cot_core], [hidden, hidden_core], 512)
    d_w_low, down_one, _ = halve(down_terms[0:4], "x^1", "x^3")
    d_w_high, down_two, _ = halve(down_terms[4:8], "x^3", "x^1")
    d_w_down = jnp.concatenate([d_w_low, d_w_high], axis=1)
    lower = z_lo == 0
    theirs = jnp.where(lower, d_w_down[256:], d_w_down[:256]).astype(bf16)
    d_w_down = jnp.where(lower, d_w_down[:256], d_w_down[256:]) + send(theirs, "z^1").astype(f32)

    branch_terms = branch_rows(order(y), after(hidden, cot_mine), w3)
    low, _, _ = halve(branch_terms[0:4], "y^1", "y^3")
    high, _, _ = halve(branch_terms[4:8], "y^3", "y^1")
    upper = z_hi == 1
    theirs = jnp.where(upper, low, high).astype(bf16)
    branch = (jnp.where(upper, high, low) + send(theirs, "z+2").astype(f32)).astype(bf16)

    pair_terms = outer("pair_terms", order(x), x_all, [d_pair, pair_z, pair_core, pair_cross], 256)
    d_w_gate, pair_one, pair_out_one = halve(pair_terms[0:4], "x^1", "x^3")
    d_w_up, pair_two, pair_out_two = halve(pair_terms[4:8], "x^3", "x^1")

    d_terms = pair_rows(order(y), after(d_pair, pair_z, down_terms), products, w3)
    d_low, _, _ = halve(d_terms[0:4], "y^1", "y^3", (down_one, down_two))
    d_high, _, _ = halve(d_terms[4:8], "y^3", "y^1", (down_one, down_two))
    mine = jnp.where(upper, d_high, d_low)
    theirs = after(jnp.where(upper, d_low, d_high).astype(bf16), pair_one, pair_two)
    mine = mine + send(theirs, "z+2").astype(f32)
    d_normed, products = mine[:, :512], mine[:, 512:513] / width

    x_own = inputs.astype(f32)
    d_input = (d_normed * gain.astype(f32) - inv[:, :1] * products * x_own).astype(bf16)
    d_gain = jnp.sum(d_normed * x_own, axis=0, keepdims=True)
    d_gain = after(d_gain, pair_out_one, pair_out_two)
    for move in ("c", "z^1", "x^1", "x+2"):
        d_gain = d_gain + send(d_gain, move)

    gain_rows = lax.dynamic_slice(gains, (0, s * 256), (1, 256)).astype(f32).reshape(256, 1)
    d_weights = jnp.stack(
        [(d_w_gate * gain_rows).astype(bf16), (d_w_up * gain_rows).astype(bf16), d_w_down.astype(bf16)], axis=1
    )
    return (branch, d_input, d_gain.reshape(512), d_weights)


def solution(mesh):
    in_specs = (P("seq", "tensor"), P("tensor"), P(None, None, "tensor"), P("seq", "tensor"))
    out_specs = (P("seq", "tensor"), P("seq", "tensor"), P("tensor"), P("seq", None, "tensor"))
    return jax.shard_map(local, mesh=mesh, in_specs=in_specs, out_specs=out_specs, check_vma=False)
```

```python
import functools
import jax
import jax.numpy as jnp
from jax import lax
from jax.experimental import pallas as pl
from jax.experimental.pallas import tpu as pltpu
from jax.sharding import PartitionSpec as P

norm_eps = 1e-05
AXES = ("tensor", "seq")
f32 = jnp.float32
bf16 = jnp.bfloat16
MiB = 1 << 20


def flat(x, y, z, c):
    x, y, z = x % 4, y % 4, z % 4
    return ((z // 2) * 4 + y) * 16 + (x * 2 + z % 2) * 2 + c


def pairs(move):
    places = [(x, y, z, c) for x in range(4) for y in range(4) for z in range(4) for c in range(2)]
    return [(flat(*place), flat(*move(*place))) for place in places]


moves = {
    "x^1": lambda x, y, z, c: (x ^ 1, y, z, c),
    "x^3": lambda x, y, z, c: (x ^ 3, y, z, c),
    "x+2": lambda x, y, z, c: (x + 2, y, z, c),
    "y+": lambda x, y, z, c: (x, y + 1, z, c),
    "y-": lambda x, y, z, c: (x, y - 1, z, c),
    "y^1": lambda x, y, z, c: (x, y ^ 1, z, c),
    "y^3": lambda x, y, z, c: (x, y ^ 3, z, c),
    "z+2": lambda x, y, z, c: (x, y, z + 2, c),
    "z^1": lambda x, y, z, c: (x, y, z ^ 1, c),
    "z^3": lambda x, y, z, c: (x, y, z ^ 3, c),
    "z^3c": lambda x, y, z, c: (x, y, z ^ 3, 1 - c),
    "c": lambda x, y, z, c: (x, y, z, 1 - c),
}


def send(value, move):
    return lax.ppermute(value, AXES, pairs(moves[move]))


def after(value, *done):
    return lax.optimization_barrier((value, *done))[0]


def rows_cat(*parts):
    return jnp.concatenate(parts, axis=0)


def dot(a, b):
    return jnp.dot(a, b, preferred_element_type=f32)


def dot_nt(a, b):
    return lax.dot_general(a, b, (((1,), (1,)), ((), ())), preferred_element_type=f32)


def dot_tn(a, b):
    return lax.dot_general(a, b, (((0,), (0,)), ((), ())), preferred_element_type=f32)


def call(body, name, shapes, scratch, limit, args, hbm=()):
    spaces = [pltpu.SMEM] + [pltpu.HBM if i in hbm else pltpu.VMEM for i in range(1, len(args))]
    return pl.pallas_call(
        body,
        in_specs=[pl.BlockSpec(memory_space=space) for space in spaces],
        out_specs=[pl.BlockSpec(memory_space=pltpu.VMEM) for _ in shapes],
        out_shape=[jax.ShapeDtypeStruct(shape, dtype) for shape, dtype in shapes],
        scratch_shapes=scratch,
        compiler_params=pltpu.CompilerParams(vmem_limit_bytes=limit * MiB),
        cost_estimate=pl.CostEstimate(flops=1, bytes_accessed=1, transcendentals=0),
        name=name,
    )(*args)


def lane(at, size, unit):
    return pl.ds(pl.multiple_of(at, unit), size)


def put(buf, spot, pieces):
    for dz, dy, row, ref, first, rows in pieces:
        buf[row:row + rows, lane(spot[dz * 4 + dy] * 512, 512, 512)] = ref[first:first + rows, :]


def fetch(w, held, sems, first, count, block_of):
    copies = []
    for k in range(8):
        rows = pl.ds(pl.multiple_of(block_of(k) * 512, 512), 512)
        copies.append(pltpu.make_async_copy(w.at[pl.ds(first, count), rows, :], held.at[k], sems.at[k]))
        copies[-1].start()
    return copies


def forward_body(spot, own, below, above, far, other, other_below, other_above, other_far, w, gate, up, hidden, inv,
                 gains, keep, core_out, z_out, cross_out, buf, held, sems):
    copies = fetch(w, held, sems, 0, 2, lambda k: k)
    put(buf, spot, [
        (0, 0, 0, own, 0, 272), (0, 3, 0, below, 0, 272), (0, 1, 0, above, 0, 272), (0, 2, 0, far, 0, 272),
        (1, 0, 0, other, 0, 272), (1, 3, 0, other_below, 0, 272), (1, 1, 0, other_above, 0, 272),
        (1, 2, 0, other_far, 0, 272),
    ])
    z_lo, core = spot[8], spot[9]
    for i in range(4):
        for ref, zl, c in ((keep, z_lo, core), (core_out, z_lo, 1 - core), (z_out, 1 - z_lo, core),
                           (cross_out, 1 - z_lo, 1 - core)):
            ref[:, i * 256:(i + 1) * 256] = buf[0:256, lane((2 * i + zl) * 512 + c * 256, 256, 256)]
    gains[...] = buf[256:272, :]
    squares = jnp.zeros((256, 1), f32)
    for k in range(8):
        copies[k].wait()
        cols = slice(k * 512, (k + 1) * 512)
        x = buf[0:256, cols].astype(f32)
        squares = squares + jnp.sum(x * x, axis=1, keepdims=True)
        scaled = (x * buf[256:272, cols][0:1].astype(f32)).astype(bf16)
        for ref, j in ((gate, 0), (up, 1)):
            value = dot(scaled, held[k, j])
            ref[...] = value if k == 0 else ref[...] + value
    inv_rms = lax.rsqrt(squares / 4096 + norm_eps)
    g = gate[...] * inv_rms
    u = up[...] * inv_rms
    gate[...] = g
    up[...] = u
    hidden[...] = (g * jax.nn.sigmoid(g) * u).astype(bf16)
    core_out[:, 1024:1792] = hidden[...]
    inv[...] = jnp.broadcast_to(inv_rms, (256, 128))


def forward(spot, pieces, w3):
    shapes = [((256, 768), f32), ((256, 768), f32), ((256, 768), bf16), ((256, 128), f32), ((16, 4096), bf16)]
    shapes += [((256, 1024), bf16), ((256, 1792), bf16), ((256, 1024), bf16), ((256, 1024), bf16)]
    scratch = [pltpu.VMEM((272, 4096), bf16), pltpu.VMEM((8, 2, 512, 768), bf16), pltpu.SemaphoreType.DMA((8,))]
    return call(forward_body, "forward", shapes, scratch, 20,
                (spot, *pieces, w3), hbm=(len(pieces) + 1,))


def backward_body(spot, both, below, above, low, high, w, gate, up, inv, pair, products, mine, core_out, buf, acc,
                  held, sems):
    copies = fetch(w, held, sems, 2, 1, lambda k: k)
    put(buf, spot, [
        (0, 0, 0, both, 0, 256), (1, 0, 0, both, 256, 256), (0, 3, 0, below, 0, 256), (1, 3, 0, below, 256, 256),
        (0, 1, 0, above, 0, 256), (1, 1, 0, above, 256, 256), (0, 2, 0, low, 0, 128), (1, 2, 0, low, 128, 128),
        (0, 2, 128, high, 0, 128), (1, 2, 128, high, 128, 128),
    ])
    core = spot[9]
    for i in range(8):
        for ref, c in ((mine, core), (core_out, 1 - core)):
            ref[:, i * 256:(i + 1) * 256] = buf[:, lane(i * 512 + c * 256, 256, 256)]
    for k in range(8):
        copies[k].wait()
        value = dot(buf[:, k * 512:(k + 1) * 512], held[k, 0])
        acc[...] = value if k == 0 else acc[...] + value
    d_hidden = acc[...] * inv[:, 0:1]
    g, u = gate[...], up[...]
    sigma = jax.nn.sigmoid(g)
    d_gate = (d_hidden * u * sigma * (1.0 + g * (1.0 - sigma))).astype(bf16)
    d_up = (d_hidden * g * sigma).astype(bf16)
    pair[:, 0:768] = d_gate
    pair[:, 768:1536] = d_up
    core_out[:, 2048:2816] = d_gate
    core_out[:, 2816:3584] = d_up
    total = jnp.sum(d_gate.astype(f32) * g + d_up.astype(f32) * u, axis=1, keepdims=True)
    products[...] = jnp.broadcast_to(total, (256, 128)).astype(bf16)


def backward(spot, pieces, w3, gate, up, inv):
    shapes = [((256, 1536), bf16), ((256, 128), bf16), ((256, 2048), bf16), ((256, 3584), bf16)]
    scratch = [pltpu.VMEM((256, 4096), bf16), pltpu.VMEM((256, 768), f32), pltpu.VMEM((8, 1, 512, 768), bf16),
               pltpu.SemaphoreType.DMA((8,))]
    return call(backward_body, "backward", shapes, scratch, 15,
                (spot, *pieces, w3, gate, up, inv), hbm=(len(pieces) + 1,))


def outer_body(a_from, b_from, rows, cols, order, *refs):
    n = len(a_from)
    a_refs, b_refs, out = refs[:n], refs[n:2 * n], refs[2 * n]

    def step(i, carry):
        total = None
        for a, a0, b, b0 in zip(a_refs, a_from, b_refs, b_from):
            value = dot_tn(a[:, lane(order[i] * rows + a0, rows, 256)], b[:, lane(i // 4 * cols + b0, cols, 128)])
            total = value if total is None else total + value
        out[i] = total.astype(bf16)
        return carry

    lax.fori_loop(0, 8, step, 0)


def outer(name, order, a_list, b_list, rows, cols):
    body = functools.partial(outer_body, [f for _, f in a_list], [f for _, f in b_list], rows, cols)
    return call(body, name, [((8, rows, cols), bf16)], [], 10, (order, *[a for a, _ in a_list], *[b for b, _ in b_list]))[0]


def branch_rows_body(order, hidden, w, out, held, sems):
    copies = fetch(w, held, sems, 2, 1, lambda k: k // 4 * 4 + order[k])
    for k in range(8):
        copies[k].wait()
        out[k] = dot_nt(hidden[...], held[k, 0]).astype(bf16)


def branch_rows(order, hidden, w3):
    scratch = [pltpu.VMEM((8, 1, 512, 768), bf16), pltpu.SemaphoreType.DMA((8,))]
    return call(branch_rows_body, "branch_rows", [((8, 256, 512), bf16)], scratch, 8,
                (order, hidden, w3), hbm=(2,))[0]


def pair_rows_body(order, pair, products, w, out, held, sems):
    copies = fetch(w, held, sems, 0, 2, lambda k: k // 4 * 4 + order[k])
    for k in range(8):
        copies[k].wait()
        value = dot_nt(pair[:, 0:768], held[k, 0]) + dot_nt(pair[:, 768:1536], held[k, 1])
        out[k, :, 0:512] = value.astype(bf16)
        out[k, :, 512:640] = products[...]


def pair_rows(order, pair, products, w3):
    scratch = [pltpu.VMEM((8, 2, 512, 768), bf16), pltpu.SemaphoreType.DMA((8,))]
    return call(pair_rows_body, "pair_rows", [((8, 256, 640), bf16)], scratch, 15,
                (order, pair, products, w3), hbm=(3,))[0]


def halve(terms, axis, done=()):
    rows, cols = terms.shape[1:]
    near, far = axis + "^1", axis + "^3"
    got = [send(terms[4 * h:4 * h + 2].reshape(2 * rows, cols), move) for h, move in ((0, near), (1, far))]
    two, six, *got = lax.optimization_barrier((terms[2], terms[6], *got, *done))[:4]
    out = [(t.astype(f32) + g[rows:].astype(f32)).astype(bf16) for t, g in zip((two, six), got)]
    last = [send(o, move) for o, move in zip(out, (far, near))]
    sums = [terms[4 * h + 3].astype(f32) + got[h][:rows].astype(f32) + last[h].astype(f32) for h in (0, 1)]
    return sums, got, out, last


def gather_inputs(own):
    below, above, other = send(own, "y+"), send(own, "y-"), send(own, "z+2")
    far = rows_cat(send(below[:128], "y+"), send(above[128:], "y-"))
    other = after(other, far)
    other_below, other_above = send(other, "y+"), send(other, "y-")
    return (own, below, above, far, other, other_below, other_above, send(far, "z+2"))


def gather_cot(own, first, second):
    other = send(after(own, *first), "z+2")
    both = after(rows_cat(own, other), *second)
    below, above = send(both, "y+"), send(both, "y-")
    low = send(rows_cat(below[:128], below[256:384]), "y+")
    high = send(rows_cat(above[128:256], above[384:]), "y-")
    return (both, below, above, low, high)


def local(inputs, gain, weights, d_out):
    width = weights.shape[0]
    t, s = lax.axis_index("tensor"), lax.axis_index("seq")
    z_hi, y = t // 4, t % 4
    x, z_lo, core = s // 4, s // 2 % 2, s % 2
    w3 = pltpu.with_memory_space_constraint(jnp.transpose(weights, (1, 0, 2)), pltpu.HBM)
    spot = jnp.stack(
        [(z_hi + dz) % 2 * 4 + (y + dy) % 4 for dz in (0, 1) for dy in range(4)] + [z_lo, core]
    ).astype(jnp.int32)

    def order(at):
        return jnp.stack([at ^ 1, at ^ 2, at ^ 3, at, at ^ 3, at ^ 2, at ^ 1, at]).astype(jnp.int32)

    x_pieces = gather_inputs(rows_cat(inputs, jnp.broadcast_to(gain.reshape(1, 512), (16, 512))))
    cot_pieces = gather_cot(d_out, x_pieces[4:5], x_pieces[5:7])
    gate, up_val, hidden, inv, gains, x_keep, core_one, x_same, x_cross = forward(spot, x_pieces, w3)
    x_same = send(x_same, "z^3")
    core_one = send(core_one, "c")
    branch_terms = branch_rows(order(y), hidden, w3)
    x_cross = send(x_cross, "z^1")
    cot_pieces = (after(cot_pieces[0], core_one, x_same, x_cross, branch_terms), *cot_pieces[1:])
    d_pair, products, cot_mine, core_two = backward(spot, cot_pieces, w3, gate, up_val, inv)
    core_two = send(core_two, "c")
    d_terms = pair_rows(order(y), d_pair, products, w3)
    pair_z = send(d_pair, "z^1")
    down_terms = outer("down_terms", order(x), [(after(cot_mine, d_terms), 0), (core_two, 0)], [(hidden, 0), (core_one, 1024)], 512, 384)
    down, down_got, _, down_last = halve(down_terms, "x")
    core_three = send(jnp.concatenate([x_cross, after(pair_z, *down_got)], axis=1), "c")
    d_w_down = jnp.concatenate(down, axis=1)
    lower = z_lo == 0
    theirs = jnp.where(lower, d_w_down[256:], d_w_down[:256]).astype(bf16)
    d_w_down = jnp.where(lower, d_w_down[:256], d_w_down[256:]) + send(theirs, "z^1").astype(f32)

    pair_terms = outer(
        "pair_terms", order(x), [(x_keep, 0), (x_same, 0), (core_one, 0), (core_three, 0)],
        [(d_pair, 0), (pair_z, 0), (core_two, 2048), (core_three, 1024)], 256, 768,
    )
    (d_w_gate, d_w_up), _, pair_out, _ = halve(after(pair_terms, *down_last), "x")

    (d_low, d_high), _, _, d_last = halve(d_terms, "y", down_got)
    (low, high), _, _, _ = halve(after(branch_terms, *d_last), "y")
    upper = z_hi == 1
    mine = jnp.where(upper, d_high, d_low)
    theirs = send(jnp.where(upper, d_low, d_high).astype(bf16), "z+2")
    mine = mine + theirs.astype(f32)
    theirs = send(after(jnp.where(upper, low, high).astype(bf16), theirs), "z+2")
    branch = (jnp.where(upper, high, low) + theirs.astype(f32)).astype(bf16)
    d_normed, products = mine[:, :512], mine[:, 512:513] / width

    x_own = inputs.astype(f32)
    d_input = (d_normed * gain.astype(f32) - inv[:, :1] * products * x_own).astype(bf16)
    d_gain = jnp.sum(d_normed * x_own, axis=0, keepdims=True)
    for move in ("c", "z^1", "x^1", "x+2"):
        if move == "x^1":
            d_gain = after(d_gain, *pair_out)
        d_gain = d_gain + send(d_gain, move)

    gain_rows = lax.dynamic_slice(gains, (0, s * 256), (1, 256)).astype(f32).reshape(256, 1)
    d_weights = jnp.stack(
        [(d_w_gate * gain_rows).astype(bf16), (d_w_up * gain_rows).astype(bf16), d_w_down.astype(bf16)], axis=1
    )
    return (branch, d_input, d_gain.reshape(512), d_weights)


def solution(mesh):
    in_specs = (P("seq", "tensor"), P("tensor"), P(None, None, "tensor"), P("seq", "tensor"))
    out_specs = (P("seq", "tensor"), P("seq", "tensor"), P("tensor"), P("seq", None, "tensor"))
    return jax.shard_map(local, mesh=mesh, in_specs=in_specs, out_specs=out_specs, check_vma=False)
```

```python
import functools
import jax
import jax.numpy as jnp
from jax import lax
from jax.experimental import pallas as pl
from jax.experimental.pallas import tpu as pltpu
from jax.sharding import PartitionSpec as P

norm_eps = 1e-05
AXES = ("tensor", "seq")
f32 = jnp.float32
bf16 = jnp.bfloat16
MiB = 1 << 20


def flat(x, y, z, c):
    x, y, z = x % 4, y % 4, z % 4
    return ((z // 2) * 4 + y) * 16 + (x * 2 + z % 2) * 2 + c


def pairs(move):
    places = [(x, y, z, c) for x in range(4) for y in range(4) for z in range(4) for c in range(2)]
    return [(flat(*place), flat(*move(*place))) for place in places]


moves = {
    "x^1": lambda x, y, z, c: (x ^ 1, y, z, c),
    "x^3": lambda x, y, z, c: (x ^ 3, y, z, c),
    "x+2": lambda x, y, z, c: (x + 2, y, z, c),
    "y+": lambda x, y, z, c: (x, y + 1, z, c),
    "y-": lambda x, y, z, c: (x, y - 1, z, c),
    "y^1": lambda x, y, z, c: (x, y ^ 1, z, c),
    "y^3": lambda x, y, z, c: (x, y ^ 3, z, c),
    "z+2": lambda x, y, z, c: (x, y, z + 2, c),
    "z^1": lambda x, y, z, c: (x, y, z ^ 1, c),
    "z^3": lambda x, y, z, c: (x, y, z ^ 3, c),
    "z^3c": lambda x, y, z, c: (x, y, z ^ 3, 1 - c),
    "c": lambda x, y, z, c: (x, y, z, 1 - c),
}


def send(value, move):
    return lax.ppermute(value, AXES, pairs(moves[move]))


def after(value, *done):
    return lax.optimization_barrier((value, *done))[0]


def rows_cat(*parts):
    return jnp.concatenate(parts, axis=0)


def dot(a, b):
    return jnp.dot(a, b, preferred_element_type=f32)


def dot_nt(a, b):
    return lax.dot_general(a, b, (((1,), (1,)), ((), ())), preferred_element_type=f32)


def dot_tn(a, b):
    return lax.dot_general(a, b, (((0,), (0,)), ((), ())), preferred_element_type=f32)


def call(body, name, shapes, scratch, limit, args, hbm=()):
    spaces = [pltpu.SMEM] + [pltpu.HBM if i in hbm else pltpu.VMEM for i in range(1, len(args))]
    return pl.pallas_call(
        body,
        in_specs=[pl.BlockSpec(memory_space=space) for space in spaces],
        out_specs=[pl.BlockSpec(memory_space=pltpu.VMEM) for _ in shapes],
        out_shape=[jax.ShapeDtypeStruct(shape, dtype) for shape, dtype in shapes],
        scratch_shapes=scratch,
        compiler_params=pltpu.CompilerParams(vmem_limit_bytes=limit * MiB),
        cost_estimate=pl.CostEstimate(flops=1, bytes_accessed=1, transcendentals=0),
        name=name,
    )(*args)


def lane(at, size, unit):
    return pl.ds(pl.multiple_of(at, unit), size)


def put(buf, spot, pieces):
    for dz, dy, row, ref, first, rows in pieces:
        buf[row:row + rows, lane(spot[dz * 4 + dy] * 512, 512, 512)] = ref[first:first + rows, :]


def fetch(w, held, sems, first, count, block_of):
    copies = []
    for k in range(8):
        rows = pl.ds(pl.multiple_of(block_of(k) * 512, 512), 512)
        copies.append(pltpu.make_async_copy(w.at[pl.ds(first, count), rows, :], held.at[k], sems.at[k]))
        copies[-1].start()
    return copies


def forward_body(spot, own, below, above, other, up2, down2, other_far, w, gate, up, hidden, inv, gains, keep, core_out,
                 z_out, cross_out, buf, held, sems):
    copies = fetch(w, held, sems, 0, 2, lambda k: k)
    put(buf, spot, [
        (0, 0, 0, own, 0, 272), (0, 3, 0, below, 0, 272), (0, 1, 0, above, 0, 272), (1, 0, 0, other, 0, 272),
        (0, 2, 0, up2, 0, 128), (1, 3, 0, up2, 128, 272), (0, 2, 128, down2, 0, 144), (1, 1, 0, down2, 144, 272),
        (1, 2, 0, other_far, 0, 272),
    ])
    z_lo, core = spot[8], spot[9]
    for i in range(4):
        for ref, zl, c in ((keep, z_lo, core), (core_out, z_lo, 1 - core), (z_out, 1 - z_lo, core),
                           (cross_out, 1 - z_lo, 1 - core)):
            ref[:, i * 256:(i + 1) * 256] = buf[0:256, lane((2 * i + zl) * 512 + c * 256, 256, 256)]
    gains[...] = buf[256:272, :]
    squares = jnp.zeros((256, 1), f32)
    for k in range(8):
        copies[k].wait()
        cols = slice(k * 512, (k + 1) * 512)
        x = buf[0:256, cols].astype(f32)
        squares = squares + jnp.sum(x * x, axis=1, keepdims=True)
        scaled = (x * buf[256:272, cols][0:1].astype(f32)).astype(bf16)
        for ref, j in ((gate, 0), (up, 1)):
            value = dot(scaled, held[k, j])
            ref[...] = value if k == 0 else ref[...] + value
    inv_rms = lax.rsqrt(squares / 4096 + norm_eps)
    g = gate[...] * inv_rms
    u = up[...] * inv_rms
    gate[...] = g
    up[...] = u
    hidden[...] = (g * jax.nn.sigmoid(g) * u).astype(bf16)
    core_out[:, 1024:1792] = hidden[...]
    inv[...] = jnp.broadcast_to(inv_rms, (256, 128))


def forward(spot, pieces, w3):
    shapes = [((256, 768), f32), ((256, 768), f32), ((256, 768), bf16), ((256, 128), f32), ((16, 4096), bf16)]
    shapes += [((256, 1024), bf16), ((256, 1792), bf16), ((256, 1024), bf16), ((256, 1024), bf16)]
    scratch = [pltpu.VMEM((272, 4096), bf16), pltpu.VMEM((8, 2, 512, 768), bf16), pltpu.SemaphoreType.DMA((8,))]
    return call(forward_body, "forward", shapes, scratch, 20,
                (spot, *pieces, w3), hbm=(len(pieces) + 1,))


def backward_body(spot, cot, up, down, other, cot_up, cot_down, far, w, gate, up_val, inv, pair, products, mine,
                  core_out, buf, acc, held, sems):
    copies = fetch(w, held, sems, 2, 1, lambda k: k)
    put(buf, spot, [
        (0, 0, 0, cot, 0, 256), (0, 3, 0, up, 400, 256), (0, 1, 0, down, 416, 256), (1, 0, 0, other, 0, 256),
        (0, 2, 0, cot_up, 0, 128), (1, 3, 0, cot_up, 128, 256), (0, 2, 128, cot_down, 0, 128),
        (1, 1, 0, cot_down, 128, 256), (1, 2, 0, far, 0, 256),
    ])
    core = spot[9]
    for i in range(8):
        for ref, c in ((mine, core), (core_out, 1 - core)):
            ref[:, i * 256:(i + 1) * 256] = buf[:, lane(i * 512 + c * 256, 256, 256)]
    for k in range(8):
        copies[k].wait()
        value = dot(buf[:, k * 512:(k + 1) * 512], held[k, 0])
        acc[...] = value if k == 0 else acc[...] + value
    d_hidden = acc[...] * inv[:, 0:1]
    g, u = gate[...], up_val[...]
    sigma = jax.nn.sigmoid(g)
    d_gate = (d_hidden * u * sigma * (1.0 + g * (1.0 - sigma))).astype(bf16)
    d_up = (d_hidden * g * sigma).astype(bf16)
    pair[:, 0:768] = d_gate
    pair[:, 768:1536] = d_up
    core_out[:, 2048:2816] = d_gate
    core_out[:, 2816:3584] = d_up
    total = jnp.sum(d_gate.astype(f32) * g + d_up.astype(f32) * u, axis=1, keepdims=True)
    products[...] = jnp.broadcast_to(total, (256, 128)).astype(bf16)


def backward(spot, pieces, w3, gate, up, inv):
    shapes = [((256, 1536), bf16), ((256, 128), bf16), ((256, 2048), bf16), ((256, 3584), bf16)]
    scratch = [pltpu.VMEM((256, 4096), bf16), pltpu.VMEM((256, 768), f32), pltpu.VMEM((8, 1, 512, 768), bf16),
               pltpu.SemaphoreType.DMA((8,))]
    return call(backward_body, "backward", shapes, scratch, 15, (spot, *pieces, w3, gate, up, inv),
                hbm=(len(pieces) + 1,))


def outer_body(a_from, b_from, rows, cols, order, *refs):
    n = len(a_from)
    a_refs, b_refs, out = refs[:n], refs[n:2 * n], refs[2 * n]

    def step(i, carry):
        total = None
        for a, a0, b, b0 in zip(a_refs, a_from, b_refs, b_from):
            value = dot_tn(a[:, lane(order[i] * rows + a0, rows, 256)], b[:, lane(i // 4 * cols + b0, cols, 128)])
            total = value if total is None else total + value
        out[i] = total.astype(bf16)
        return carry

    lax.fori_loop(0, 8, step, 0)


def outer(name, order, a_list, b_list, rows, cols):
    body = functools.partial(outer_body, [f for _, f in a_list], [f for _, f in b_list], rows, cols)
    return call(body, name, [((8, rows, cols), bf16)], [], 10, (order, *[a for a, _ in a_list], *[b for b, _ in b_list]))[0]


def branch_rows_body(order, hidden, w, out, held, sems):
    copies = fetch(w, held, sems, 2, 1, lambda k: k // 4 * 4 + order[k])
    for k in range(8):
        copies[k].wait()
        out[k] = dot_nt(hidden[...], held[k, 0]).astype(bf16)


def branch_rows(order, hidden, w3):
    scratch = [pltpu.VMEM((8, 1, 512, 768), bf16), pltpu.SemaphoreType.DMA((8,))]
    return call(branch_rows_body, "branch_rows", [((8, 256, 512), bf16)], scratch, 8,
                (order, hidden, w3), hbm=(2,))[0]


def pair_rows_body(order, pair, products, w, out, held, sems):
    copies = fetch(w, held, sems, 0, 2, lambda k: k // 4 * 4 + order[k])
    for k in range(8):
        copies[k].wait()
        value = dot_nt(pair[:, 0:768], held[k, 0]) + dot_nt(pair[:, 768:1536], held[k, 1])
        out[k, :, 0:512] = value.astype(bf16)
        out[k, :, 512:640] = products[...]


def pair_rows(order, pair, products, w3):
    scratch = [pltpu.VMEM((8, 2, 512, 768), bf16), pltpu.SemaphoreType.DMA((8,))]
    return call(pair_rows_body, "pair_rows", [((8, 256, 640), bf16)], scratch, 15,
                (order, pair, products, w3), hbm=(3,))[0]


def halve(terms, axis, done=()):
    rows, cols = terms.shape[1:]
    near, far = axis + "^1", axis + "^3"
    got = [send(terms[4 * h:4 * h + 2].reshape(2 * rows, cols), move) for h, move in ((0, near), (1, far))]
    two, six, *got = lax.optimization_barrier((terms[2], terms[6], *got, *done))[:4]
    out = [(t.astype(f32) + g[rows:].astype(f32)).astype(bf16) for t, g in zip((two, six), got)]
    last = [send(o, move) for o, move in zip(out, (far, near))]
    return got, out, last


def finish(terms, got, last, done=()):
    three, seven = lax.optimization_barrier((terms[3], terms[7], *done))[:2]
    rows = terms.shape[1]
    return [t.astype(f32) + g[:rows].astype(f32) + e.astype(f32) for t, g, e in zip((three, seven), got, last)]


def gather_both(own, cot):
    below, above, other = send(own, "y+"), send(own, "y-"), send(own, "z+2")
    up = send(rows_cat(below[:128], other, cot), "y+")
    down = send(rows_cat(above[128:], other, cot), "y-")
    cot_other = send(after(cot, other), "z+2")
    other_far = send(after(rows_cat(up[:128], down[:144]), cot_other), "z+2")
    cot_up = send(rows_cat(up[400:528], cot_other), "y+")
    cot_down = send(rows_cat(down[544:], cot_other), "y-")
    cot_far = send(rows_cat(cot_up[:128], cot_down[:128]), "z+2")
    return (own, below, above, other, up, down, other_far), (cot, up, down, cot_other, cot_up, cot_down, cot_far)


def local(inputs, gain, weights, d_out):
    width = weights.shape[0]
    t, s = lax.axis_index("tensor"), lax.axis_index("seq")
    z_hi, y = t // 4, t % 4
    x, z_lo, core = s // 4, s // 2 % 2, s % 2
    w3 = pltpu.with_memory_space_constraint(jnp.transpose(weights, (1, 0, 2)), pltpu.HBM)
    spot = jnp.stack(
        [(z_hi + dz) % 2 * 4 + (y + dy) % 4 for dz in (0, 1) for dy in range(4)] + [z_lo, core]
    ).astype(jnp.int32)

    def order(at):
        return jnp.stack([at ^ 1, at ^ 2, at ^ 3, at, at ^ 3, at ^ 2, at ^ 1, at]).astype(jnp.int32)

    own = rows_cat(inputs, jnp.broadcast_to(gain.reshape(1, 512), (16, 512)))
    x_pieces, cot_pieces = gather_both(own, d_out)
    gate, up_val, hidden, inv, gains, x_keep, core_one, x_same, x_cross = forward(spot, x_pieces, w3)
    x_same, x_cross = lax.optimization_barrier((x_same, x_cross, *cot_pieces[4:6]))[:2]
    x_same, x_cross = send(x_same, "z^3"), send(x_cross, "z^1")
    core_one = send(core_one, "c")
    branch_terms = branch_rows(order(y), hidden, w3)
    cot_pieces = (after(cot_pieces[0], core_one, x_same, x_cross, branch_terms), *cot_pieces[1:])
    d_pair, products, cot_mine, core_two = backward(spot, cot_pieces, w3, gate, up_val, inv)
    core_two = send(core_two, "c")
    pair_z = send(d_pair, "z^1")
    down_terms = outer("down_terms", order(x), [(cot_mine, 0), (core_two, 0)], [(hidden, 0), (core_one, 1024)], 512, 384)
    down_got, _, down_last = halve(down_terms, "x")
    d_terms = pair_rows(order(y), after(d_pair, down_terms), products, w3)
    core_three = send(jnp.concatenate([x_cross, after(pair_z, *down_got)], axis=1), "c")
    pair_terms = outer(
        "pair_terms", order(x), [(x_keep, 0), (x_same, 0), (core_one, 0), (core_three, 0)],
        [(d_pair, 0), (pair_z, 0), (core_two, 2048), (core_three, 1024)], 256, 768,
    )
    down_last = lax.optimization_barrier((*down_last, pair_terms))[:2]
    pair_got, pair_out, pair_last = halve(after(pair_terms, *down_last), "x")
    d_w_gate, d_w_up = finish(pair_terms, pair_got, pair_last)
    down = finish(down_terms, down_got, down_last, (pair_terms,))
    d_w_down = jnp.concatenate(down, axis=1)
    lower = z_lo == 0
    theirs = jnp.where(lower, d_w_down[256:], d_w_down[:256]).astype(bf16)
    d_w_down = jnp.where(lower, d_w_down[:256], d_w_down[256:]) + send(theirs, "z^1").astype(f32)

    d_got, _, d_last = halve(d_terms, "y", down_got)
    d_low, d_high = finish(d_terms, d_got, d_last)
    branch_terms = after(branch_terms, *d_last)
    branch_got, _, branch_last = halve(branch_terms, "y", (pair_terms,))
    low, high = finish(branch_terms, branch_got, branch_last)
    upper = z_hi == 1
    mine = jnp.where(upper, d_high, d_low)
    theirs = send(jnp.where(upper, d_low, d_high).astype(bf16), "z+2")
    mine = after(mine, pair_terms) + theirs.astype(f32)
    theirs = send(after(jnp.where(upper, low, high).astype(bf16), theirs), "z+2")
    branch = (jnp.where(upper, high, low) + theirs.astype(f32)).astype(bf16)
    d_normed, products = mine[:, :512], mine[:, 512:513] / width

    x_own = inputs.astype(f32)
    d_input = (d_normed * gain.astype(f32) - inv[:, :1] * products * x_own).astype(bf16)
    d_gain = jnp.sum(d_normed * x_own, axis=0, keepdims=True)
    for move in ("c", "z^1", "x^1", "x+2"):
        if move == "x^1":
            d_gain = after(d_gain, *pair_out)
        d_gain = d_gain + send(d_gain, move)

    gain_rows = lax.dynamic_slice(gains, (0, s * 256), (1, 256)).astype(f32).reshape(256, 1)
    d_weights = jnp.stack(
        [(d_w_gate * gain_rows).astype(bf16), (d_w_up * gain_rows).astype(bf16), d_w_down.astype(bf16)], axis=1
    )
    return (branch, d_input, d_gain.reshape(512), d_weights)


def solution(mesh):
    in_specs = (P("seq", "tensor"), P("tensor"), P(None, None, "tensor"), P("seq", "tensor"))
    out_specs = (P("seq", "tensor"), P("seq", "tensor"), P("tensor"), P("seq", None, "tensor"))
    return jax.shard_map(local, mesh=mesh, in_specs=in_specs, out_specs=out_specs, check_vma=False)
```

```python
import functools
import jax
import jax.numpy as jnp
from jax import lax
from jax.experimental import pallas as pl
from jax.experimental.pallas import tpu as pltpu
from jax.sharding import PartitionSpec as P

norm_eps = 1e-05
AXES = ("tensor", "seq")
f32 = jnp.float32
bf16 = jnp.bfloat16
MiB = 1 << 20


def flat(x, y, z, c):
    x, y, z = x % 4, y % 4, z % 4
    return ((z // 2) * 4 + y) * 16 + (x * 2 + z % 2) * 2 + c


def pairs(move):
    places = [(x, y, z, c) for x in range(4) for y in range(4) for z in range(4) for c in range(2)]
    return [(flat(*place), flat(*move(*place))) for place in places]


moves = {
    "x^1": lambda x, y, z, c: (x ^ 1, y, z, c),
    "x^3": lambda x, y, z, c: (x ^ 3, y, z, c),
    "x+2": lambda x, y, z, c: (x + 2, y, z, c),
    "y+": lambda x, y, z, c: (x, y + 1, z, c),
    "y-": lambda x, y, z, c: (x, y - 1, z, c),
    "y^1": lambda x, y, z, c: (x, y ^ 1, z, c),
    "y^3": lambda x, y, z, c: (x, y ^ 3, z, c),
    "z+2": lambda x, y, z, c: (x, y, z + 2, c),
    "z^1": lambda x, y, z, c: (x, y, z ^ 1, c),
    "z^3": lambda x, y, z, c: (x, y, z ^ 3, c),
    "z^3c": lambda x, y, z, c: (x, y, z ^ 3, 1 - c),
    "c": lambda x, y, z, c: (x, y, z, 1 - c),
}


def send(value, move):
    return lax.ppermute(value, AXES, pairs(moves[move]))


def after(value, *done):
    return lax.optimization_barrier((value, *done))[0]


def rows_cat(*parts):
    return jnp.concatenate(parts, axis=0)


def dot(a, b):
    return jnp.dot(a, b, preferred_element_type=f32)


def dot_nt(a, b):
    return lax.dot_general(a, b, (((1,), (1,)), ((), ())), preferred_element_type=f32)


def dot_tn(a, b):
    return lax.dot_general(a, b, (((0,), (0,)), ((), ())), preferred_element_type=f32)


def call(body, name, shapes, scratch, limit, flops, size, args, hbm=(), scalars=1):
    spaces = [pltpu.SMEM] * scalars + [pltpu.HBM if i in hbm else pltpu.VMEM for i in range(scalars, len(args))]
    return pl.pallas_call(
        body,
        in_specs=[pl.BlockSpec(memory_space=space) for space in spaces],
        out_specs=[pl.BlockSpec(memory_space=pltpu.VMEM) for _ in shapes],
        out_shape=[jax.ShapeDtypeStruct(shape, dtype) for shape, dtype in shapes],
        scratch_shapes=scratch,
        compiler_params=pltpu.CompilerParams(vmem_limit_bytes=limit * MiB),
        cost_estimate=pl.CostEstimate(flops=flops, bytes_accessed=size, transcendentals=0),
        name=name,
    )(*args)


def lane(at, size, unit):
    return pl.ds(pl.multiple_of(at, unit), size)


def put(buf, spot, pieces):
    for dz, dy, row, ref, first, rows in pieces:
        buf[row:row + rows, lane(spot[dz * 4 + dy] * 512, 512, 512)] = ref[first:first + rows, :]


def fetch(w, held, sems, first, count, block_of):
    copies = []
    for k in range(8):
        rows = pl.ds(pl.multiple_of(block_of(k) * 512, 512), 512)
        copies.append(pltpu.make_async_copy(w.at[pl.ds(first, count), rows, :], held.at[k], sems.at[k]))
        copies[-1].start()
    return copies


def assemble_body(spot, own, below, above, other, up2, down2, other_far, full, keep, core_out, z_out, cross_out):
    put(full, spot, [
        (0, 0, 0, own, 0, 272), (0, 3, 0, below, 0, 272), (0, 1, 0, above, 0, 272), (1, 0, 0, other, 0, 272),
        (0, 2, 0, up2, 0, 128), (1, 3, 0, up2, 128, 272), (0, 2, 128, down2, 0, 144), (1, 1, 0, down2, 144, 272),
        (1, 2, 0, other_far, 0, 272),
    ])
    z_lo, core = spot[8], spot[9]
    for i in range(4):
        for ref, zl, c in ((keep, z_lo, core), (core_out, z_lo, 1 - core), (z_out, 1 - z_lo, core),
                           (cross_out, 1 - z_lo, 1 - core)):
            ref[:, i * 256:(i + 1) * 256] = full[0:256, lane((2 * i + zl) * 512 + c * 256, 256, 256)]


def assemble(spot, pieces):
    shapes = [((272, 4096), bf16)] + [((256, 1024), bf16)] * 4
    return call(assemble_body, "assemble", shapes, [], 4, 0, 8 * MiB, (spot, *pieces))


def forward_body(x_ref, x_core, w, gate, up, hidden, inv, core_out, held, sems):
    copies = fetch(w, held, sems, 0, 2, lambda k: k)
    squares = jnp.zeros((256, 1), f32)
    for k in range(8):
        copies[k].wait()
        cols = slice(k * 512, (k + 1) * 512)
        x = x_ref[0:256, cols].astype(f32)
        squares = squares + jnp.sum(x * x, axis=1, keepdims=True)
        scaled = (x * x_ref[256:272, cols][0:1].astype(f32)).astype(bf16)
        for ref, j in ((gate, 0), (up, 1)):
            value = dot(scaled, held[k, j])
            ref[...] = value if k == 0 else ref[...] + value
    inv_rms = lax.rsqrt(squares / 4096 + norm_eps)
    g = gate[...] * inv_rms
    u = up[...] * inv_rms
    gate[...] = g
    up[...] = u
    hidden[...] = (g * jax.nn.sigmoid(g) * u).astype(bf16)
    core_out[:, 0:1024] = x_core[...]
    core_out[:, 1024:1792] = hidden[...]
    inv[...] = jnp.broadcast_to(inv_rms, (256, 128))


def forward(x_full, x_core, w3):
    shapes = [((256, 768), f32), ((256, 768), f32), ((256, 768), bf16), ((256, 128), f32), ((256, 1792), bf16)]
    scratch = [pltpu.VMEM((8, 2, 512, 768), bf16), pltpu.SemaphoreType.DMA((8,))]
    return call(forward_body, "forward", shapes, scratch, 18, 2 * 256 * 4096 * 1536, 16 * MiB,
                (x_full, x_core, w3), hbm=(2,), scalars=0)


def backward_body(spot, both, below, above, low, high, w, gate, up_val, inv, pair, products, mine, core_out, buf, acc,
                  held, sems):
    copies = fetch(w, held, sems, 2, 1, lambda k: k)
    put(buf, spot, [
        (0, 0, 0, both, 0, 256), (1, 0, 0, both, 256, 256), (0, 3, 0, below, 0, 256), (1, 3, 0, below, 256, 256),
        (0, 1, 0, above, 0, 256), (1, 1, 0, above, 256, 256), (0, 2, 0, low, 0, 128), (1, 2, 0, low, 128, 128),
        (0, 2, 128, high, 0, 128), (1, 2, 128, high, 128, 128),
    ])
    core = spot[9]
    for i in range(8):
        for ref, c in ((mine, core), (core_out, 1 - core)):
            ref[:, i * 256:(i + 1) * 256] = buf[:, lane(i * 512 + c * 256, 256, 256)]
    for k in range(8):
        copies[k].wait()
        value = dot(buf[:, k * 512:(k + 1) * 512], held[k, 0])
        acc[...] = value if k == 0 else acc[...] + value
    d_hidden = acc[...] * inv[:, 0:1]
    g, u = gate[...], up_val[...]
    sigma = jax.nn.sigmoid(g)
    d_gate = (d_hidden * u * sigma * (1.0 + g * (1.0 - sigma))).astype(bf16)
    d_up = (d_hidden * g * sigma).astype(bf16)
    pair[:, 0:768] = d_gate
    pair[:, 768:1536] = d_up
    core_out[:, 2048:2816] = d_gate
    core_out[:, 2816:3584] = d_up
    total = jnp.sum(d_gate.astype(f32) * g + d_up.astype(f32) * u, axis=1, keepdims=True)
    products[...] = jnp.broadcast_to(total, (256, 128)).astype(bf16)


def backward(spot, pieces, w3, gate, up, inv):
    shapes = [((256, 1536), bf16), ((256, 128), bf16), ((256, 2048), bf16), ((256, 3584), bf16)]
    scratch = [pltpu.VMEM((256, 4096), bf16), pltpu.VMEM((256, 768), f32), pltpu.VMEM((8, 1, 512, 768), bf16),
               pltpu.SemaphoreType.DMA((8,))]
    return call(backward_body, "backward", shapes, scratch, 15, 2 * 256 * 4096 * 768, 8 * MiB, (spot, *pieces, w3, gate, up, inv),
                hbm=(len(pieces) + 1,))


def outer_body(a_from, b_from, rows, cols, order, *refs):
    n = len(a_from)
    a_refs, b_refs, out = refs[:n], refs[n:2 * n], refs[2 * n]

    def step(i, carry):
        total = None
        for a, a0, b, b0 in zip(a_refs, a_from, b_refs, b_from):
            value = dot_tn(a[:, lane(order[i] * rows + a0, rows, 256)], b[:, lane(i // 4 * cols + b0, cols, 128)])
            total = value if total is None else total + value
        out[i] = total.astype(bf16)
        return carry

    lax.fori_loop(0, 8, step, 0)


def outer(name, order, a_list, b_list, rows, cols):
    body = functools.partial(outer_body, [f for _, f in a_list], [f for _, f in b_list], rows, cols)
    flops = 2 * 256 * len(a_list) * rows * 8 * cols
    return call(body, name, [((8, rows, cols), bf16)], [], 10, flops, 8 * MiB, (order, *[a for a, _ in a_list], *[b for b, _ in b_list]))[0]


def branch_rows_body(order, hidden, w, out, held, sems):
    copies = fetch(w, held, sems, 2, 1, lambda k: k // 4 * 4 + order[k])
    for k in range(8):
        copies[k].wait()
        out[k] = dot_nt(hidden[...], held[k, 0]).astype(bf16)


def branch_rows(order, hidden, w3):
    scratch = [pltpu.VMEM((8, 1, 512, 768), bf16), pltpu.SemaphoreType.DMA((8,))]
    return call(branch_rows_body, "branch_rows", [((8, 256, 512), bf16)], scratch, 8, 2 * 256 * 768 * 4096, 8 * MiB,
                (order, hidden, w3), hbm=(2,))[0]


def pair_rows_body(order, pair, products, w, out, held, sems):
    copies = fetch(w, held, sems, 0, 2, lambda k: k // 4 * 4 + order[k])
    for k in range(8):
        copies[k].wait()
        value = dot_nt(pair[:, 0:768], held[k, 0]) + dot_nt(pair[:, 768:1536], held[k, 1])
        out[k, :, 0:512] = value.astype(bf16)
        out[k, :, 512:640] = products[...]


def pair_rows(order, pair, products, w3):
    scratch = [pltpu.VMEM((8, 2, 512, 768), bf16), pltpu.SemaphoreType.DMA((8,))]
    return call(pair_rows_body, "pair_rows", [((8, 256, 640), bf16)], scratch, 15, 2 * 256 * 1536 * 4096, 16 * MiB,
                (order, pair, products, w3), hbm=(3,))[0]


def first_two(terms):
    return [terms[4 * h:4 * h + 2].reshape(2 * terms.shape[1], terms.shape[2]) for h in (0, 1)]


def second_step(terms, got, axis, done=()):
    rows = terms.shape[1]
    two, six, *got = lax.optimization_barrier((terms[2], terms[6], *got, *done))[:4]
    out = [(t.astype(f32) + g[rows:].astype(f32)).astype(bf16) for t, g in zip((two, six), got)]
    return out, [send(o, axis + move) for o, move in zip(out, ("^3", "^1"))]


def halve(terms, axis, done=()):
    got = [send(value, axis + move) for value, move in zip(first_two(terms), ("^1", "^3"))]
    return (got, *second_step(terms, got, axis, done))


def finish(terms, got, last, done=()):
    three, seven = lax.optimization_barrier((terms[3], terms[7], *done))[:2]
    rows = terms.shape[1]
    return [t.astype(f32) + g[:rows].astype(f32) + e.astype(f32) for t, g, e in zip((three, seven), got, last)]


def gather_both(own, cot):
    below, above, other = send(own, "y+"), send(own, "y-"), send(own, "z+2")
    up = send(rows_cat(below[:128], other), "y+")
    down = send(rows_cat(above[128:], other), "y-")
    cot_other = send(after(cot, other), "z+2")
    other_far = send(after(rows_cat(up[:128], down[:144]), cot_other), "z+2")
    both = after(rows_cat(cot, cot_other), up, down)
    cot_below, cot_above = send(both, "y+"), send(both, "y-")
    low = send(rows_cat(cot_below[:128], cot_below[256:384]), "y+")
    high = send(rows_cat(cot_above[128:256], cot_above[384:]), "y-")
    return (own, below, above, other, up, down, other_far), (both, cot_below, cot_above, low, high)


def local(inputs, gain, weights, d_out):
    width = weights.shape[0]
    t, s = lax.axis_index("tensor"), lax.axis_index("seq")
    z_hi, y = t // 4, t % 4
    x, z_lo, core = s // 4, s // 2 % 2, s % 2
    w3 = pltpu.with_memory_space_constraint(jnp.transpose(weights, (1, 0, 2)), pltpu.HBM)
    spot = jnp.stack(
        [(z_hi + dz) % 2 * 4 + (y + dy) % 4 for dz in (0, 1) for dy in range(4)] + [z_lo, core]
    ).astype(jnp.int32)

    def order(at):
        return jnp.stack([at ^ 1, at ^ 2, at ^ 3, at, at ^ 3, at ^ 2, at ^ 1, at]).astype(jnp.int32)

    own = rows_cat(inputs, jnp.broadcast_to(gain.reshape(1, 512), (16, 512)))
    x_pieces, cot_pieces = gather_both(own, d_out)
    x_full, x_keep, x_core, x_same, x_cross = assemble(spot, x_pieces)
    x_same, x_cross = send(x_same, "z^3"), send(x_cross, "z^1")
    gate, up_val, hidden, inv, core_one = forward(after(x_full, *cot_pieces[1:3]), x_core, w3)
    core_one = send(core_one, "c")
    cot_pieces = (after(cot_pieces[0], x_same, x_cross), *cot_pieces[1:])
    d_pair, products, cot_mine, core_two = backward(spot, cot_pieces, w3, gate, up_val, inv)
    core_two = send(core_two, "c")
    branch_terms = branch_rows(order(y), after(hidden, d_pair), w3)
    pair_z = send(d_pair, "z^1")
    down_terms = outer("down_terms", order(x), [(after(cot_mine, branch_terms), 0), (core_two, 0)], [(hidden, 0), (core_one, 1024)], 512, 384)
    branch_got = [send(value, move) for value, move in zip(first_two(branch_terms), ("y^1", "y^3"))]
    d_terms = pair_rows(order(y), after(d_pair, down_terms, *branch_got), products, w3)
    down_got, _, down_last = halve(down_terms, "x")
    d_got, _, d_last = halve(d_terms, "y", down_got)
    core_three = send(jnp.concatenate([x_cross, after(pair_z, *down_got, *d_got)], axis=1), "c")
    pair_terms = outer(
        "pair_terms", order(x), [(x_keep, 0), (x_same, 0), (core_one, 0), (core_three, 0)],
        [(d_pair, 0), (pair_z, 0), (core_two, 2048), (core_three, 1024)], 256, 768,
    )
    down_last = lax.optimization_barrier((*down_last, pair_terms))[:2]
    pair_got, pair_out, pair_last = halve(after(pair_terms, *down_last), "x")
    d_w_gate, d_w_up = finish(pair_terms, pair_got, pair_last)
    down = finish(down_terms, down_got, down_last, (pair_terms,))
    d_w_down = jnp.concatenate(down, axis=1)
    lower = z_lo == 0
    theirs = jnp.where(lower, d_w_down[256:], d_w_down[:256]).astype(bf16)
    d_w_down = jnp.where(lower, d_w_down[:256], d_w_down[256:]) + send(theirs, "z^1").astype(f32)

    d_last = lax.optimization_barrier((*d_last, pair_terms))[:2]
    d_low, d_high = finish(d_terms, d_got, d_last)
    _, branch_last = second_step(branch_terms, branch_got, "y", (pair_terms, *d_last))
    low, high = finish(branch_terms, branch_got, branch_last)
    upper = z_hi == 1
    mine = jnp.where(upper, d_high, d_low)
    theirs = send(jnp.where(upper, d_low, d_high).astype(bf16), "z+2")
    mine = after(mine, pair_terms) + theirs.astype(f32)
    theirs = send(after(jnp.where(upper, low, high).astype(bf16), theirs), "z+2")
    branch = (jnp.where(upper, high, low) + theirs.astype(f32)).astype(bf16)
    d_normed, products = mine[:, :512], mine[:, 512:513] / width

    x_own = inputs.astype(f32)
    d_input = (d_normed * gain.astype(f32) - inv[:, :1] * products * x_own).astype(bf16)
    d_gain = jnp.sum(d_normed * x_own, axis=0, keepdims=True)
    for move in ("c", "z^1", "x^1", "x+2"):
        if move == "x^1":
            d_gain = after(d_gain, *pair_out)
        d_gain = d_gain + send(d_gain, move)

    gain_rows = lax.dynamic_slice(x_full, (256, s * 256), (1, 256)).astype(f32).reshape(256, 1)
    d_weights = jnp.stack(
        [(d_w_gate * gain_rows).astype(bf16), (d_w_up * gain_rows).astype(bf16), d_w_down.astype(bf16)], axis=1
    )
    return (branch, d_input, d_gain.reshape(512), d_weights)


def solution(mesh):
    in_specs = (P("seq", "tensor"), P("tensor"), P(None, None, "tensor"), P("seq", "tensor"))
    out_specs = (P("seq", "tensor"), P("seq", "tensor"), P("tensor"), P("seq", None, "tensor"))
    return jax.shard_map(local, mesh=mesh, in_specs=in_specs, out_specs=out_specs, check_vma=False)
```

```python
import functools
import jax
import jax.numpy as jnp
from jax import lax
from jax.experimental import pallas as pl
from jax.experimental.pallas import tpu as pltpu
from jax.sharding import PartitionSpec as P

norm_eps = 1e-05
AXES = ("tensor", "seq")
f32 = jnp.float32
bf16 = jnp.bfloat16
MiB = 1 << 20


def flat(x, y, z, c):
    x, y, z = x % 4, y % 4, z % 4
    return ((z // 2) * 4 + y) * 16 + (x * 2 + z % 2) * 2 + c


def pairs(move):
    places = [(x, y, z, c) for x in range(4) for y in range(4) for z in range(4) for c in range(2)]
    return [(flat(*place), flat(*move(*place))) for place in places]


moves = {
    "x^1": lambda x, y, z, c: (x ^ 1, y, z, c),
    "x^3": lambda x, y, z, c: (x ^ 3, y, z, c),
    "x+2": lambda x, y, z, c: (x + 2, y, z, c),
    "y+": lambda x, y, z, c: (x, y + 1, z, c),
    "y-": lambda x, y, z, c: (x, y - 1, z, c),
    "y^1": lambda x, y, z, c: (x, y ^ 1, z, c),
    "y^3": lambda x, y, z, c: (x, y ^ 3, z, c),
    "z+2": lambda x, y, z, c: (x, y, z + 2, c),
    "z^1": lambda x, y, z, c: (x, y, z ^ 1, c),
    "z^3": lambda x, y, z, c: (x, y, z ^ 3, c),
    "z^3c": lambda x, y, z, c: (x, y, z ^ 3, 1 - c),
    "c": lambda x, y, z, c: (x, y, z, 1 - c),
}


def send(value, move):
    return lax.ppermute(value, AXES, pairs(moves[move]))


def after(value, *done):
    return lax.optimization_barrier((value, *done))[0]


def rows_cat(*parts):
    return jnp.concatenate(parts, axis=0)


def dot(a, b):
    return jnp.dot(a, b, preferred_element_type=f32)


def dot_nt(a, b):
    return lax.dot_general(a, b, (((1,), (1,)), ((), ())), preferred_element_type=f32)


def dot_tn(a, b):
    return lax.dot_general(a, b, (((0,), (0,)), ((), ())), preferred_element_type=f32)


def call(body, name, shapes, scratch, limit, flops, size, args, hbm=(), scalars=1, direct=()):
    loads = [i for i in range(scalars, len(args)) if i not in hbm and i not in direct]
    spaces = [pltpu.SMEM] * scalars + [
        pltpu.HBM if i in hbm else pltpu.VMEM if i in direct else pl.ANY for i in range(scalars, len(args))
    ]

    def whole(*refs):
        ins, rest = list(refs[:len(args)]), refs[len(args):]
        outs, rest = rest[:len(shapes)], rest[len(shapes):]
        own, rest = rest[:len(scratch)], rest[len(scratch):]
        copies = []
        for n, i in enumerate(loads):
            copies.append(pltpu.make_async_copy(ins[i], rest[n], rest[-1].at[n]))
            copies[-1].start()
            ins[i] = rest[n]

        def ready():
            for copy in copies:
                copy.wait()

        body(ready, *ins, *outs, *own)

    held = [pltpu.VMEM(args[i].shape, args[i].dtype) for i in loads] + [pltpu.SemaphoreType.DMA((max(len(loads), 1),))]
    return pl.pallas_call(
        whole,
        in_specs=[pl.BlockSpec(memory_space=space) for space in spaces],
        out_specs=[pl.BlockSpec(memory_space=pltpu.VMEM) for _ in shapes],
        out_shape=[jax.ShapeDtypeStruct(shape, dtype) for shape, dtype in shapes],
        scratch_shapes=list(scratch) + held,
        compiler_params=pltpu.CompilerParams(vmem_limit_bytes=limit * MiB),
        cost_estimate=pl.CostEstimate(flops=flops, bytes_accessed=size, transcendentals=0),
        name=name,
    )(*args)


def lane(at, size, unit):
    return pl.ds(pl.multiple_of(at, unit), size)


def put(buf, spot, pieces):
    for dz, dy, row, ref, first, rows in pieces:
        buf[row:row + rows, lane(spot[dz * 4 + dy] * 512, 512, 512)] = ref[first:first + rows, :]


def fetch(w, held, sems, first, count, block_of):
    copies = []
    for k in range(8):
        rows = pl.ds(pl.multiple_of(block_of(k) * 512, 512), 512)
        copies.append(pltpu.make_async_copy(w.at[pl.ds(first, count), rows, :], held.at[k], sems.at[k]))
        copies[-1].start()
    return copies


def assemble_body(ready, spot, own, below, above, other, up2, down2, other_far, full, gains, keep, core_out, z_out,
                  cross_out):
    put(full, spot, [
        (0, 0, 0, own, 0, 272), (0, 3, 0, below, 0, 272), (0, 1, 0, above, 0, 272), (1, 0, 0, other, 0, 272),
        (0, 2, 0, up2, 0, 128), (1, 3, 0, up2, 128, 272), (0, 2, 128, down2, 0, 144), (1, 1, 0, down2, 144, 272),
        (1, 2, 0, other_far, 0, 272),
    ])
    gains[...] = full[256:272, :]
    z_lo, core = spot[8], spot[9]
    for i in range(4):
        for ref, zl, c in ((keep, z_lo, core), (core_out, z_lo, 1 - core), (z_out, 1 - z_lo, core),
                           (cross_out, 1 - z_lo, 1 - core)):
            ref[:, i * 256:(i + 1) * 256] = full[0:256, lane((2 * i + zl) * 512 + c * 256, 256, 256)]


def assemble(spot, pieces):
    shapes = [((272, 4096), bf16), ((16, 4096), bf16)] + [((256, 1024), bf16)] * 4
    return call(assemble_body, "assemble", shapes, [], 4, 0, 8 * MiB, (spot, *pieces), direct=range(1, 8))


def forward_body(ready, x_ref, x_core, w, gate, up, hidden, inv, core_out, held, sems):
    copies = fetch(w, held, sems, 0, 2, lambda k: k)
    squares = jnp.zeros((256, 1), f32)
    ready()
    for k in range(8):
        copies[k].wait()
        cols = slice(k * 512, (k + 1) * 512)
        x = x_ref[0:256, cols].astype(f32)
        squares = squares + jnp.sum(x * x, axis=1, keepdims=True)
        scaled = (x * x_ref[256:272, cols][0:1].astype(f32)).astype(bf16)
        for ref, j in ((gate, 0), (up, 1)):
            value = dot(scaled, held[k, j])
            ref[...] = value if k == 0 else ref[...] + value
    inv_rms = lax.rsqrt(squares / 4096 + norm_eps)
    g = gate[...] * inv_rms
    u = up[...] * inv_rms
    gate[...] = g
    up[...] = u
    hidden[...] = (g * jax.nn.sigmoid(g) * u).astype(bf16)
    core_out[:, 0:1024] = x_core[...]
    core_out[:, 1024:1792] = hidden[...]
    inv[...] = jnp.broadcast_to(inv_rms, (256, 128))


def forward(x_full, x_core, w3):
    shapes = [((256, 768), f32), ((256, 768), f32), ((256, 768), bf16), ((256, 128), f32), ((256, 1792), bf16)]
    scratch = [pltpu.VMEM((8, 2, 512, 768), bf16), pltpu.SemaphoreType.DMA((8,))]
    return call(forward_body, "forward", shapes, scratch, 18, 2 * 256 * 4096 * 1536, 16 * MiB,
                (x_full, x_core, w3), hbm=(2,), scalars=0, direct=(0,))


def backward_body(ready, spot, both, below, above, low, high, w, gate, up_val, inv, pair, products, mine, core_out, buf, acc,
                  held, sems):
    copies = fetch(w, held, sems, 2, 1, lambda k: k)
    put(buf, spot, [
        (0, 0, 0, both, 0, 256), (1, 0, 0, both, 256, 256), (0, 3, 0, below, 0, 256), (1, 3, 0, below, 256, 256),
        (0, 1, 0, above, 0, 256), (1, 1, 0, above, 256, 256), (0, 2, 0, low, 0, 128), (1, 2, 0, low, 128, 128),
        (0, 2, 128, high, 0, 128), (1, 2, 128, high, 128, 128),
    ])
    core = spot[9]
    for i in range(8):
        for ref, c in ((mine, core), (core_out, 1 - core)):
            ref[:, i * 256:(i + 1) * 256] = buf[:, lane(i * 512 + c * 256, 256, 256)]
    for k in range(8):
        copies[k].wait()
        value = dot(buf[:, k * 512:(k + 1) * 512], held[k, 0])
        acc[...] = value if k == 0 else acc[...] + value
    ready()
    d_hidden = acc[...] * inv[:, 0:1]
    g, u = gate[...], up_val[...]
    sigma = jax.nn.sigmoid(g)
    d_gate = (d_hidden * u * sigma * (1.0 + g * (1.0 - sigma))).astype(bf16)
    d_up = (d_hidden * g * sigma).astype(bf16)
    pair[:, 0:768] = d_gate
    pair[:, 768:1536] = d_up
    core_out[:, 2048:2816] = d_gate
    core_out[:, 2816:3584] = d_up
    total = jnp.sum(d_gate.astype(f32) * g + d_up.astype(f32) * u, axis=1, keepdims=True)
    products[...] = jnp.broadcast_to(total, (256, 128)).astype(bf16)


def backward(spot, pieces, w3, gate, up, inv):
    shapes = [((256, 1536), bf16), ((256, 128), bf16), ((256, 2048), bf16), ((256, 3584), bf16)]
    scratch = [pltpu.VMEM((256, 4096), bf16), pltpu.VMEM((256, 768), f32), pltpu.VMEM((8, 1, 512, 768), bf16),
               pltpu.SemaphoreType.DMA((8,))]
    return call(backward_body, "backward", shapes, scratch, 16, 2 * 256 * 4096 * 768, 8 * MiB, (spot, *pieces, w3, gate, up, inv),
                hbm=(6,), direct=range(1, 6))


def store(outs, k, value):
    half, i = k // 4, k % 4
    if i < 2:
        rows = value.shape[0]
        outs[half][i * rows:(i + 1) * rows, :] = value
    else:
        outs[2 * i - 2 + half][...] = value


def halving_shapes(rows, cols):
    return [((2 * rows, cols), bf16)] * 2 + [((rows, cols), bf16)] * 4


def outer_body(a_from, b_from, rows, cols, ready, order, *refs):
    n = len(a_from)
    a_refs, b_refs, outs = refs[:n], refs[n:2 * n], refs[2 * n:]
    ready()
    for k in range(8):
        total = None
        for a, a0, b, b0 in zip(a_refs, a_from, b_refs, b_from):
            b0 = k // 4 * cols + b0
            value = dot_tn(a[:, lane(order[k] * rows + a0, rows, 256)], b[:, b0:b0 + cols])
            total = value if total is None else total + value
        store(outs, k, total.astype(bf16))


def outer(name, order, a_list, b_list, rows, cols):
    body = functools.partial(outer_body, [f for _, f in a_list], [f for _, f in b_list], rows, cols)
    flops = 2 * 256 * len(a_list) * rows * 8 * cols
    return call(body, name, halving_shapes(rows, cols), [], 16, flops, 8 * MiB,
                (order, *[a for a, _ in a_list], *[b for b, _ in b_list]))


def branch_rows_body(ready, order, hidden, w, *refs):
    outs, held, sems = refs[:6], refs[6], refs[7]
    copies = fetch(w, held, sems, 2, 1, lambda k: k // 4 * 4 + order[k])
    ready()
    for k in range(8):
        copies[k].wait()
        store(outs, k, dot_nt(hidden[...], held[k, 0]).astype(bf16))


def branch_rows(order, hidden, w3):
    scratch = [pltpu.VMEM((8, 1, 512, 768), bf16), pltpu.SemaphoreType.DMA((8,))]
    return call(branch_rows_body, "branch_rows", halving_shapes(256, 512), scratch, 10, 2 * 256 * 768 * 4096, 8 * MiB,
                (order, hidden, w3), hbm=(2,))


def pair_rows_body(ready, order, pair, products, w, *refs):
    outs, held, sems = refs[:6], refs[6], refs[7]
    copies = fetch(w, held, sems, 0, 2, lambda k: k // 4 * 4 + order[k])
    ready()
    for k in range(8):
        copies[k].wait()
        value = dot_nt(pair[:, 0:768], held[k, 0]) + dot_nt(pair[:, 768:1536], held[k, 1])
        store(outs, k, jnp.concatenate([value.astype(bf16), products[...]], axis=1))


def pair_rows(order, pair, products, w3):
    scratch = [pltpu.VMEM((8, 2, 512, 768), bf16), pltpu.SemaphoreType.DMA((8,))]
    return call(pair_rows_body, "pair_rows", halving_shapes(256, 640), scratch, 16, 2 * 256 * 1536 * 4096, 16 * MiB,
                (order, pair, products, w3), hbm=(3,))


def second_step(terms, got, axis, done=()):
    rows = terms[2].shape[0]
    two, six, *got = lax.optimization_barrier((terms[2], terms[3], *got, *done))[:4]
    out = [(t.astype(f32) + g[rows:].astype(f32)).astype(bf16) for t, g in zip((two, six), got)]
    return out, [send(o, axis + move) for o, move in zip(out, ("^3", "^1"))]


def halve(terms, axis, done=()):
    got = [send(value, axis + move) for value, move in zip(terms[0:2], ("^1", "^3"))]
    return (got, *second_step(terms, got, axis, done))


def finish(terms, got, last, done=()):
    low, high = lax.optimization_barrier((terms[4], terms[5], *done))[:2]
    rows = terms[4].shape[0]
    return [t.astype(f32) + g[:rows].astype(f32) + e.astype(f32) for t, g, e in zip((low, high), got, last)]


def gather_both(own, cot):
    below, above, other = send(own, "y+"), send(own, "y-"), send(own, "z+2")
    up = send(rows_cat(below[:128], other), "y+")
    down = send(rows_cat(above[128:], other), "y-")
    cot_other = send(after(cot, other), "z+2")
    other_far = send(after(rows_cat(up[:128], down[:144]), cot_other), "z+2")
    both = after(rows_cat(cot, cot_other), up, down)
    cot_below, cot_above = send(both, "y+"), send(both, "y-")
    low = send(rows_cat(cot_below[:128], cot_below[256:384]), "y+")
    high = send(rows_cat(cot_above[128:256], cot_above[384:]), "y-")
    return (own, below, above, other, up, down, other_far), (both, cot_below, cot_above, low, high)


def local(inputs, gain, weights, d_out):
    width = weights.shape[0]
    t, s = lax.axis_index("tensor"), lax.axis_index("seq")
    z_hi, y = t // 4, t % 4
    x, z_lo, core = s // 4, s // 2 % 2, s % 2
    w3 = pltpu.with_memory_space_constraint(jnp.transpose(weights, (1, 0, 2)), pltpu.HBM)
    spot = jnp.stack(
        [(z_hi + dz) % 2 * 4 + (y + dy) % 4 for dz in (0, 1) for dy in range(4)] + [z_lo, core]
    ).astype(jnp.int32)

    def order(at):
        return jnp.stack([at ^ 1, at ^ 2, at ^ 3, at, at ^ 3, at ^ 2, at ^ 1, at]).astype(jnp.int32)

    own = rows_cat(inputs, jnp.broadcast_to(gain.reshape(1, 512), (16, 512)))
    x_pieces, cot_pieces = gather_both(own, d_out)
    x_full, gains, x_keep, x_core, x_same, x_cross = assemble(spot, x_pieces)
    x_same, x_cross = send(x_same, "z^3"), send(x_cross, "z^1")
    gate, up_val, hidden, inv, core_one = forward(after(x_full, *cot_pieces[1:3]), x_core, w3)
    core_one = send(core_one, "c")
    cot_pieces = (after(cot_pieces[0], x_same, x_cross), *cot_pieces[1:])
    d_pair, products, cot_mine, core_two = backward(spot, cot_pieces, w3, gate, up_val, inv)
    core_two = send(core_two, "c")
    branch_terms = branch_rows(order(y), after(hidden, d_pair), w3)
    pair_z = send(d_pair, "z^1")
    down_terms = outer("down_terms", order(x), [(after(cot_mine, branch_terms[0]), 0), (core_two, 0)], [(hidden, 0), (core_one, 1024)], 512, 384)
    branch_got = [send(value, move) for value, move in zip(branch_terms[0:2], ("y^1", "y^3"))]
    d_terms = pair_rows(order(y), after(d_pair, down_terms[0]), products, w3)
    down_got, _, down_last = halve(down_terms, "x")
    d_terms = lax.optimization_barrier((*d_terms, *branch_got))[:6]
    d_got = [send(value, move) for value, move in zip(d_terms[0:2], ("y^1", "y^3"))]
    core_three = send(jnp.concatenate([x_cross, after(pair_z, d_terms[0], *down_got)], axis=1), "c")
    pair_terms = outer(
        "pair_terms", order(x), [(x_keep, 0), (x_same, 0), (core_one, 0), (core_three, 0)],
        [(d_pair, 0), (pair_z, 0), (core_two, 2048), (core_three, 1024)], 256, 768,
    )
    down_last = lax.optimization_barrier((*down_last, pair_terms[0]))[:2]
    pair_terms = lax.optimization_barrier((*pair_terms, *down_last))[:6]
    pair_got, pair_out, pair_last = halve(pair_terms, "x")
    d_w_gate, d_w_up = finish(pair_terms, pair_got, pair_last)
    down = finish(down_terms, down_got, down_last, (pair_terms[0],))
    d_w_down = jnp.concatenate(down, axis=1)
    lower = z_lo == 0
    theirs = jnp.where(lower, d_w_down[256:], d_w_down[:256]).astype(bf16)
    d_w_down = jnp.where(lower, d_w_down[:256], d_w_down[256:]) + send(theirs, "z^1").astype(f32)

    _, d_last = second_step(d_terms, d_got, "y", (pair_terms[0],))
    d_low, d_high = finish(d_terms, d_got, d_last)
    _, branch_last = second_step(branch_terms, branch_got, "y", (pair_terms[0], *d_last))
    low, high = finish(branch_terms, branch_got, branch_last)
    upper = z_hi == 1
    mine = jnp.where(upper, d_high, d_low)
    theirs = send(jnp.where(upper, d_low, d_high).astype(bf16), "z+2")
    mine = mine + theirs.astype(f32)
    theirs = send(after(jnp.where(upper, low, high).astype(bf16), theirs), "z+2")
    branch = (jnp.where(upper, high, low) + theirs.astype(f32)).astype(bf16)
    d_normed, products = mine[:, :512], mine[:, 512:513] / width

    x_own = inputs.astype(f32)
    d_input = (d_normed * gain.astype(f32) - inv[:, :1] * products * x_own).astype(bf16)
    d_gain = jnp.sum(d_normed * x_own, axis=0, keepdims=True)
    for move in ("c", "z^1", "x^1", "x+2"):
        if move == "x^1":
            d_gain = after(d_gain, *pair_out)
        d_gain = d_gain + send(d_gain, move)

    gain_rows = lax.dynamic_slice(gains, (0, s * 256), (1, 256)).astype(f32).reshape(256, 1)
    d_weights = jnp.stack(
        [(d_w_gate * gain_rows).astype(bf16), (d_w_up * gain_rows).astype(bf16), d_w_down.astype(bf16)], axis=1
    )
    return (branch, d_input, d_gain.reshape(512), d_weights)


def solution(mesh):
    in_specs = (P("seq", "tensor"), P("tensor"), P(None, None, "tensor"), P("seq", "tensor"))
    out_specs = (P("seq", "tensor"), P("seq", "tensor"), P("tensor"), P("seq", None, "tensor"))
    return jax.shard_map(local, mesh=mesh, in_specs=in_specs, out_specs=out_specs, check_vma=False)
```

```python
import functools
import jax
import jax.numpy as jnp
from jax import lax
from jax.experimental import pallas as pl
from jax.experimental.pallas import tpu as pltpu
from jax.sharding import PartitionSpec as P

norm_eps = 1e-05
AXES = ("tensor", "seq")
f32 = jnp.float32
bf16 = jnp.bfloat16
MiB = 1 << 20


def flat(x, y, z, c):
    x, y, z = x % 4, y % 4, z % 4
    return ((z // 2) * 4 + y) * 16 + (x * 2 + z % 2) * 2 + c


def pairs(move):
    places = [(x, y, z, c) for x in range(4) for y in range(4) for z in range(4) for c in range(2)]
    return [(flat(*place), flat(*move(*place))) for place in places]


moves = {
    "x^1": lambda x, y, z, c: (x ^ 1, y, z, c),
    "x^3": lambda x, y, z, c: (x ^ 3, y, z, c),
    "x+2": lambda x, y, z, c: (x + 2, y, z, c),
    "y+": lambda x, y, z, c: (x, y + 1, z, c),
    "y-": lambda x, y, z, c: (x, y - 1, z, c),
    "y^1": lambda x, y, z, c: (x, y ^ 1, z, c),
    "y^3": lambda x, y, z, c: (x, y ^ 3, z, c),
    "z+2": lambda x, y, z, c: (x, y, z + 2, c),
    "z^1": lambda x, y, z, c: (x, y, z ^ 1, c),
    "z^3": lambda x, y, z, c: (x, y, z ^ 3, c),
    "z^3c": lambda x, y, z, c: (x, y, z ^ 3, 1 - c),
    "c": lambda x, y, z, c: (x, y, z, 1 - c),
}


def send(value, move):
    return lax.ppermute(value, AXES, pairs(moves[move]))


def after(value, *done):
    return lax.optimization_barrier((value, *done))[0]


def rows_cat(*parts):
    return jnp.concatenate(parts, axis=0)


def dot(a, b):
    return jnp.dot(a, b, preferred_element_type=f32)


def dot_nt(a, b):
    return lax.dot_general(a, b, (((1,), (1,)), ((), ())), preferred_element_type=f32)


def dot_tn(a, b):
    return lax.dot_general(a, b, (((0,), (0,)), ((), ())), preferred_element_type=f32)


def call(body, name, shapes, scratch, limit, flops, size, args, hbm=(), scalars=1, direct=()):
    loads = [i for i in range(scalars, len(args)) if i not in hbm and i not in direct]
    spaces = [pltpu.SMEM] * scalars + [
        pltpu.HBM if i in hbm else pltpu.VMEM if i in direct else pl.ANY for i in range(scalars, len(args))
    ]

    def whole(*refs):
        ins, rest = list(refs[:len(args)]), refs[len(args):]
        outs, rest = rest[:len(shapes)], rest[len(shapes):]
        own, rest = rest[:len(scratch)], rest[len(scratch):]
        copies = []
        for n, i in enumerate(loads):
            copies.append(pltpu.make_async_copy(ins[i], rest[n], rest[-1].at[n]))
            copies[-1].start()
            ins[i] = rest[n]

        def ready():
            for copy in copies:
                copy.wait()

        body(ready, *ins, *outs, *own)

    held = [pltpu.VMEM(args[i].shape, args[i].dtype) for i in loads] + [pltpu.SemaphoreType.DMA((max(len(loads), 1),))]
    return pl.pallas_call(
        whole,
        in_specs=[pl.BlockSpec(memory_space=space) for space in spaces],
        out_specs=[pl.BlockSpec(memory_space=pltpu.VMEM) for _ in shapes],
        out_shape=[jax.ShapeDtypeStruct(shape, dtype) for shape, dtype in shapes],
        scratch_shapes=list(scratch) + held,
        compiler_params=pltpu.CompilerParams(vmem_limit_bytes=limit * MiB),
        cost_estimate=pl.CostEstimate(flops=flops, bytes_accessed=size, transcendentals=0),
        name=name,
    )(*args)


def lane(at, size, unit):
    return pl.ds(pl.multiple_of(at, unit), size)


def put(buf, spot, pieces):
    for dz, dy, row, ref, first, rows in pieces:
        buf[row:row + rows, lane(spot[dz * 4 + dy] * 512, 512, 512)] = ref[first:first + rows, :]


def fetch(w, held, sems, first, count, block_of):
    copies = []
    for k in range(8):
        rows = pl.ds(pl.multiple_of(block_of(k) * 512, 512), 512)
        copies.append(pltpu.make_async_copy(w.at[pl.ds(first, count), rows, :], held.at[k], sems.at[k]))
        copies[-1].start()
    return copies


def assemble_body(ready, spot, own, below, above, other, up2, down2, other_far, full, gains, keep, core_out, z_out,
                  cross_out):
    put(full, spot, [
        (0, 0, 0, own, 0, 272), (0, 3, 0, below, 0, 272), (0, 1, 0, above, 0, 272), (1, 0, 0, other, 0, 272),
        (0, 2, 0, up2, 0, 128), (1, 3, 0, up2, 128, 272), (0, 2, 128, down2, 0, 144), (1, 1, 0, down2, 144, 272),
        (1, 2, 0, other_far, 0, 272),
    ])
    gains[...] = full[256:272, :]
    z_lo, core = spot[8], spot[9]
    for i in range(4):
        for ref, zl, c in ((keep, z_lo, core), (core_out, z_lo, 1 - core), (z_out, 1 - z_lo, core),
                           (cross_out, 1 - z_lo, 1 - core)):
            ref[:, i * 256:(i + 1) * 256] = full[0:256, lane((2 * i + zl) * 512 + c * 256, 256, 256)]


def assemble(spot, pieces):
    shapes = [((272, 4096), bf16), ((16, 4096), bf16)] + [((256, 1024), bf16)] * 4
    return call(assemble_body, "assemble", shapes, [], 4, 0, 8 * MiB, (spot, *pieces), direct=range(1, 8))


def forward_body(ready, x_ref, x_core, w, gate, up, hidden, inv, core_out, held, sems):
    copies = fetch(w, held, sems, 0, 2, lambda k: k)
    squares = jnp.zeros((256, 1), f32)
    ready()
    for k in range(8):
        copies[k].wait()
        cols = slice(k * 512, (k + 1) * 512)
        x = x_ref[0:256, cols].astype(f32)
        squares = squares + jnp.sum(x * x, axis=1, keepdims=True)
        scaled = (x * x_ref[256:272, cols][0:1].astype(f32)).astype(bf16)
        for ref, j in ((gate, 0), (up, 1)):
            value = dot(scaled, held[k, j])
            ref[...] = value if k == 0 else ref[...] + value
    inv_rms = lax.rsqrt(squares / 4096 + norm_eps)
    g = gate[...] * inv_rms
    u = up[...] * inv_rms
    gate[...] = g
    up[...] = u
    hidden[...] = (g * jax.nn.sigmoid(g) * u).astype(bf16)
    core_out[:, 0:1024] = x_core[...]
    core_out[:, 1024:1792] = hidden[...]
    inv[...] = jnp.broadcast_to(inv_rms, (256, 128))


def forward(x_full, x_core, w3):
    shapes = [((256, 768), f32), ((256, 768), f32), ((256, 768), bf16), ((256, 128), f32), ((256, 1792), bf16)]
    scratch = [pltpu.VMEM((8, 2, 512, 768), bf16), pltpu.SemaphoreType.DMA((8,))]
    return call(forward_body, "forward", shapes, scratch, 18, 2 * 256 * 4096 * 1536, 16 * MiB,
                (x_full, x_core, w3), hbm=(2,), scalars=0, direct=(0,))


def backward_body(ready, spot, both, below, above, low, high, w, gate, up_val, inv, pair, products, mine, core_out, buf, acc,
                  held, sems):
    copies = fetch(w, held, sems, 2, 1, lambda k: k)
    put(buf, spot, [
        (0, 0, 0, both, 0, 256), (1, 0, 0, both, 256, 256), (0, 3, 0, below, 0, 256), (1, 3, 0, below, 256, 256),
        (0, 1, 0, above, 0, 256), (1, 1, 0, above, 256, 256), (0, 2, 0, low, 0, 128), (1, 2, 0, low, 128, 128),
        (0, 2, 128, high, 0, 128), (1, 2, 128, high, 128, 128),
    ])
    core = spot[9]
    for i in range(8):
        for ref, c in ((mine, core), (core_out, 1 - core)):
            ref[:, i * 256:(i + 1) * 256] = buf[:, lane(i * 512 + c * 256, 256, 256)]
    for k in range(8):
        copies[k].wait()
        value = dot(buf[:, k * 512:(k + 1) * 512], held[k, 0])
        acc[...] = value if k == 0 else acc[...] + value
    ready()
    d_hidden = acc[...] * inv[:, 0:1]
    g, u = gate[...], up_val[...]
    sigma = jax.nn.sigmoid(g)
    d_gate = (d_hidden * u * sigma * (1.0 + g * (1.0 - sigma))).astype(bf16)
    d_up = (d_hidden * g * sigma).astype(bf16)
    pair[:, 0:768] = d_gate
    pair[:, 768:1536] = d_up
    core_out[:, 2048:2816] = d_gate
    core_out[:, 2816:3584] = d_up
    total = jnp.sum(d_gate.astype(f32) * g + d_up.astype(f32) * u, axis=1, keepdims=True)
    products[...] = jnp.broadcast_to(total, (256, 128)).astype(bf16)


def backward(spot, pieces, w3, gate, up, inv):
    shapes = [((256, 1536), bf16), ((256, 128), bf16), ((256, 2048), bf16), ((256, 3584), bf16)]
    scratch = [pltpu.VMEM((256, 4096), bf16), pltpu.VMEM((256, 768), f32), pltpu.VMEM((8, 1, 512, 768), bf16),
               pltpu.SemaphoreType.DMA((8,))]
    return call(backward_body, "backward", shapes, scratch, 16, 2 * 256 * 4096 * 768, 8 * MiB, (spot, *pieces, w3, gate, up, inv),
                hbm=(6,), direct=range(1, 6))


def store(outs, k, value):
    half, i = k // 4, k % 4
    if i < 2:
        rows = value.shape[0]
        outs[half][i * rows:(i + 1) * rows, :] = value
    else:
        outs[2 * i - 2 + half][...] = value


def halving_shapes(rows, cols):
    return [((2 * rows, cols), bf16)] * 2 + [((rows, cols), bf16)] * 4


def outer_body(a_from, b_from, rows, cols, ready, order, *refs):
    n = len(a_from)
    a_refs, b_refs, outs = refs[:n], refs[n:2 * n], refs[2 * n:]
    ready()
    for k in range(8):
        total = None
        for a, a0, b, b0 in zip(a_refs, a_from, b_refs, b_from):
            b0 = k // 4 * cols + b0
            value = dot_tn(a[:, lane(order[k] * rows + a0, rows, 256)], b[:, b0:b0 + cols])
            total = value if total is None else total + value
        store(outs, k, total.astype(bf16))


def outer(name, order, a_list, b_list, rows, cols):
    body = functools.partial(outer_body, [f for _, f in a_list], [f for _, f in b_list], rows, cols)
    flops = 2 * 256 * len(a_list) * rows * 8 * cols
    return call(body, name, halving_shapes(rows, cols), [], 16, flops, 8 * MiB,
                (order, *[a for a, _ in a_list], *[b for b, _ in b_list]))


def branch_rows_body(ready, order, hidden, w, *refs):
    outs, held, sems = refs[:6], refs[6], refs[7]
    copies = fetch(w, held, sems, 2, 1, lambda k: k // 4 * 4 + order[k])
    ready()
    for k in range(8):
        copies[k].wait()
        store(outs, k, dot_nt(hidden[...], held[k, 0]).astype(bf16))


def branch_rows(order, hidden, w3):
    scratch = [pltpu.VMEM((8, 1, 512, 768), bf16), pltpu.SemaphoreType.DMA((8,))]
    return call(branch_rows_body, "branch_rows", halving_shapes(256, 512), scratch, 10, 2 * 256 * 768 * 4096, 8 * MiB,
                (order, hidden, w3), hbm=(2,))


def pair_rows_body(ready, order, pair, products, w, *refs):
    outs, held, sems = refs[:6], refs[6], refs[7]
    copies = fetch(w, held, sems, 0, 2, lambda k: k // 4 * 4 + order[k])
    ready()
    for k in range(8):
        copies[k].wait()
        value = dot_nt(pair[:, 0:768], held[k, 0]) + dot_nt(pair[:, 768:1536], held[k, 1])
        store(outs, k, jnp.concatenate([value.astype(bf16), products[...]], axis=1))


def pair_rows(order, pair, products, w3):
    scratch = [pltpu.VMEM((8, 2, 512, 768), bf16), pltpu.SemaphoreType.DMA((8,))]
    return call(pair_rows_body, "pair_rows", halving_shapes(256, 640), scratch, 16, 2 * 256 * 1536 * 4096, 16 * MiB,
                (order, pair, products, w3), hbm=(3,))


def second_step(terms, got, axis, done=()):
    rows = terms[2].shape[0]
    two, six, *got = lax.optimization_barrier((terms[2], terms[3], *got, *done))[:4]
    out = [(t.astype(f32) + g[rows:].astype(f32)).astype(bf16) for t, g in zip((two, six), got)]
    return out, [send(o, axis + move) for o, move in zip(out, ("^3", "^1"))]


def halve(terms, axis, done=()):
    got = [send(value, axis + move) for value, move in zip(terms[0:2], ("^1", "^3"))]
    return (got, *second_step(terms, got, axis, done))


def finish(terms, got, last, done=()):
    low, high = lax.optimization_barrier((terms[4], terms[5], *done))[:2]
    rows = terms[4].shape[0]
    return [t.astype(f32) + g[:rows].astype(f32) + e.astype(f32) for t, g, e in zip((low, high), got, last)]


def gather_both(own, cot):
    below, above, other = send(own, "y+"), send(own, "y-"), send(own, "z+2")
    up = send(rows_cat(below[:128], other), "y+")
    down = send(rows_cat(above[128:], other), "y-")
    cot_other = send(after(cot, other), "z+2")
    other_far = send(after(rows_cat(up[:128], down[:144]), cot_other), "z+2")
    both = after(rows_cat(cot, cot_other), up, down)
    cot_below, cot_above = send(both, "y+"), send(both, "y-")
    low = send(rows_cat(cot_below[:128], cot_below[256:384]), "y+")
    high = send(rows_cat(cot_above[128:256], cot_above[384:]), "y-")
    return (own, below, above, other, up, down, other_far), (both, cot_below, cot_above, low, high)


def local(inputs, gain, weights, d_out):
    width = weights.shape[0]
    t, s = lax.axis_index("tensor"), lax.axis_index("seq")
    z_hi, y = t // 4, t % 4
    x, z_lo, core = s // 4, s // 2 % 2, s % 2
    w3 = pltpu.with_memory_space_constraint(jnp.transpose(weights, (1, 0, 2)), pltpu.HBM)
    spot = jnp.stack(
        [(z_hi + dz) % 2 * 4 + (y + dy) % 4 for dz in (0, 1) for dy in range(4)] + [z_lo, core]
    ).astype(jnp.int32)

    def order(at):
        return jnp.stack([at ^ 1, at ^ 2, at ^ 3, at, at ^ 3, at ^ 2, at ^ 1, at]).astype(jnp.int32)

    own = rows_cat(inputs, jnp.broadcast_to(gain.reshape(1, 512), (16, 512)))
    x_pieces, cot_pieces = gather_both(own, d_out)
    x_full, gains, x_keep, x_core, x_same, x_cross = assemble(spot, x_pieces)
    x_same, x_cross = send(x_same, "z^3"), send(x_cross, "z^1")
    gate, up_val, hidden, inv, core_one = forward(after(x_full, *cot_pieces[1:3]), x_core, w3)
    core_one = send(core_one, "c")
    branch_terms = branch_rows(order(y), hidden, w3)
    cot_pieces = (after(cot_pieces[0], x_same, x_cross, branch_terms[0]), *cot_pieces[1:])
    d_pair, products, cot_mine, core_two = backward(spot, cot_pieces, w3, gate, up_val, inv)
    core_two = send(core_two, "c")
    pair_z = send(d_pair, "z^1")
    down_terms = outer("down_terms", order(x), [(cot_mine, 0), (core_two, 0)], [(hidden, 0), (core_one, 1024)], 512, 384)
    branch_got, _, branch_last = halve(branch_terms, "y", (down_terms[0],))
    low, high = finish(branch_terms, branch_got, branch_last)
    d_terms = pair_rows(order(y), after(d_pair, down_terms[0]), products, w3)
    down_got, _, down_last = halve(down_terms, "x")
    d_terms = lax.optimization_barrier((*d_terms, *branch_last))[:6]
    d_got = [send(value, move) for value, move in zip(d_terms[0:2], ("y^1", "y^3"))]
    core_three = send(jnp.concatenate([x_cross, after(pair_z, d_terms[0], *branch_last, *down_got)], axis=1), "c")
    pair_terms = outer(
        "pair_terms", order(x), [(x_keep, 0), (x_same, 0), (core_one, 0), (core_three, 0)],
        [(d_pair, 0), (pair_z, 0), (core_two, 2048), (core_three, 1024)], 256, 768,
    )
    down_last = lax.optimization_barrier((*down_last, pair_terms[0]))[:2]
    pair_terms = lax.optimization_barrier((*pair_terms, *down_last))[:6]
    pair_got, pair_out, pair_last = halve(pair_terms, "x")
    d_w_gate, d_w_up = finish(pair_terms, pair_got, pair_last)
    down = finish(down_terms, down_got, down_last, (pair_terms[0],))
    d_w_down = jnp.concatenate(down, axis=1)
    lower = z_lo == 0
    theirs = jnp.where(lower, d_w_down[256:], d_w_down[:256]).astype(bf16)
    d_w_down = jnp.where(lower, d_w_down[:256], d_w_down[256:]) + send(theirs, "z^1").astype(f32)

    _, d_last = second_step(d_terms, d_got, "y", (pair_terms[0],))
    d_low, d_high = finish(d_terms, d_got, d_last)
    upper = z_hi == 1
    mine = jnp.where(upper, d_high, d_low)
    theirs = send(jnp.where(upper, d_low, d_high).astype(bf16), "z+2")
    mine = mine + theirs.astype(f32)
    theirs = send(after(jnp.where(upper, low, high).astype(bf16), theirs), "z+2")
    branch = (jnp.where(upper, high, low) + theirs.astype(f32)).astype(bf16)
    d_normed, products = mine[:, :512], mine[:, 512:513] / width

    x_own = inputs.astype(f32)
    d_input = (d_normed * gain.astype(f32) - inv[:, :1] * products * x_own).astype(bf16)
    d_gain = jnp.sum(d_normed * x_own, axis=0, keepdims=True)
    for move in ("c", "z^1", "x^1", "x+2"):
        if move in ("c", "x+2"):
            d_gain = after(d_gain, *(pair_out if move == "c" else pair_last))
        d_gain = d_gain + send(d_gain, move)

    gain_rows = lax.dynamic_slice(gains, (0, s * 256), (1, 256)).astype(f32).reshape(256, 1)
    d_weights = jnp.stack(
        [(d_w_gate * gain_rows).astype(bf16), (d_w_up * gain_rows).astype(bf16), d_w_down.astype(bf16)], axis=1
    )
    return (branch, d_input, d_gain.reshape(512), d_weights)


def solution(mesh):
    in_specs = (P("seq", "tensor"), P("tensor"), P(None, None, "tensor"), P("seq", "tensor"))
    out_specs = (P("seq", "tensor"), P("seq", "tensor"), P("tensor"), P("seq", None, "tensor"))
    return jax.shard_map(local, mesh=mesh, in_specs=in_specs, out_specs=out_specs, check_vma=False)
```

```python
import functools
import jax
import jax.numpy as jnp
from jax import lax
from jax.experimental import pallas as pl
from jax.experimental.pallas import tpu as pltpu
from jax.sharding import PartitionSpec as P

norm_eps = 1e-05
AXES = ("tensor", "seq")
f32 = jnp.float32
bf16 = jnp.bfloat16
MiB = 1 << 20


def flat(x, y, z, c):
    x, y, z = x % 4, y % 4, z % 4
    return ((z // 2) * 4 + y) * 16 + (x * 2 + z % 2) * 2 + c


def pairs(move):
    places = [(x, y, z, c) for x in range(4) for y in range(4) for z in range(4) for c in range(2)]
    return [(flat(*place), flat(*move(*place))) for place in places]


moves = {
    "x^1": lambda x, y, z, c: (x ^ 1, y, z, c),
    "x^3": lambda x, y, z, c: (x ^ 3, y, z, c),
    "x+2": lambda x, y, z, c: (x + 2, y, z, c),
    "y+": lambda x, y, z, c: (x, y + 1, z, c),
    "y-": lambda x, y, z, c: (x, y - 1, z, c),
    "y^1": lambda x, y, z, c: (x, y ^ 1, z, c),
    "y^3": lambda x, y, z, c: (x, y ^ 3, z, c),
    "z+2": lambda x, y, z, c: (x, y, z + 2, c),
    "z^1": lambda x, y, z, c: (x, y, z ^ 1, c),
    "z^3": lambda x, y, z, c: (x, y, z ^ 3, c),
    "z^3c": lambda x, y, z, c: (x, y, z ^ 3, 1 - c),
    "c": lambda x, y, z, c: (x, y, z, 1 - c),
}


def send(value, move):
    return lax.ppermute(value, AXES, pairs(moves[move]))


def after(value, *done):
    return lax.optimization_barrier((value, *done))[0]


def rows_cat(*parts):
    return jnp.concatenate(parts, axis=0)


def dot(a, b):
    return jnp.dot(a, b, preferred_element_type=f32)


def dot_nt(a, b):
    return lax.dot_general(a, b, (((1,), (1,)), ((), ())), preferred_element_type=f32)


def dot_tn(a, b):
    return lax.dot_general(a, b, (((0,), (0,)), ((), ())), preferred_element_type=f32)


def call(body, name, shapes, scratch, limit, flops, size, args, hbm=(), scalars=1, direct=()):
    loads = [i for i in range(scalars, len(args)) if i not in hbm and i not in direct]
    spaces = [pltpu.SMEM] * scalars + [
        pltpu.HBM if i in hbm else pltpu.VMEM if i in direct else pl.ANY for i in range(scalars, len(args))
    ]

    def whole(*refs):
        ins, rest = list(refs[:len(args)]), refs[len(args):]
        outs, rest = rest[:len(shapes)], rest[len(shapes):]
        own, rest = rest[:len(scratch)], rest[len(scratch):]
        copies = []
        for n, i in enumerate(loads):
            copies.append(pltpu.make_async_copy(ins[i], rest[n], rest[-1].at[n]))
            copies[-1].start()
            ins[i] = rest[n]

        def ready():
            for copy in copies:
                copy.wait()

        body(ready, *ins, *outs, *own)

    held = [pltpu.VMEM(args[i].shape, args[i].dtype) for i in loads] + [pltpu.SemaphoreType.DMA((max(len(loads), 1),))]
    return pl.pallas_call(
        whole,
        in_specs=[pl.BlockSpec(memory_space=space) for space in spaces],
        out_specs=[pl.BlockSpec(memory_space=pltpu.VMEM) for _ in shapes],
        out_shape=[jax.ShapeDtypeStruct(shape, dtype) for shape, dtype in shapes],
        scratch_shapes=list(scratch) + held,
        compiler_params=pltpu.CompilerParams(vmem_limit_bytes=limit * MiB),
        cost_estimate=pl.CostEstimate(flops=flops, bytes_accessed=size, transcendentals=0),
        name=name,
    )(*args)


def lane(at, size, unit):
    return pl.ds(pl.multiple_of(at, unit), size)


def put(buf, spot, pieces):
    for dz, dy, row, ref, first, rows in pieces:
        buf[row:row + rows, lane(spot[dz * 4 + dy] * 512, 512, 512)] = ref[first:first + rows, :]


def fetch(w, held, sems, first, count, block_of):
    copies = []
    for k in range(8):
        rows = pl.ds(pl.multiple_of(block_of(k) * 512, 512), 512)
        copies.append(pltpu.make_async_copy(w.at[pl.ds(first, count), rows, :], held.at[k], sems.at[k]))
        copies[-1].start()
    return copies


def assemble_body(ready, spot, own, below, above, other, up2, down2, other_far, full, gains, keep, core_out, z_out,
                  cross_out):
    put(full, spot, [
        (0, 0, 0, own, 0, 272), (0, 3, 0, below, 0, 272), (0, 1, 0, above, 0, 272), (1, 0, 0, other, 0, 272),
        (0, 2, 0, up2, 0, 128), (1, 3, 0, up2, 128, 272), (0, 2, 128, down2, 0, 144), (1, 1, 0, down2, 144, 272),
        (1, 2, 0, other_far, 0, 272),
    ])
    gains[...] = full[256:272, :]
    z_lo, core = spot[8], spot[9]
    for i in range(4):
        for ref, zl, c in ((keep, z_lo, core), (core_out, z_lo, 1 - core), (z_out, 1 - z_lo, core),
                           (cross_out, 1 - z_lo, 1 - core)):
            ref[:, i * 256:(i + 1) * 256] = full[0:256, lane((2 * i + zl) * 512 + c * 256, 256, 256)]


def assemble(spot, pieces):
    shapes = [((272, 4096), bf16), ((16, 4096), bf16)] + [((256, 1024), bf16)] * 4
    return call(assemble_body, "assemble", shapes, [], 4, 0, 8 * MiB, (spot, *pieces), direct=range(1, 8))


def forward_body(ready, x_ref, x_core, w, gate, up, hidden, inv, core_out, held, sems):
    copies = fetch(w, held, sems, 0, 2, lambda k: k)
    squares = jnp.zeros((256, 1), f32)
    ready()
    for k in range(8):
        copies[k].wait()
        cols = slice(k * 512, (k + 1) * 512)
        x = x_ref[0:256, cols].astype(f32)
        squares = squares + jnp.sum(x * x, axis=1, keepdims=True)
        scaled = (x * x_ref[256:272, cols][0:1].astype(f32)).astype(bf16)
        for ref, j in ((gate, 0), (up, 1)):
            value = dot(scaled, held[k, j])
            ref[...] = value if k == 0 else ref[...] + value
    inv_rms = lax.rsqrt(squares / 4096 + norm_eps)
    g = gate[...] * inv_rms
    u = up[...] * inv_rms
    gate[...] = g
    up[...] = u
    hidden[...] = (g * jax.nn.sigmoid(g) * u).astype(bf16)
    core_out[:, 0:1024] = x_core[...]
    core_out[:, 1024:1792] = hidden[...]
    inv[...] = jnp.broadcast_to(inv_rms, (256, 128))


def forward(x_full, x_core, w3):
    shapes = [((256, 768), f32), ((256, 768), f32), ((256, 768), bf16), ((256, 128), f32), ((256, 1792), bf16)]
    scratch = [pltpu.VMEM((8, 2, 512, 768), bf16), pltpu.SemaphoreType.DMA((8,))]
    return call(forward_body, "forward", shapes, scratch, 18, 2 * 256 * 4096 * 1536, 16 * MiB,
                (x_full, x_core, w3), hbm=(2,), scalars=0, direct=(0,))


def backward_body(ready, spot, both, below, above, low, high, w, gate, up_val, inv, pair, products, mine, core_out, buf, acc,
                  held, sems):
    copies = fetch(w, held, sems, 2, 1, lambda k: k)
    put(buf, spot, [
        (0, 0, 0, both, 0, 256), (1, 0, 0, both, 256, 256), (0, 3, 0, below, 0, 256), (1, 3, 0, below, 256, 256),
        (0, 1, 0, above, 0, 256), (1, 1, 0, above, 256, 256), (0, 2, 0, low, 0, 128), (1, 2, 0, low, 128, 128),
        (0, 2, 128, high, 0, 128), (1, 2, 128, high, 128, 128),
    ])
    core = spot[9]
    for i in range(8):
        for ref, c in ((mine, core), (core_out, 1 - core)):
            ref[:, i * 256:(i + 1) * 256] = buf[:, lane(i * 512 + c * 256, 256, 256)]
    for k in range(8):
        copies[k].wait()
        value = dot(buf[:, k * 512:(k + 1) * 512], held[k, 0])
        acc[...] = value if k == 0 else acc[...] + value
    ready()
    d_hidden = acc[...] * inv[:, 0:1]
    g, u = gate[...], up_val[...]
    sigma = jax.nn.sigmoid(g)
    d_gate = (d_hidden * u * sigma * (1.0 + g * (1.0 - sigma))).astype(bf16)
    d_up = (d_hidden * g * sigma).astype(bf16)
    pair[:, 0:768] = d_gate
    pair[:, 768:1536] = d_up
    core_out[:, 2048:2816] = d_gate
    core_out[:, 2816:3584] = d_up
    total = jnp.sum(d_gate.astype(f32) * g + d_up.astype(f32) * u, axis=1, keepdims=True)
    products[...] = jnp.broadcast_to(total, (256, 128)).astype(bf16)


def backward(spot, pieces, w3, gate, up, inv):
    shapes = [((256, 1536), bf16), ((256, 128), bf16), ((256, 2048), bf16), ((256, 3584), bf16)]
    scratch = [pltpu.VMEM((256, 4096), bf16), pltpu.VMEM((256, 768), f32), pltpu.VMEM((8, 1, 512, 768), bf16),
               pltpu.SemaphoreType.DMA((8,))]
    return call(backward_body, "backward", shapes, scratch, 16, 2 * 256 * 4096 * 768, 8 * MiB, (spot, *pieces, w3, gate, up, inv),
                hbm=(6,), direct=range(1, 6))


def store(outs, k, value):
    half, i = k // 4, k % 4
    if i < 2:
        rows = value.shape[0]
        outs[half][i * rows:(i + 1) * rows, :] = value
    else:
        outs[2 * i - 2 + half][...] = value


def halving_shapes(rows, cols):
    return [((2 * rows, cols), bf16)] * 2 + [((rows, cols), bf16)] * 4


def outer_body(a_from, b_from, rows, cols, ready, order, *refs):
    n = len(a_from)
    a_refs, b_refs, outs = refs[:n], refs[n:2 * n], refs[2 * n:]
    ready()
    for k in range(8):
        total = None
        for a, a0, b, b0 in zip(a_refs, a_from, b_refs, b_from):
            b0 = k // 4 * cols + b0
            value = dot_tn(a[:, lane(order[k] * rows + a0, rows, 256)], b[:, b0:b0 + cols])
            total = value if total is None else total + value
        store(outs, k, total.astype(bf16))


def outer(name, order, a_list, b_list, rows, cols):
    body = functools.partial(outer_body, [f for _, f in a_list], [f for _, f in b_list], rows, cols)
    flops = 2 * 256 * len(a_list) * rows * 8 * cols
    return call(body, name, halving_shapes(rows, cols), [], 16, flops, 8 * MiB,
                (order, *[a for a, _ in a_list], *[b for b, _ in b_list]))


def branch_rows_body(ready, order, hidden, w, *refs):
    outs, held, sems = refs[:6], refs[6], refs[7]
    copies = fetch(w, held, sems, 2, 1, lambda k: k // 4 * 4 + order[k])
    ready()
    for k in range(8):
        copies[k].wait()
        store(outs, k, dot_nt(hidden[...], held[k, 0]).astype(bf16))


def branch_rows(order, hidden, w3):
    scratch = [pltpu.VMEM((8, 1, 512, 768), bf16), pltpu.SemaphoreType.DMA((8,))]
    return call(branch_rows_body, "branch_rows", halving_shapes(256, 512), scratch, 10, 2 * 256 * 768 * 4096, 8 * MiB,
                (order, hidden, w3), hbm=(2,))


def pair_rows_body(ready, order, pair, products, w, *refs):
    outs, held, sems = refs[:6], refs[6], refs[7]
    copies = fetch(w, held, sems, 0, 2, lambda k: k // 4 * 4 + order[k])
    ready()
    for k in range(8):
        copies[k].wait()
        value = dot_nt(pair[:, 0:768], held[k, 0]) + dot_nt(pair[:, 768:1536], held[k, 1])
        store(outs, k, jnp.concatenate([value.astype(bf16), products[...]], axis=1))


def pair_rows(order, pair, products, w3):
    scratch = [pltpu.VMEM((8, 2, 512, 768), bf16), pltpu.SemaphoreType.DMA((8,))]
    return call(pair_rows_body, "pair_rows", halving_shapes(256, 640), scratch, 16, 2 * 256 * 1536 * 4096, 16 * MiB,
                (order, pair, products, w3), hbm=(3,))


def second_step(terms, got, axis, done=()):
    rows = terms[2].shape[0]
    two, six, *got = lax.optimization_barrier((terms[2], terms[3], *got, *done))[:4]
    out = [(t.astype(f32) + g[rows:].astype(f32)).astype(bf16) for t, g in zip((two, six), got)]
    return out, [send(o, axis + move) for o, move in zip(out, ("^3", "^1"))]


def halve(terms, axis, done=()):
    got = [send(value, axis + move) for value, move in zip(terms[0:2], ("^1", "^3"))]
    return (got, *second_step(terms, got, axis, done))


def finish(terms, got, last, done=()):
    low, high = lax.optimization_barrier((terms[4], terms[5], *done))[:2]
    rows = terms[4].shape[0]
    return [t.astype(f32) + g[:rows].astype(f32) + e.astype(f32) for t, g, e in zip((low, high), got, last)]


def gather_both(own, cot):
    below, above, other = send(own, "y+"), send(own, "y-"), send(own, "z+2")
    up = send(rows_cat(below[:128], other), "y+")
    down = send(rows_cat(above[128:], other), "y-")
    cot_other = send(after(cot, other), "z+2")
    other_far = send(after(rows_cat(up[:128], down[:144]), cot_other), "z+2")
    both = after(rows_cat(cot, cot_other), up, down)
    cot_below, cot_above = send(both, "y+"), send(both, "y-")
    low = send(rows_cat(cot_below[:128], cot_below[256:384]), "y+")
    high = send(rows_cat(cot_above[128:256], cot_above[384:]), "y-")
    return (own, below, above, other, up, down, other_far), (both, cot_below, cot_above, low, high)


def local(inputs, gain, weights, d_out):
    width = weights.shape[0]
    t, s = lax.axis_index("tensor"), lax.axis_index("seq")
    z_hi, y = t // 4, t % 4
    x, z_lo, core = s // 4, s // 2 % 2, s % 2
    w3 = pltpu.with_memory_space_constraint(jnp.transpose(weights, (1, 0, 2)), pltpu.HBM)
    spot = jnp.stack(
        [(z_hi + dz) % 2 * 4 + (y + dy) % 4 for dz in (0, 1) for dy in range(4)] + [z_lo, core]
    ).astype(jnp.int32)

    def order(at):
        return jnp.stack([at ^ 1, at ^ 2, at ^ 3, at, at ^ 3, at ^ 2, at ^ 1, at]).astype(jnp.int32)

    own = rows_cat(inputs, jnp.broadcast_to(gain.reshape(1, 512), (16, 512)))
    x_pieces, cot_pieces = gather_both(own, d_out)
    x_full, gains, x_keep, x_core, x_same, x_cross = assemble(spot, x_pieces)
    x_same, x_cross = send(x_same, "z^3"), send(x_cross, "z^1")
    gate, up_val, hidden, inv, core_one = forward(after(x_full, *cot_pieces[1:3]), x_core, w3)
    core_one = send(core_one, "c")
    cot_pieces = (after(cot_pieces[0], x_same, x_cross), *cot_pieces[1:])
    d_pair, products, cot_mine, core_two = backward(spot, cot_pieces, w3, gate, up_val, inv)
    core_two = send(core_two, "c")
    branch_terms = branch_rows(order(y), after(hidden, d_pair), w3)
    pair_z = send(d_pair, "z^1")
    down_terms = outer("down_terms", order(x), [(after(cot_mine, branch_terms[0]), 0), (core_two, 0)], [(hidden, 0), (core_one, 1024)], 512, 384)
    branch_got = [send(value, move) for value, move in zip(branch_terms[0:2], ("y^1", "y^3"))]
    d_terms = pair_rows(order(y), after(d_pair, down_terms[0]), products, w3)
    down_got, _, down_last = halve(down_terms, "x")
    d_terms = lax.optimization_barrier((*d_terms, *branch_got))[:6]
    d_got = [send(value, move) for value, move in zip(d_terms[0:2], ("y^1", "y^3"))]
    core_three = send(jnp.concatenate([x_cross, after(pair_z, d_terms[0], *down_got)], axis=1), "c")
    pair_terms = outer(
        "pair_terms", order(x), [(x_keep, 0), (x_same, 0), (core_one, 0), (core_three, 0)],
        [(d_pair, 0), (pair_z, 0), (core_two, 2048), (core_three, 1024)], 256, 768,
    )
    down_last = lax.optimization_barrier((*down_last, pair_terms[0]))[:2]
    pair_terms = lax.optimization_barrier((*pair_terms, *down_last))[:6]
    pair_got, pair_out, pair_last = halve(pair_terms, "x")
    d_w_gate, d_w_up = finish(pair_terms, pair_got, pair_last)
    down = finish(down_terms, down_got, down_last, (pair_terms[0],))
    d_w_down = jnp.concatenate(down, axis=1)
    lower = z_lo == 0
    theirs = after(jnp.where(lower, d_w_down[256:], d_w_down[:256]).astype(bf16), *pair_got)
    d_w_down = jnp.where(lower, d_w_down[:256], d_w_down[256:]) + send(theirs, "z^1").astype(f32)

    _, d_last = second_step(d_terms, d_got, "y", (pair_terms[0],))
    d_low, d_high = finish(d_terms, d_got, d_last)
    _, branch_last = second_step(branch_terms, branch_got, "y", (pair_terms[0], *d_last))
    low, high = finish(branch_terms, branch_got, branch_last)
    upper = z_hi == 1
    mine = jnp.where(upper, d_high, d_low)
    theirs = send(jnp.where(upper, d_low, d_high).astype(bf16), "z+2")
    mine = after(mine, *pair_got) + theirs.astype(f32)
    theirs = send(after(jnp.where(upper, low, high).astype(bf16), theirs), "z+2")
    branch = (jnp.where(upper, high, low) + theirs.astype(f32)).astype(bf16)
    d_normed, products = mine[:, :512], mine[:, 512:513] / width

    x_own = inputs.astype(f32)
    d_input = (d_normed * gain.astype(f32) - inv[:, :1] * products * x_own).astype(bf16)
    d_gain = jnp.sum(d_normed * x_own, axis=0, keepdims=True)
    for move in ("c", "z^1", "x^1", "x+2"):
        if move in ("c", "x+2"):
            d_gain = after(d_gain, *(pair_out if move == "c" else pair_last))
        d_gain = d_gain + send(d_gain, move)

    gain_rows = lax.dynamic_slice(gains, (0, s * 256), (1, 256)).astype(f32).reshape(256, 1)
    d_weights = jnp.stack(
        [(d_w_gate * gain_rows).astype(bf16), (d_w_up * gain_rows).astype(bf16), d_w_down.astype(bf16)], axis=1
    )
    return (branch, d_input, d_gain.reshape(512), d_weights)


def solution(mesh):
    in_specs = (P("seq", "tensor"), P("tensor"), P(None, None, "tensor"), P("seq", "tensor"))
    out_specs = (P("seq", "tensor"), P("seq", "tensor"), P("tensor"), P("seq", None, "tensor"))
    return jax.shard_map(local, mesh=mesh, in_specs=in_specs, out_specs=out_specs, check_vma=False)
```

```python
import functools
import jax
import jax.numpy as jnp
from jax import lax
from jax.experimental import pallas as pl
from jax.experimental.pallas import tpu as pltpu
from jax.sharding import PartitionSpec as P

norm_eps = 1e-05
AXES = ("tensor", "seq")
f32 = jnp.float32
bf16 = jnp.bfloat16
MiB = 1 << 20


def flat(x, y, z, c):
    x, y, z = x % 4, y % 4, z % 4
    return ((z // 2) * 4 + y) * 16 + (x * 2 + z % 2) * 2 + c


def pairs(move):
    places = [(x, y, z, c) for x in range(4) for y in range(4) for z in range(4) for c in range(2)]
    return [(flat(*place), flat(*move(*place))) for place in places]


moves = {
    "x^1": lambda x, y, z, c: (x ^ 1, y, z, c),
    "x^3": lambda x, y, z, c: (x ^ 3, y, z, c),
    "x+2": lambda x, y, z, c: (x + 2, y, z, c),
    "y+": lambda x, y, z, c: (x, y + 1, z, c),
    "y-": lambda x, y, z, c: (x, y - 1, z, c),
    "y^1": lambda x, y, z, c: (x, y ^ 1, z, c),
    "y^3": lambda x, y, z, c: (x, y ^ 3, z, c),
    "z+2": lambda x, y, z, c: (x, y, z + 2, c),
    "z^1": lambda x, y, z, c: (x, y, z ^ 1, c),
    "z^3": lambda x, y, z, c: (x, y, z ^ 3, c),
    "z^3c": lambda x, y, z, c: (x, y, z ^ 3, 1 - c),
    "c": lambda x, y, z, c: (x, y, z, 1 - c),
}


def send(value, move):
    return lax.ppermute(value, AXES, pairs(moves[move]))


def after(value, *done):
    return lax.optimization_barrier((value, *done))[0]


def rows_cat(*parts):
    return jnp.concatenate(parts, axis=0)


def dot(a, b):
    return jnp.dot(a, b, preferred_element_type=f32)


def dot_nt(a, b):
    return lax.dot_general(a, b, (((1,), (1,)), ((), ())), preferred_element_type=f32)


def dot_tn(a, b):
    return lax.dot_general(a, b, (((0,), (0,)), ((), ())), preferred_element_type=f32)


def call(body, name, shapes, scratch, limit, flops, size, args, hbm=(), scalars=1, direct=()):
    loads = [i for i in range(scalars, len(args)) if i not in hbm and i not in direct]
    spaces = [pltpu.SMEM] * scalars + [
        pltpu.HBM if i in hbm else pltpu.VMEM if i in direct else pl.ANY for i in range(scalars, len(args))
    ]

    def whole(*refs):
        ins, rest = list(refs[:len(args)]), refs[len(args):]
        outs, rest = rest[:len(shapes)], rest[len(shapes):]
        own, rest = rest[:len(scratch)], rest[len(scratch):]
        copies = []
        for n, i in enumerate(loads):
            copies.append(pltpu.make_async_copy(ins[i], rest[n], rest[-1].at[n]))
            copies[-1].start()
            ins[i] = rest[n]

        def ready():
            for copy in copies:
                copy.wait()

        body(ready, *ins, *outs, *own)

    held = [pltpu.VMEM(args[i].shape, args[i].dtype) for i in loads] + [pltpu.SemaphoreType.DMA((max(len(loads), 1),))]
    return pl.pallas_call(
        whole,
        in_specs=[pl.BlockSpec(memory_space=space) for space in spaces],
        out_specs=[pl.BlockSpec(memory_space=pltpu.VMEM) for _ in shapes],
        out_shape=[jax.ShapeDtypeStruct(shape, dtype) for shape, dtype in shapes],
        scratch_shapes=list(scratch) + held,
        compiler_params=pltpu.CompilerParams(vmem_limit_bytes=limit * MiB),
        cost_estimate=pl.CostEstimate(flops=flops, bytes_accessed=size, transcendentals=0),
        name=name,
    )(*args)


def lane(at, size, unit):
    return pl.ds(pl.multiple_of(at, unit), size)


def put(buf, spot, pieces):
    for dz, dy, row, ref, first, rows in pieces:
        buf[row:row + rows, lane(spot[dz * 4 + dy] * 512, 512, 512)] = ref[first:first + rows, :]


def fetch(w, held, sems, first, count, block_of):
    copies = []
    for k in range(8):
        rows = pl.ds(pl.multiple_of(block_of(k) * 512, 512), 512)
        copies.append(pltpu.make_async_copy(w.at[pl.ds(first, count), rows, :], held.at[k], sems.at[k]))
        copies[-1].start()
    return copies


def assemble_body(ready, spot, own, below, above, other, up2, down2, other_far, full, gains, keep, core_out, z_out,
                  cross_out):
    put(full, spot, [
        (0, 0, 0, own, 0, 272), (0, 3, 0, below, 0, 272), (0, 1, 0, above, 0, 272), (1, 0, 0, other, 0, 272),
        (0, 2, 0, up2, 0, 128), (1, 3, 0, up2, 128, 272), (0, 2, 128, down2, 0, 144), (1, 1, 0, down2, 144, 272),
        (1, 2, 0, other_far, 0, 272),
    ])
    gains[...] = full[256:272, :]
    z_lo, core = spot[8], spot[9]
    for i in range(4):
        for ref, zl, c in ((keep, z_lo, core), (core_out, z_lo, 1 - core), (z_out, 1 - z_lo, core),
                           (cross_out, 1 - z_lo, 1 - core)):
            ref[:, i * 256:(i + 1) * 256] = full[0:256, lane((2 * i + zl) * 512 + c * 256, 256, 256)]


def assemble(spot, pieces):
    shapes = [((272, 4096), bf16), ((16, 4096), bf16)] + [((256, 1024), bf16)] * 4
    return call(assemble_body, "assemble", shapes, [], 4, 0, 8 * MiB, (spot, *pieces), direct=range(1, 8))


def forward_body(ready, x_ref, x_core, w, gate, up, hidden, inv, core_out, held, sems):
    copies = fetch(w, held, sems, 0, 2, lambda k: k)
    squares = jnp.zeros((256, 1), f32)
    ready()
    for k in range(8):
        copies[k].wait()
        cols = slice(k * 512, (k + 1) * 512)
        x = x_ref[0:256, cols].astype(f32)
        squares = squares + jnp.sum(x * x, axis=1, keepdims=True)
        scaled = (x * x_ref[256:272, cols][0:1].astype(f32)).astype(bf16)
        for ref, j in ((gate, 0), (up, 1)):
            value = dot(scaled, held[k, j])
            ref[...] = value if k == 0 else ref[...] + value
    inv_rms = lax.rsqrt(squares / 4096 + norm_eps)
    g = gate[...] * inv_rms
    u = up[...] * inv_rms
    gate[...] = g
    up[...] = u
    hidden[...] = (g * jax.nn.sigmoid(g) * u).astype(bf16)
    core_out[:, 0:1024] = x_core[...]
    core_out[:, 1024:1792] = hidden[...]
    inv[...] = jnp.broadcast_to(inv_rms, (256, 128))


def forward(x_full, x_core, w3):
    shapes = [((256, 768), f32), ((256, 768), f32), ((256, 768), bf16), ((256, 128), f32), ((256, 1792), bf16)]
    scratch = [pltpu.VMEM((8, 2, 512, 768), bf16), pltpu.SemaphoreType.DMA((8,))]
    return call(forward_body, "forward", shapes, scratch, 18, 2 * 256 * 4096 * 1536, 16 * MiB,
                (x_full, x_core, w3), hbm=(2,), scalars=0, direct=(0,))


def backward_body(ready, spot, both, below, above, low, high, w, gate, up_val, inv, pair, products, mine, core_out, buf, acc,
                  held, sems):
    copies = fetch(w, held, sems, 2, 1, lambda k: k)
    put(buf, spot, [
        (0, 0, 0, both, 0, 256), (1, 0, 0, both, 256, 256), (0, 3, 0, below, 0, 256), (1, 3, 0, below, 256, 256),
        (0, 1, 0, above, 0, 256), (1, 1, 0, above, 256, 256), (0, 2, 0, low, 0, 128), (1, 2, 0, low, 128, 128),
        (0, 2, 128, high, 0, 128), (1, 2, 128, high, 128, 128),
    ])
    core = spot[9]
    for i in range(8):
        for ref, c in ((mine, core), (core_out, 1 - core)):
            ref[:, i * 256:(i + 1) * 256] = buf[:, lane(i * 512 + c * 256, 256, 256)]
    for k in range(8):
        copies[k].wait()
        value = dot(buf[:, k * 512:(k + 1) * 512], held[k, 0])
        acc[...] = value if k == 0 else acc[...] + value
    ready()
    d_hidden = acc[...] * inv[:, 0:1]
    g, u = gate[...], up_val[...]
    sigma = jax.nn.sigmoid(g)
    d_gate = (d_hidden * u * sigma * (1.0 + g * (1.0 - sigma))).astype(bf16)
    d_up = (d_hidden * g * sigma).astype(bf16)
    pair[:, 0:768] = d_gate
    pair[:, 768:1536] = d_up
    core_out[:, 2048:2816] = d_gate
    core_out[:, 2816:3584] = d_up
    total = jnp.sum(d_gate.astype(f32) * g + d_up.astype(f32) * u, axis=1, keepdims=True)
    products[...] = jnp.broadcast_to(total, (256, 128)).astype(bf16)


def backward(spot, pieces, w3, gate, up, inv):
    shapes = [((256, 1536), bf16), ((256, 128), bf16), ((256, 2048), bf16), ((256, 3584), bf16)]
    scratch = [pltpu.VMEM((256, 4096), bf16), pltpu.VMEM((256, 768), f32), pltpu.VMEM((8, 1, 512, 768), bf16),
               pltpu.SemaphoreType.DMA((8,))]
    return call(backward_body, "backward", shapes, scratch, 16, 2 * 256 * 4096 * 768, 8 * MiB, (spot, *pieces, w3, gate, up, inv),
                hbm=(6,), direct=range(1, 6))


def store(outs, k, value):
    half, i = k // 4, k % 4
    if i < 2:
        rows = value.shape[0]
        outs[half][i * rows:(i + 1) * rows, :] = value
    else:
        outs[2 * i - 2 + half][...] = value


def halving_shapes(rows, cols):
    return [((2 * rows, cols), bf16)] * 2 + [((rows, cols), bf16)] * 4


def outer_body(a_from, b_from, rows, cols, ready, order, *refs):
    n = len(a_from)
    a_refs, b_refs, outs = refs[:n], refs[n:2 * n], refs[2 * n:]
    ready()
    for k in range(8):
        total = None
        for a, a0, b, b0 in zip(a_refs, a_from, b_refs, b_from):
            b0 = k // 4 * cols + b0
            value = dot_tn(a[:, lane(order[k] * rows + a0, rows, 256)], b[:, b0:b0 + cols])
            total = value if total is None else total + value
        store(outs, k, total.astype(bf16))


def outer(name, order, a_list, b_list, rows, cols):
    body = functools.partial(outer_body, [f for _, f in a_list], [f for _, f in b_list], rows, cols)
    flops = 2 * 256 * len(a_list) * rows * 8 * cols
    return call(body, name, halving_shapes(rows, cols), [], 16, flops, 8 * MiB,
                (order, *[a for a, _ in a_list], *[b for b, _ in b_list]))


def branch_rows_body(ready, order, hidden, w, *refs):
    outs, held, sems = refs[:6], refs[6], refs[7]
    copies = fetch(w, held, sems, 2, 1, lambda k: k // 4 * 4 + order[k])
    ready()
    for k in range(8):
        copies[k].wait()
        store(outs, k, dot_nt(hidden[...], held[k, 0]).astype(bf16))


def branch_rows(order, hidden, w3):
    scratch = [pltpu.VMEM((8, 1, 512, 768), bf16), pltpu.SemaphoreType.DMA((8,))]
    return call(branch_rows_body, "branch_rows", halving_shapes(256, 512), scratch, 10, 2 * 256 * 768 * 4096, 8 * MiB,
                (order, hidden, w3), hbm=(2,))


def pair_rows_body(ready, order, pair, products, w, *refs):
    outs, held, sems = refs[:6], refs[6], refs[7]
    copies = fetch(w, held, sems, 0, 2, lambda k: k // 4 * 4 + order[k])
    ready()
    for k in range(8):
        copies[k].wait()
        value = dot_nt(pair[:, 0:768], held[k, 0]) + dot_nt(pair[:, 768:1536], held[k, 1])
        store(outs, k, jnp.concatenate([value.astype(bf16), products[...]], axis=1))


def pair_rows(order, pair, products, w3):
    scratch = [pltpu.VMEM((8, 2, 512, 768), bf16), pltpu.SemaphoreType.DMA((8,))]
    return call(pair_rows_body, "pair_rows", halving_shapes(256, 640), scratch, 16, 2 * 256 * 1536 * 4096, 16 * MiB,
                (order, pair, products, w3), hbm=(3,))


def second_step(terms, got, axis, done=()):
    rows = terms[2].shape[0]
    two, six, *got = lax.optimization_barrier((terms[2], terms[3], *got, *done))[:4]
    out = [(t.astype(f32) + g[rows:].astype(f32)).astype(bf16) for t, g in zip((two, six), got)]
    return out, [send(o, axis + move) for o, move in zip(out, ("^3", "^1"))]


def halve(terms, axis, done=()):
    got = [send(value, axis + move) for value, move in zip(terms[0:2], ("^1", "^3"))]
    return (got, *second_step(terms, got, axis, done))


def finish(terms, got, last, done=()):
    low, high = lax.optimization_barrier((terms[4], terms[5], *done))[:2]
    rows = terms[4].shape[0]
    return [t.astype(f32) + g[:rows].astype(f32) + e.astype(f32) for t, g, e in zip((low, high), got, last)]


def gather_both(own, cot):
    below, above, other = send(own, "y+"), send(own, "y-"), send(own, "z+2")
    up = send(rows_cat(below[:128], other), "y+")
    down = send(rows_cat(above[128:], other), "y-")
    cot_other = send(after(cot, other), "z+2")
    other_far = send(after(rows_cat(up[:128], down[:144]), cot_other), "z+2")
    both = after(rows_cat(cot, cot_other), up, down)
    cot_below, cot_above = send(both, "y+"), send(both, "y-")
    low = send(rows_cat(cot_below[:128], cot_below[256:384]), "y+")
    high = send(rows_cat(cot_above[128:256], cot_above[384:]), "y-")
    return (own, below, above, other, up, down, other_far), (both, cot_below, cot_above, low, high)


def local(inputs, gain, weights, d_out):
    width = weights.shape[0]
    t, s = lax.axis_index("tensor"), lax.axis_index("seq")
    z_hi, y = t // 4, t % 4
    x, z_lo, core = s // 4, s // 2 % 2, s % 2
    w3 = pltpu.with_memory_space_constraint(jnp.transpose(weights, (1, 0, 2)), pltpu.HBM)
    spot = jnp.stack(
        [(z_hi + dz) % 2 * 4 + (y + dy) % 4 for dz in (0, 1) for dy in range(4)] + [z_lo, core]
    ).astype(jnp.int32)

    def order(at):
        return jnp.stack([at ^ 1, at ^ 2, at ^ 3, at, at ^ 3, at ^ 2, at ^ 1, at]).astype(jnp.int32)

    own = rows_cat(inputs, jnp.broadcast_to(gain.reshape(1, 512), (16, 512)))
    x_pieces, cot_pieces = gather_both(own, d_out)
    x_full, gains, x_keep, x_core, x_same, x_cross = assemble(spot, x_pieces)
    x_same, x_cross = send(x_same, "z^3"), send(x_cross, "z^1")
    gate, up_val, hidden, inv, core_one = forward(after(x_full, *cot_pieces[1:3]), x_core, w3)
    core_one = send(core_one, "c")
    cot_pieces = (after(cot_pieces[0], x_same, x_cross), *cot_pieces[1:])
    d_pair, products, cot_mine, core_two = backward(spot, cot_pieces, w3, gate, up_val, inv)
    core_two = send(core_two, "c")
    d_terms = pair_rows(order(y), d_pair, products, w3)
    pair_z = send(d_pair, "z^1")
    down_terms = outer("down_terms", order(x), [(after(cot_mine, d_terms[0]), 0), (core_two, 0)], [(hidden, 0), (core_one, 1024)], 512, 384)
    branch_terms = branch_rows(order(y), after(hidden, down_terms[0]), w3)
    down_got, _, down_last = halve(down_terms, "x")
    d_got, _, d_last = halve(d_terms, "y", down_got)
    core_three = send(jnp.concatenate([x_cross, after(pair_z, branch_terms[0], *down_got, *d_got)], axis=1), "c")
    pair_terms = outer(
        "pair_terms", order(x), [(x_keep, 0), (x_same, 0), (core_one, 0), (core_three, 0)],
        [(d_pair, 0), (pair_z, 0), (core_two, 2048), (core_three, 1024)], 256, 768,
    )
    down_last = lax.optimization_barrier((*down_last, pair_terms[0]))[:2]
    pair_terms = lax.optimization_barrier((*pair_terms, *down_last))[:6]
    pair_got, pair_out, pair_last = halve(pair_terms, "x")
    d_w_gate, d_w_up = finish(pair_terms, pair_got, pair_last)
    down = finish(down_terms, down_got, down_last, (pair_terms[0],))
    d_w_down = jnp.concatenate(down, axis=1)
    lower = z_lo == 0
    theirs = jnp.where(lower, d_w_down[256:], d_w_down[:256]).astype(bf16)
    d_w_down = jnp.where(lower, d_w_down[:256], d_w_down[256:]) + send(theirs, "z^1").astype(f32)

    d_last = lax.optimization_barrier((*d_last, pair_terms[0]))[:2]
    d_low, d_high = finish(d_terms, d_got, d_last)
    upper = z_hi == 1
    mine = jnp.where(upper, d_high, d_low)
    theirs = send(jnp.where(upper, d_low, d_high).astype(bf16), "z+2")
    branch_terms = lax.optimization_barrier((*branch_terms, theirs))[:6]
    branch_got, _, branch_last = halve(branch_terms, "y")
    low, high = finish(branch_terms, branch_got, branch_last)
    mine = mine + theirs.astype(f32)
    theirs = send(after(jnp.where(upper, low, high).astype(bf16), theirs), "z+2")
    branch = (jnp.where(upper, high, low) + theirs.astype(f32)).astype(bf16)
    d_normed, products = mine[:, :512], mine[:, 512:513] / width

    x_own = inputs.astype(f32)
    d_input = (d_normed * gain.astype(f32) - inv[:, :1] * products * x_own).astype(bf16)
    d_gain = jnp.sum(d_normed * x_own, axis=0, keepdims=True)
    for move in ("c", "z^1", "x^1", "x+2"):
        if move == "x^1":
            d_gain = after(d_gain, *pair_last)
        d_gain = d_gain + send(d_gain, move)

    gain_rows = lax.dynamic_slice(gains, (0, s * 256), (1, 256)).astype(f32).reshape(256, 1)
    d_weights = jnp.stack(
        [(d_w_gate * gain_rows).astype(bf16), (d_w_up * gain_rows).astype(bf16), d_w_down.astype(bf16)], axis=1
    )
    return (branch, d_input, d_gain.reshape(512), d_weights)


def solution(mesh):
    in_specs = (P("seq", "tensor"), P("tensor"), P(None, None, "tensor"), P("seq", "tensor"))
    out_specs = (P("seq", "tensor"), P("seq", "tensor"), P("tensor"), P("seq", None, "tensor"))
    return jax.shard_map(local, mesh=mesh, in_specs=in_specs, out_specs=out_specs, check_vma=False)
```

```python
import functools
import jax
import jax.numpy as jnp
from jax import lax
from jax.experimental import pallas as pl
from jax.experimental.pallas import tpu as pltpu
from jax.sharding import PartitionSpec as P

norm_eps = 1e-05
AXES = ("tensor", "seq")
f32 = jnp.float32
bf16 = jnp.bfloat16
MiB = 1 << 20


def flat(x, y, z, c):
    x, y, z = x % 4, y % 4, z % 4
    return ((z // 2) * 4 + y) * 16 + (x * 2 + z % 2) * 2 + c


def pairs(move):
    places = [(x, y, z, c) for x in range(4) for y in range(4) for z in range(4) for c in range(2)]
    return [(flat(*place), flat(*move(*place))) for place in places]


moves = {
    "x^1": lambda x, y, z, c: (x ^ 1, y, z, c),
    "x^3": lambda x, y, z, c: (x ^ 3, y, z, c),
    "x+2": lambda x, y, z, c: (x + 2, y, z, c),
    "y+": lambda x, y, z, c: (x, y + 1, z, c),
    "y-": lambda x, y, z, c: (x, y - 1, z, c),
    "y^1": lambda x, y, z, c: (x, y ^ 1, z, c),
    "y^3": lambda x, y, z, c: (x, y ^ 3, z, c),
    "z+2": lambda x, y, z, c: (x, y, z + 2, c),
    "z^1": lambda x, y, z, c: (x, y, z ^ 1, c),
    "z^3": lambda x, y, z, c: (x, y, z ^ 3, c),
    "z^3c": lambda x, y, z, c: (x, y, z ^ 3, 1 - c),
    "c": lambda x, y, z, c: (x, y, z, 1 - c),
}


def send(value, move):
    return lax.ppermute(value, AXES, pairs(moves[move]))


def after(value, *done):
    return lax.optimization_barrier((value, *done))[0]


def rows_cat(*parts):
    return jnp.concatenate(parts, axis=0)


def dot(a, b):
    return jnp.dot(a, b, preferred_element_type=f32)


def dot_nt(a, b):
    return lax.dot_general(a, b, (((1,), (1,)), ((), ())), preferred_element_type=f32)


def dot_tn(a, b):
    return lax.dot_general(a, b, (((0,), (0,)), ((), ())), preferred_element_type=f32)


def call(body, name, shapes, scratch, limit, flops, size, args, hbm=(), scalars=1, direct=()):
    loads = [i for i in range(scalars, len(args)) if i not in hbm and i not in direct]
    spaces = [pltpu.SMEM] * scalars + [
        pltpu.HBM if i in hbm else pltpu.VMEM if i in direct else pl.ANY for i in range(scalars, len(args))
    ]

    def whole(*refs):
        ins, rest = list(refs[:len(args)]), refs[len(args):]
        outs, rest = rest[:len(shapes)], rest[len(shapes):]
        own, rest = rest[:len(scratch)], rest[len(scratch):]
        copies = []
        for n, i in enumerate(loads):
            copies.append(pltpu.make_async_copy(ins[i], rest[n], rest[-1].at[n]))
            copies[-1].start()
            ins[i] = rest[n]

        def ready():
            for copy in copies:
                copy.wait()

        body(ready, *ins, *outs, *own)

    held = [pltpu.VMEM(args[i].shape, args[i].dtype) for i in loads] + [pltpu.SemaphoreType.DMA((max(len(loads), 1),))]
    return pl.pallas_call(
        whole,
        in_specs=[pl.BlockSpec(memory_space=space) for space in spaces],
        out_specs=[pl.BlockSpec(memory_space=pltpu.VMEM) for _ in shapes],
        out_shape=[jax.ShapeDtypeStruct(shape, dtype) for shape, dtype in shapes],
        scratch_shapes=list(scratch) + held,
        compiler_params=pltpu.CompilerParams(vmem_limit_bytes=limit * MiB),
        cost_estimate=pl.CostEstimate(flops=flops, bytes_accessed=size, transcendentals=0),
        name=name,
    )(*args)


def lane(at, size, unit):
    return pl.ds(pl.multiple_of(at, unit), size)


def put(buf, spot, pieces):
    for dz, dy, row, ref, first, rows in pieces:
        buf[row:row + rows, lane(spot[dz * 4 + dy] * 512, 512, 512)] = ref[first:first + rows, :]


def fetch(w, held, sems, first, count, block_of):
    copies = []
    for k in range(8):
        rows = pl.ds(pl.multiple_of(block_of(k) * 512, 512), 512)
        copies.append(pltpu.make_async_copy(w.at[pl.ds(first, count), rows, :], held.at[k], sems.at[k]))
        copies[-1].start()
    return copies


def assemble_body(ready, spot, own, below, above, other, up2, down2, other_far, full, gains, keep, core_out, z_out,
                  cross_out):
    put(full, spot, [
        (0, 0, 0, own, 0, 272), (0, 3, 0, below, 0, 272), (0, 1, 0, above, 0, 272), (1, 0, 0, other, 0, 272),
        (0, 2, 0, up2, 0, 128), (1, 3, 0, up2, 128, 272), (0, 2, 128, down2, 0, 144), (1, 1, 0, down2, 144, 272),
        (1, 2, 0, other_far, 0, 272),
    ])
    gains[...] = full[256:272, :]
    z_lo, core = spot[8], spot[9]
    for i in range(4):
        for ref, zl, c in ((keep, z_lo, core), (core_out, z_lo, 1 - core), (z_out, 1 - z_lo, core),
                           (cross_out, 1 - z_lo, 1 - core)):
            ref[:, i * 256:(i + 1) * 256] = full[0:256, lane((2 * i + zl) * 512 + c * 256, 256, 256)]


def assemble(spot, pieces):
    shapes = [((272, 4096), bf16), ((16, 4096), bf16)] + [((256, 1024), bf16)] * 4
    return call(assemble_body, "assemble", shapes, [], 4, 0, 8 * MiB, (spot, *pieces), direct=range(1, 8))


def forward_body(ready, x_ref, x_core, w, gate, up, hidden, inv, core_out, held, sems):
    copies = fetch(w, held, sems, 0, 2, lambda k: k)
    squares = jnp.zeros((256, 1), f32)
    ready()
    for k in range(8):
        copies[k].wait()
        cols = slice(k * 512, (k + 1) * 512)
        x = x_ref[0:256, cols].astype(f32)
        squares = squares + jnp.sum(x * x, axis=1, keepdims=True)
        scaled = (x * x_ref[256:272, cols][0:1].astype(f32)).astype(bf16)
        for ref, j in ((gate, 0), (up, 1)):
            value = dot(scaled, held[k, j])
            ref[...] = value if k == 0 else ref[...] + value
    inv_rms = lax.rsqrt(squares / 4096 + norm_eps)
    g = gate[...] * inv_rms
    u = up[...] * inv_rms
    gate[...] = g
    up[...] = u
    hidden[...] = (g * jax.nn.sigmoid(g) * u).astype(bf16)
    core_out[:, 0:1024] = x_core[...]
    core_out[:, 1024:1792] = hidden[...]
    inv[...] = jnp.broadcast_to(inv_rms, (256, 128))


def forward(x_full, x_core, w3):
    shapes = [((256, 768), f32), ((256, 768), f32), ((256, 768), bf16), ((256, 128), f32), ((256, 1792), bf16)]
    scratch = [pltpu.VMEM((8, 2, 512, 768), bf16), pltpu.SemaphoreType.DMA((8,))]
    return call(forward_body, "forward", shapes, scratch, 18, 2 * 256 * 4096 * 1536, 16 * MiB,
                (x_full, x_core, w3), hbm=(2,), scalars=0, direct=(0,))


def backward_body(ready, spot, both, below, above, low, high, w, gate, up_val, inv, pair, products, mine, core_out, buf, acc,
                  held, sems):
    copies = fetch(w, held, sems, 2, 1, lambda k: k)
    put(buf, spot, [
        (0, 0, 0, both, 0, 256), (1, 0, 0, both, 256, 256), (0, 3, 0, below, 0, 256), (1, 3, 0, below, 256, 256),
        (0, 1, 0, above, 0, 256), (1, 1, 0, above, 256, 256), (0, 2, 0, low, 0, 128), (1, 2, 0, low, 128, 128),
        (0, 2, 128, high, 0, 128), (1, 2, 128, high, 128, 128),
    ])
    core = spot[9]
    for i in range(8):
        for ref, c in ((mine, core), (core_out, 1 - core)):
            ref[:, i * 256:(i + 1) * 256] = buf[:, lane(i * 512 + c * 256, 256, 256)]
    for k in range(8):
        copies[k].wait()
        value = dot(buf[:, k * 512:(k + 1) * 512], held[k, 0])
        acc[...] = value if k == 0 else acc[...] + value
    ready()
    d_hidden = acc[...] * inv[:, 0:1]
    g, u = gate[...], up_val[...]
    sigma = jax.nn.sigmoid(g)
    d_gate = (d_hidden * u * sigma * (1.0 + g * (1.0 - sigma))).astype(bf16)
    d_up = (d_hidden * g * sigma).astype(bf16)
    pair[:, 0:768] = d_gate
    pair[:, 768:1536] = d_up
    core_out[:, 2048:2816] = d_gate
    core_out[:, 2816:3584] = d_up
    total = jnp.sum(d_gate.astype(f32) * g + d_up.astype(f32) * u, axis=1, keepdims=True)
    products[...] = jnp.broadcast_to(total, (256, 128)).astype(bf16)


def backward(spot, pieces, w3, gate, up, inv):
    shapes = [((256, 1536), bf16), ((256, 128), bf16), ((256, 2048), bf16), ((256, 3584), bf16)]
    scratch = [pltpu.VMEM((256, 4096), bf16), pltpu.VMEM((256, 768), f32), pltpu.VMEM((8, 1, 512, 768), bf16),
               pltpu.SemaphoreType.DMA((8,))]
    return call(backward_body, "backward", shapes, scratch, 16, 2 * 256 * 4096 * 768, 8 * MiB, (spot, *pieces, w3, gate, up, inv),
                hbm=(6,), direct=range(1, 6))


def store(outs, k, value):
    half, i = k // 4, k % 4
    if i < 2:
        rows = value.shape[0]
        outs[half][i * rows:(i + 1) * rows, :] = value
    else:
        outs[2 * i - 2 + half][...] = value


def halving_shapes(rows, cols):
    return [((2 * rows, cols), bf16)] * 2 + [((rows, cols), bf16)] * 4


def outer_body(a_from, b_from, rows, cols, ready, order, *refs):
    n = len(a_from)
    a_refs, b_refs, outs = refs[:n], refs[n:2 * n], refs[2 * n:]
    ready()
    for k in range(8):
        total = None
        for a, a0, b, b0 in zip(a_refs, a_from, b_refs, b_from):
            b0 = k // 4 * cols + b0
            value = dot_tn(a[:, lane(order[k] * rows + a0, rows, 256)], b[:, b0:b0 + cols])
            total = value if total is None else total + value
        store(outs, k, total.astype(bf16))


def outer(name, order, a_list, b_list, rows, cols):
    body = functools.partial(outer_body, [f for _, f in a_list], [f for _, f in b_list], rows, cols)
    flops = 2 * 256 * len(a_list) * rows * 8 * cols
    return call(body, name, halving_shapes(rows, cols), [], 16, flops, 8 * MiB,
                (order, *[a for a, _ in a_list], *[b for b, _ in b_list]))


def branch_rows_body(ready, order, hidden, w, *refs):
    outs, held, sems = refs[:6], refs[6], refs[7]
    copies = fetch(w, held, sems, 2, 1, lambda k: k // 4 * 4 + order[k])
    ready()
    for k in range(8):
        copies[k].wait()
        store(outs, k, dot_nt(hidden[...], held[k, 0]).astype(bf16))


def branch_rows(order, hidden, w3):
    scratch = [pltpu.VMEM((8, 1, 512, 768), bf16), pltpu.SemaphoreType.DMA((8,))]
    return call(branch_rows_body, "branch_rows", halving_shapes(256, 512), scratch, 10, 2 * 256 * 768 * 4096, 8 * MiB,
                (order, hidden, w3), hbm=(2,))


def pair_rows_body(ready, order, pair, products, w, *refs):
    outs, held, sems = refs[:6], refs[6], refs[7]
    copies = fetch(w, held, sems, 0, 2, lambda k: k // 4 * 4 + order[k])
    ready()
    for k in range(8):
        copies[k].wait()
        value = dot_nt(pair[:, 0:768], held[k, 0]) + dot_nt(pair[:, 768:1536], held[k, 1])
        store(outs, k, jnp.concatenate([value.astype(bf16), products[...]], axis=1))


def pair_rows(order, pair, products, w3):
    scratch = [pltpu.VMEM((8, 2, 512, 768), bf16), pltpu.SemaphoreType.DMA((8,))]
    return call(pair_rows_body, "pair_rows", halving_shapes(256, 640), scratch, 16, 2 * 256 * 1536 * 4096, 16 * MiB,
                (order, pair, products, w3), hbm=(3,))


def second_step(terms, got, axis, done=()):
    rows = terms[2].shape[0]
    two, six, *got = lax.optimization_barrier((terms[2], terms[3], *got, *done))[:4]
    out = [(t.astype(f32) + g[rows:].astype(f32)).astype(bf16) for t, g in zip((two, six), got)]
    return out, [send(o, axis + move) for o, move in zip(out, ("^3", "^1"))]


def halve(terms, axis, done=()):
    got = [send(value, axis + move) for value, move in zip(terms[0:2], ("^1", "^3"))]
    return (got, *second_step(terms, got, axis, done))


def finish(terms, got, last, done=()):
    low, high = lax.optimization_barrier((terms[4], terms[5], *done))[:2]
    rows = terms[4].shape[0]
    return [t.astype(f32) + g[:rows].astype(f32) + e.astype(f32) for t, g, e in zip((low, high), got, last)]


def gather_both(own, cot):
    below, above, other = send(own, "y+"), send(own, "y-"), send(own, "z+2")
    up = send(rows_cat(below[:128], other), "y+")
    down = send(rows_cat(above[128:], other), "y-")
    cot_other = send(after(cot, other), "z+2")
    other_far = send(after(rows_cat(up[:128], down[:144]), cot_other), "z+2")
    both = after(rows_cat(cot, cot_other), up, down)
    cot_below, cot_above = send(both, "y+"), send(both, "y-")
    low = send(rows_cat(cot_below[:128], cot_below[256:384]), "y+")
    high = send(rows_cat(cot_above[128:256], cot_above[384:]), "y-")
    return (own, below, above, other, up, down, other_far), (both, cot_below, cot_above, low, high)


def local(inputs, gain, weights, d_out):
    width = weights.shape[0]
    t, s = lax.axis_index("tensor"), lax.axis_index("seq")
    z_hi, y = t // 4, t % 4
    x, z_lo, core = s // 4, s // 2 % 2, s % 2
    w3 = pltpu.with_memory_space_constraint(jnp.transpose(weights, (1, 0, 2)), pltpu.HBM)
    spot = jnp.stack(
        [(z_hi + dz) % 2 * 4 + (y + dy) % 4 for dz in (0, 1) for dy in range(4)] + [z_lo, core]
    ).astype(jnp.int32)

    def order(at):
        return jnp.stack([at ^ 1, at ^ 2, at ^ 3, at, at ^ 3, at ^ 2, at ^ 1, at]).astype(jnp.int32)

    own = rows_cat(inputs, jnp.broadcast_to(gain.reshape(1, 512), (16, 512)))
    x_pieces, cot_pieces = gather_both(own, d_out)
    x_full, gains, x_keep, x_core, x_same, x_cross = assemble(spot, x_pieces)
    x_same, x_cross = send(x_same, "z^3"), send(x_cross, "z^1")
    gate, up_val, hidden, inv, core_one = forward(after(x_full, *cot_pieces[1:3]), x_core, w3)
    core_one = send(core_one, "c")
    cot_pieces = (after(cot_pieces[0], x_same, x_cross), *cot_pieces[1:])
    d_pair, products, cot_mine, core_two = backward(spot, cot_pieces, w3, gate, up_val, inv)
    core_two = send(core_two, "c")
    branch_terms = branch_rows(order(y), after(hidden, d_pair), w3)
    pair_z = send(d_pair, "z^1")
    down_terms = outer("down_terms", order(x), [(after(cot_mine, branch_terms[0]), 0), (core_two, 0)], [(hidden, 0), (core_one, 1024)], 512, 384)
    branch_got = [send(value, move) for value, move in zip(branch_terms[0:2], ("y^1", "y^3"))]
    d_terms = pair_rows(order(y), after(d_pair, down_terms[0]), products, w3)
    down_got, _, down_last = halve(down_terms, "x")
    d_terms = lax.optimization_barrier((*d_terms, *branch_got))[:6]
    d_got = [send(value, move) for value, move in zip(d_terms[0:2], ("y^1", "y^3"))]
    core_three = send(jnp.concatenate([x_cross, after(pair_z, d_terms[0], *down_got)], axis=1), "c")
    pair_terms = outer(
        "pair_terms", order(x), [(x_keep, 0), (x_same, 0), (core_one, 0), (core_three, 0)],
        [(d_pair, 0), (pair_z, 0), (core_two, 2048), (core_three, 1024)], 256, 768,
    )
    down_last = lax.optimization_barrier((*down_last, pair_terms[0]))[:2]
    pair_terms = lax.optimization_barrier((*pair_terms, *down_last))[:6]
    down = finish(down_terms, down_got, down_last, (pair_terms[0],))
    d_w_down = jnp.concatenate(down, axis=1)
    lower = z_lo == 0
    theirs = jnp.where(lower, d_w_down[256:], d_w_down[:256]).astype(bf16)
    down_z = send(theirs, "z^1")
    pair_got, pair_out, pair_last = halve(pair_terms, "x", (down_z,))
    d_w_gate, d_w_up = finish(pair_terms, pair_got, pair_last)
    d_w_down = jnp.where(lower, d_w_down[:256], d_w_down[256:]) + down_z.astype(f32)

    _, d_last = second_step(d_terms, d_got, "y", (pair_terms[0],))
    d_low, d_high = finish(d_terms, d_got, d_last)
    _, branch_last = second_step(branch_terms, branch_got, "y", (pair_terms[0], *d_last))
    low, high = finish(branch_terms, branch_got, branch_last)
    upper = z_hi == 1
    mine = jnp.where(upper, d_high, d_low)
    theirs = send(after(jnp.where(upper, d_low, d_high).astype(bf16), *pair_got), "z+2")
    mine = after(mine, *pair_got) + theirs.astype(f32)
    theirs = send(after(jnp.where(upper, low, high).astype(bf16), theirs), "z+2")
    branch = (jnp.where(upper, high, low) + theirs.astype(f32)).astype(bf16)
    d_normed, products = mine[:, :512], mine[:, 512:513] / width

    x_own = inputs.astype(f32)
    d_input = (d_normed * gain.astype(f32) - inv[:, :1] * products * x_own).astype(bf16)
    d_gain = jnp.sum(d_normed * x_own, axis=0, keepdims=True)
    for move in ("c", "z^1", "x^1", "x+2"):
        if move == "x^1":
            d_gain = after(d_gain, *pair_last)
        d_gain = d_gain + send(d_gain, move)

    gain_rows = lax.dynamic_slice(gains, (0, s * 256), (1, 256)).astype(f32).reshape(256, 1)
    d_weights = jnp.stack(
        [(d_w_gate * gain_rows).astype(bf16), (d_w_up * gain_rows).astype(bf16), d_w_down.astype(bf16)], axis=1
    )
    return (branch, d_input, d_gain.reshape(512), d_weights)


def solution(mesh):
    in_specs = (P("seq", "tensor"), P("tensor"), P(None, None, "tensor"), P("seq", "tensor"))
    out_specs = (P("seq", "tensor"), P("seq", "tensor"), P("tensor"), P("seq", None, "tensor"))
    return jax.shard_map(local, mesh=mesh, in_specs=in_specs, out_specs=out_specs, check_vma=False)
```

```python
import functools
import jax
import jax.numpy as jnp
from jax import lax
from jax.experimental import pallas as pl
from jax.experimental.pallas import tpu as pltpu
from jax.sharding import PartitionSpec as P

norm_eps = 1e-05
AXES = ("tensor", "seq")
f32 = jnp.float32
bf16 = jnp.bfloat16
MiB = 1 << 20


def flat(x, y, z, c):
    x, y, z = x % 4, y % 4, z % 4
    return ((z // 2) * 4 + y) * 16 + (x * 2 + z % 2) * 2 + c


def pairs(move):
    places = [(x, y, z, c) for x in range(4) for y in range(4) for z in range(4) for c in range(2)]
    return [(flat(*place), flat(*move(*place))) for place in places]


moves = {
    "x^1": lambda x, y, z, c: (x ^ 1, y, z, c),
    "x^3": lambda x, y, z, c: (x ^ 3, y, z, c),
    "x+2": lambda x, y, z, c: (x + 2, y, z, c),
    "y+": lambda x, y, z, c: (x, y + 1, z, c),
    "y-": lambda x, y, z, c: (x, y - 1, z, c),
    "y^1": lambda x, y, z, c: (x, y ^ 1, z, c),
    "y^3": lambda x, y, z, c: (x, y ^ 3, z, c),
    "z+2": lambda x, y, z, c: (x, y, z + 2, c),
    "z^1": lambda x, y, z, c: (x, y, z ^ 1, c),
    "z^3": lambda x, y, z, c: (x, y, z ^ 3, c),
    "z^3c": lambda x, y, z, c: (x, y, z ^ 3, 1 - c),
    "c": lambda x, y, z, c: (x, y, z, 1 - c),
}


def send(value, move):
    return lax.ppermute(value, AXES, pairs(moves[move]))


def after(value, *done):
    return lax.optimization_barrier((value, *done))[0]


def rows_cat(*parts):
    return jnp.concatenate(parts, axis=0)


def dot(a, b):
    return jnp.dot(a, b, preferred_element_type=f32)


def dot_nt(a, b):
    return lax.dot_general(a, b, (((1,), (1,)), ((), ())), preferred_element_type=f32)


def dot_tn(a, b):
    return lax.dot_general(a, b, (((0,), (0,)), ((), ())), preferred_element_type=f32)


def call(body, name, shapes, scratch, limit, flops, size, args, hbm=(), scalars=1, direct=()):
    loads = [i for i in range(scalars, len(args)) if i not in hbm and i not in direct]
    spaces = [pltpu.SMEM] * scalars + [
        pltpu.HBM if i in hbm else pltpu.VMEM if i in direct else pl.ANY for i in range(scalars, len(args))
    ]

    def whole(*refs):
        ins, rest = list(refs[:len(args)]), refs[len(args):]
        outs, rest = rest[:len(shapes)], rest[len(shapes):]
        own, rest = rest[:len(scratch)], rest[len(scratch):]
        copies = []
        for n, i in enumerate(loads):
            copies.append(pltpu.make_async_copy(ins[i], rest[n], rest[-1].at[n]))
            copies[-1].start()
            ins[i] = rest[n]

        def ready():
            for copy in copies:
                copy.wait()

        body(ready, *ins, *outs, *own)

    held = [pltpu.VMEM(args[i].shape, args[i].dtype) for i in loads] + [pltpu.SemaphoreType.DMA((max(len(loads), 1),))]
    return pl.pallas_call(
        whole,
        in_specs=[pl.BlockSpec(memory_space=space) for space in spaces],
        out_specs=[pl.BlockSpec(memory_space=pltpu.VMEM) for _ in shapes],
        out_shape=[jax.ShapeDtypeStruct(shape, dtype) for shape, dtype in shapes],
        scratch_shapes=list(scratch) + held,
        compiler_params=pltpu.CompilerParams(vmem_limit_bytes=limit * MiB),
        cost_estimate=pl.CostEstimate(flops=flops, bytes_accessed=size, transcendentals=0),
        name=name,
    )(*args)


def lane(at, size, unit):
    return pl.ds(pl.multiple_of(at, unit), size)


def put(buf, spot, pieces):
    for dz, dy, row, ref, first, rows in pieces:
        buf[row:row + rows, lane(spot[dz * 4 + dy] * 512, 512, 512)] = ref[first:first + rows, :]


def fetch(w, held, sems, first, count, block_of):
    copies = []
    for k in range(8):
        rows = pl.ds(pl.multiple_of(block_of(k) * 512, 512), 512)
        copies.append(pltpu.make_async_copy(w.at[pl.ds(first, count), rows, :], held.at[k], sems.at[k]))
        copies[-1].start()
    return copies


def assemble_body(ready, spot, own, below, above, other, up2, down2, other_far, full, gains, keep, core_out, z_out,
                  cross_out):
    put(full, spot, [
        (0, 0, 0, own, 0, 272), (0, 3, 0, below, 0, 272), (0, 1, 0, above, 0, 272), (1, 0, 0, other, 0, 272),
        (0, 2, 0, up2, 0, 128), (1, 3, 0, up2, 128, 272), (0, 2, 128, down2, 0, 144), (1, 1, 0, down2, 144, 272),
        (1, 2, 0, other_far, 0, 272),
    ])
    gains[...] = full[256:272, :]
    z_lo, core = spot[8], spot[9]
    for i in range(4):
        for ref, zl, c in ((keep, z_lo, core), (core_out, z_lo, 1 - core), (z_out, 1 - z_lo, core),
                           (cross_out, 1 - z_lo, 1 - core)):
            ref[:, i * 256:(i + 1) * 256] = full[0:256, lane((2 * i + zl) * 512 + c * 256, 256, 256)]


def assemble(spot, pieces):
    shapes = [((272, 4096), bf16), ((16, 4096), bf16)] + [((256, 1024), bf16)] * 4
    return call(assemble_body, "assemble", shapes, [], 4, 0, 8 * MiB, (spot, *pieces), direct=range(1, 8))


def forward_body(ready, x_ref, x_core, w, gate, up, hidden, inv, core_out, held, sems):
    copies = fetch(w, held, sems, 0, 2, lambda k: k)
    squares = jnp.zeros((256, 1), f32)
    ready()
    for k in range(8):
        copies[k].wait()
        cols = slice(k * 512, (k + 1) * 512)
        x = x_ref[0:256, cols].astype(f32)
        squares = squares + jnp.sum(x * x, axis=1, keepdims=True)
        scaled = (x * x_ref[256:272, cols][0:1].astype(f32)).astype(bf16)
        for ref, j in ((gate, 0), (up, 1)):
            value = dot(scaled, held[k, j])
            ref[...] = value if k == 0 else ref[...] + value
    inv_rms = lax.rsqrt(squares / 4096 + norm_eps)
    g = gate[...] * inv_rms
    u = up[...] * inv_rms
    gate[...] = g
    up[...] = u
    hidden[...] = (g * jax.nn.sigmoid(g) * u).astype(bf16)
    core_out[:, 0:1024] = x_core[...]
    core_out[:, 1024:1792] = hidden[...]
    inv[...] = jnp.broadcast_to(inv_rms, (256, 128))


def forward(x_full, x_core, w3):
    shapes = [((256, 768), f32), ((256, 768), f32), ((256, 768), bf16), ((256, 128), f32), ((256, 1792), bf16)]
    scratch = [pltpu.VMEM((8, 2, 512, 768), bf16), pltpu.SemaphoreType.DMA((8,))]
    return call(forward_body, "forward", shapes, scratch, 18, 2 * 256 * 4096 * 1536, 16 * MiB,
                (x_full, x_core, w3), hbm=(2,), scalars=0, direct=(0,))


def backward_body(ready, spot, both, below, above, low, high, w, gate, up_val, inv, pair, products, mine, core_out, buf, acc,
                  held, sems):
    copies = fetch(w, held, sems, 2, 1, lambda k: k)
    put(buf, spot, [
        (0, 0, 0, both, 0, 256), (1, 0, 0, both, 256, 256), (0, 3, 0, below, 0, 256), (1, 3, 0, below, 256, 256),
        (0, 1, 0, above, 0, 256), (1, 1, 0, above, 256, 256), (0, 2, 0, low, 0, 128), (1, 2, 0, low, 128, 128),
        (0, 2, 128, high, 0, 128), (1, 2, 128, high, 128, 128),
    ])
    core = spot[9]
    for i in range(8):
        for ref, c in ((mine, core), (core_out, 1 - core)):
            ref[:, i * 256:(i + 1) * 256] = buf[:, lane(i * 512 + c * 256, 256, 256)]
    for k in range(8):
        copies[k].wait()
        value = dot(buf[:, k * 512:(k + 1) * 512], held[k, 0])
        acc[...] = value if k == 0 else acc[...] + value
    ready()
    d_hidden = acc[...] * inv[:, 0:1]
    g, u = gate[...], up_val[...]
    sigma = jax.nn.sigmoid(g)
    d_gate = (d_hidden * u * sigma * (1.0 + g * (1.0 - sigma))).astype(bf16)
    d_up = (d_hidden * g * sigma).astype(bf16)
    pair[:, 0:768] = d_gate
    pair[:, 768:1536] = d_up
    core_out[:, 2048:2816] = d_gate
    core_out[:, 2816:3584] = d_up
    total = jnp.sum(d_gate.astype(f32) * g + d_up.astype(f32) * u, axis=1, keepdims=True)
    products[...] = jnp.broadcast_to(total, (256, 128)).astype(bf16)


def backward(spot, pieces, w3, gate, up, inv):
    shapes = [((256, 1536), bf16), ((256, 128), bf16), ((256, 2048), bf16), ((256, 3584), bf16)]
    scratch = [pltpu.VMEM((256, 4096), bf16), pltpu.VMEM((256, 768), f32), pltpu.VMEM((8, 1, 512, 768), bf16),
               pltpu.SemaphoreType.DMA((8,))]
    return call(backward_body, "backward", shapes, scratch, 16, 2 * 256 * 4096 * 768, 8 * MiB, (spot, *pieces, w3, gate, up, inv),
                hbm=(6,), direct=range(1, 6))


def store(outs, k, value):
    half, i = k // 4, k % 4
    if i < 2:
        rows = value.shape[0]
        outs[half][i * rows:(i + 1) * rows, :] = value
    else:
        outs[2 * i - 2 + half][...] = value


def halving_shapes(rows, cols):
    return [((2 * rows, cols), bf16)] * 2 + [((rows, cols), bf16)] * 4


def outer_body(a_from, b_from, rows, cols, ready, order, *refs):
    n = len(a_from)
    a_refs, b_refs, outs = refs[:n], refs[n:2 * n], refs[2 * n:]
    ready()
    for k in range(8):
        total = None
        for a, a0, b, b0 in zip(a_refs, a_from, b_refs, b_from):
            b0 = k // 4 * cols + b0
            value = dot_tn(a[:, lane(order[k] * rows + a0, rows, 256)], b[:, b0:b0 + cols])
            total = value if total is None else total + value
        store(outs, k, total.astype(bf16))


def outer(name, order, a_list, b_list, rows, cols):
    body = functools.partial(outer_body, [f for _, f in a_list], [f for _, f in b_list], rows, cols)
    flops = 2 * 256 * len(a_list) * rows * 8 * cols
    return call(body, name, halving_shapes(rows, cols), [], 16, flops, 8 * MiB,
                (order, *[a for a, _ in a_list], *[b for b, _ in b_list]))


def branch_rows_body(ready, order, hidden, w, *refs):
    outs, held, sems = refs[:6], refs[6], refs[7]
    copies = fetch(w, held, sems, 2, 1, lambda k: k // 4 * 4 + order[k])
    ready()
    for k in range(8):
        copies[k].wait()
        store(outs, k, dot_nt(hidden[...], held[k, 0]).astype(bf16))


def branch_rows(order, hidden, w3):
    scratch = [pltpu.VMEM((8, 1, 512, 768), bf16), pltpu.SemaphoreType.DMA((8,))]
    return call(branch_rows_body, "branch_rows", halving_shapes(256, 512), scratch, 10, 2 * 256 * 768 * 4096, 8 * MiB,
                (order, hidden, w3), hbm=(2,))


def pair_rows_body(ready, order, pair, products, w, *refs):
    outs, held, sems = refs[:6], refs[6], refs[7]
    copies = fetch(w, held, sems, 0, 2, lambda k: k // 4 * 4 + order[k])
    ready()
    for k in range(8):
        copies[k].wait()
        value = dot_nt(pair[:, 0:768], held[k, 0]) + dot_nt(pair[:, 768:1536], held[k, 1])
        store(outs, k, jnp.concatenate([value.astype(bf16), products[...]], axis=1))


def pair_rows(order, pair, products, w3):
    scratch = [pltpu.VMEM((8, 2, 512, 768), bf16), pltpu.SemaphoreType.DMA((8,))]
    return call(pair_rows_body, "pair_rows", halving_shapes(256, 640), scratch, 16, 2 * 256 * 1536 * 4096, 16 * MiB,
                (order, pair, products, w3), hbm=(3,))


def second_step(terms, got, axis, done=()):
    rows = terms[2].shape[0]
    two, six, *got = lax.optimization_barrier((terms[2], terms[3], *got, *done))[:4]
    out = [(t.astype(f32) + g[rows:].astype(f32)).astype(bf16) for t, g in zip((two, six), got)]
    return out, [send(o, axis + move) for o, move in zip(out, ("^3", "^1"))]


def halve(terms, axis, done=()):
    got = [send(value, axis + move) for value, move in zip(terms[0:2], ("^1", "^3"))]
    return (got, *second_step(terms, got, axis, done))


def finish(terms, got, last, done=()):
    low, high = lax.optimization_barrier((terms[4], terms[5], *done))[:2]
    rows = terms[4].shape[0]
    return [t.astype(f32) + g[:rows].astype(f32) + e.astype(f32) for t, g, e in zip((low, high), got, last)]


def gather_both(own, cot):
    below, above, other = send(own, "y+"), send(own, "y-"), send(own, "z+2")
    up = send(rows_cat(below[:128], other), "y+")
    down = send(rows_cat(above[128:], other), "y-")
    cot_other = send(after(cot, other), "z+2")
    other_far = send(after(rows_cat(up[:128], down[:144]), cot_other), "z+2")
    both = after(rows_cat(cot, cot_other), up, down)
    cot_below, cot_above = send(both, "y+"), send(both, "y-")
    low = send(rows_cat(cot_below[:128], cot_below[256:384]), "y+")
    high = send(rows_cat(cot_above[128:256], cot_above[384:]), "y-")
    return (own, below, above, other, up, down, other_far), (both, cot_below, cot_above, low, high)


def local(inputs, gain, weights, d_out):
    width = weights.shape[0]
    t, s = lax.axis_index("tensor"), lax.axis_index("seq")
    z_hi, y = t // 4, t % 4
    x, z_lo, core = s // 4, s // 2 % 2, s % 2
    w3 = pltpu.with_memory_space_constraint(jnp.transpose(weights, (1, 0, 2)), pltpu.HBM)
    spot = jnp.stack(
        [(z_hi + dz) % 2 * 4 + (y + dy) % 4 for dz in (0, 1) for dy in range(4)] + [z_lo, core]
    ).astype(jnp.int32)

    def order(at):
        return jnp.stack([at ^ 1, at ^ 2, at ^ 3, at, at ^ 3, at ^ 2, at ^ 1, at]).astype(jnp.int32)

    own = rows_cat(inputs, jnp.broadcast_to(gain.reshape(1, 512), (16, 512)))
    x_pieces, cot_pieces = gather_both(own, d_out)
    x_full, gains, x_keep, x_core, x_same, x_cross = assemble(spot, x_pieces)
    x_same, x_cross = send(x_same, "z^3"), send(x_cross, "z^1")
    gate, up_val, hidden, inv, core_one = forward(after(x_full, *cot_pieces[1:3]), x_core, w3)
    core_one = send(core_one, "c")
    cot_pieces = (after(cot_pieces[0], x_same, x_cross), *cot_pieces[1:])
    d_pair, products, cot_mine, core_two = backward(spot, cot_pieces, w3, gate, up_val, inv)
    core_two = send(core_two, "c")
    branch_terms = branch_rows(order(y), after(hidden, d_pair), w3)
    pair_z = send(d_pair, "z^1")
    down_terms = outer("down_terms", order(x), [(after(cot_mine, branch_terms[0]), 0), (core_two, 0)], [(hidden, 0), (core_one, 1024)], 512, 384)
    branch_got = [send(value, move) for value, move in zip(branch_terms[0:2], ("y^1", "y^3"))]
    d_terms = pair_rows(order(y), after(d_pair, down_terms[0]), products, w3)
    down_got, _, down_last = halve(down_terms, "x")
    d_terms = lax.optimization_barrier((*d_terms, *branch_got))[:6]
    d_got = [send(value, move) for value, move in zip(d_terms[0:2], ("y^1", "y^3"))]
    core_three = send(jnp.concatenate([x_cross, after(pair_z, d_terms[0], *down_got)], axis=1), "c")
    pair_terms = outer(
        "pair_terms", order(x), [(x_keep, 0), (x_same, 0), (core_one, 0), (core_three, 0)],
        [(d_pair, 0), (pair_z, 0), (core_two, 2048), (core_three, 1024)], 256, 768,
    )
    down_last = lax.optimization_barrier((*down_last, pair_terms[0]))[:2]
    pair_terms = lax.optimization_barrier((*pair_terms, *down_last))[:6]
    down = finish(down_terms, down_got, down_last, (pair_terms[0],))
    d_w_down = jnp.concatenate(down, axis=1)
    lower = z_lo == 0
    theirs = jnp.where(lower, d_w_down[256:], d_w_down[:256]).astype(bf16)
    down_z = send(theirs, "z^1")
    pair_got, pair_out, pair_last = halve(pair_terms, "x", (down_z,))
    d_w_gate, d_w_up = finish(pair_terms, pair_got, pair_last)
    d_w_down = jnp.where(lower, d_w_down[:256], d_w_down[256:]) + down_z.astype(f32)

    _, d_last = second_step(d_terms, d_got, "y", (pair_terms[0],))
    d_low, d_high = finish(d_terms, d_got, d_last)
    _, branch_last = second_step(branch_terms, branch_got, "y", (pair_terms[0], *d_last))
    low, high = finish(branch_terms, branch_got, branch_last)
    upper = z_hi == 1
    mine = jnp.where(upper, d_high, d_low)
    theirs = send(jnp.where(upper, d_low, d_high).astype(bf16), "z+2")
    mine = mine + theirs.astype(f32)
    theirs = send(after(jnp.where(upper, low, high).astype(bf16), theirs), "z+2")
    branch = (jnp.where(upper, high, low) + theirs.astype(f32)).astype(bf16)
    d_normed, products = mine[:, :512], mine[:, 512:513] / width

    x_own = inputs.astype(f32)
    d_input = (d_normed * gain.astype(f32) - inv[:, :1] * products * x_own).astype(bf16)
    d_gain = jnp.sum(d_normed * x_own, axis=0, keepdims=True)
    for move in ("c", "z^1", "x^1", "x+2"):
        if move == "x^1":
            d_gain = after(d_gain, *pair_last)
        d_gain = d_gain + send(d_gain, move)

    gain_rows = lax.dynamic_slice(gains, (0, s * 256), (1, 256)).astype(f32).reshape(256, 1)
    d_weights = jnp.stack(
        [(d_w_gate * gain_rows).astype(bf16), (d_w_up * gain_rows).astype(bf16), d_w_down.astype(bf16)], axis=1
    )
    return (branch, d_input, d_gain.reshape(512), d_weights)


def solution(mesh):
    in_specs = (P("seq", "tensor"), P("tensor"), P(None, None, "tensor"), P("seq", "tensor"))
    out_specs = (P("seq", "tensor"), P("seq", "tensor"), P("tensor"), P("seq", None, "tensor"))
    return jax.shard_map(local, mesh=mesh, in_specs=in_specs, out_specs=out_specs, check_vma=False)
```

```python
import functools
import jax
import jax.numpy as jnp
from jax import lax
from jax.experimental import pallas as pl
from jax.experimental.pallas import tpu as pltpu
from jax.sharding import PartitionSpec as P

norm_eps = 1e-05
AXES = ("tensor", "seq")
f32 = jnp.float32
bf16 = jnp.bfloat16
MiB = 1 << 20


def flat(x, y, z, c):
    x, y, z = x % 4, y % 4, z % 4
    return ((z // 2) * 4 + y) * 16 + (x * 2 + z % 2) * 2 + c


def pairs(move):
    places = [(x, y, z, c) for x in range(4) for y in range(4) for z in range(4) for c in range(2)]
    return [(flat(*place), flat(*move(*place))) for place in places]


moves = {
    "x^1": lambda x, y, z, c: (x ^ 1, y, z, c),
    "x^3": lambda x, y, z, c: (x ^ 3, y, z, c),
    "x+2": lambda x, y, z, c: (x + 2, y, z, c),
    "y+": lambda x, y, z, c: (x, y + 1, z, c),
    "y-": lambda x, y, z, c: (x, y - 1, z, c),
    "y^1": lambda x, y, z, c: (x, y ^ 1, z, c),
    "y^3": lambda x, y, z, c: (x, y ^ 3, z, c),
    "z+2": lambda x, y, z, c: (x, y, z + 2, c),
    "z^1": lambda x, y, z, c: (x, y, z ^ 1, c),
    "z^3": lambda x, y, z, c: (x, y, z ^ 3, c),
    "z^3c": lambda x, y, z, c: (x, y, z ^ 3, 1 - c),
    "c": lambda x, y, z, c: (x, y, z, 1 - c),
}


def send(value, move):
    return lax.ppermute(value, AXES, pairs(moves[move]))


def after(value, *done):
    return lax.optimization_barrier((value, *done))[0]


def rows_cat(*parts):
    return jnp.concatenate(parts, axis=0)


def dot(a, b):
    return jnp.dot(a, b, preferred_element_type=f32)


def dot_nt(a, b):
    return lax.dot_general(a, b, (((1,), (1,)), ((), ())), preferred_element_type=f32)


def dot_tn(a, b):
    return lax.dot_general(a, b, (((0,), (0,)), ((), ())), preferred_element_type=f32)


def call(body, name, shapes, scratch, limit, flops, size, args, hbm=(), scalars=1, direct=()):
    loads = [i for i in range(scalars, len(args)) if i not in hbm and i not in direct]
    spaces = [pltpu.SMEM] * scalars + [
        pltpu.HBM if i in hbm else pltpu.VMEM if i in direct else pl.ANY for i in range(scalars, len(args))
    ]

    def whole(*refs):
        ins, rest = list(refs[:len(args)]), refs[len(args):]
        outs, rest = rest[:len(shapes)], rest[len(shapes):]
        own, rest = rest[:len(scratch)], rest[len(scratch):]
        copies = []
        for n, i in enumerate(loads):
            copies.append(pltpu.make_async_copy(ins[i], rest[n], rest[-1].at[n]))
            copies[-1].start()
            ins[i] = rest[n]

        def ready():
            for copy in copies:
                copy.wait()

        body(ready, *ins, *outs, *own)

    held = [pltpu.VMEM(args[i].shape, args[i].dtype) for i in loads] + [pltpu.SemaphoreType.DMA((max(len(loads), 1),))]
    return pl.pallas_call(
        whole,
        in_specs=[pl.BlockSpec(memory_space=space) for space in spaces],
        out_specs=[pl.BlockSpec(memory_space=pltpu.VMEM) for _ in shapes],
        out_shape=[jax.ShapeDtypeStruct(shape, dtype) for shape, dtype in shapes],
        scratch_shapes=list(scratch) + held,
        compiler_params=pltpu.CompilerParams(vmem_limit_bytes=limit * MiB),
        cost_estimate=pl.CostEstimate(flops=flops, bytes_accessed=size, transcendentals=0),
        name=name,
    )(*args)


def lane(at, size, unit):
    return pl.ds(pl.multiple_of(at, unit), size)


def put(buf, spot, pieces):
    for dz, dy, row, ref, first, rows in pieces:
        buf[row:row + rows, lane(spot[dz * 4 + dy] * 512, 512, 512)] = ref[first:first + rows, :]


def fetch(w, held, sems, first, count, block_of):
    copies = []
    for k in range(8):
        rows = pl.ds(pl.multiple_of(block_of(k) * 512, 512), 512)
        copies.append(pltpu.make_async_copy(w.at[pl.ds(first, count), rows, :], held.at[k], sems.at[k]))
        copies[-1].start()
    return copies


def assemble_body(ready, spot, own, below, above, other, up2, down2, other_far, full, gains, keep, core_out, z_out,
                  cross_out):
    put(full, spot, [
        (0, 0, 0, own, 0, 272), (0, 3, 0, below, 0, 272), (0, 1, 0, above, 0, 272), (1, 0, 0, other, 0, 272),
        (0, 2, 0, up2, 0, 128), (1, 3, 0, up2, 128, 272), (0, 2, 128, down2, 0, 144), (1, 1, 0, down2, 144, 272),
        (1, 2, 0, other_far, 0, 272),
    ])
    gains[...] = full[256:272, :]
    z_lo, core = spot[8], spot[9]
    for i in range(4):
        for ref, zl, c in ((keep, z_lo, core), (core_out, z_lo, 1 - core), (z_out, 1 - z_lo, core),
                           (cross_out, 1 - z_lo, 1 - core)):
            ref[:, i * 256:(i + 1) * 256] = full[0:256, lane((2 * i + zl) * 512 + c * 256, 256, 256)]


def assemble(spot, pieces):
    shapes = [((272, 4096), bf16), ((16, 4096), bf16)] + [((256, 1024), bf16)] * 4
    return call(assemble_body, "assemble", shapes, [], 4, 0, 8 * MiB, (spot, *pieces), direct=range(1, 8))


def forward_body(ready, x_ref, x_core, w, gate, up, hidden, inv, core_out, held, sems):
    copies = fetch(w, held, sems, 0, 2, lambda k: k)
    squares = jnp.zeros((256, 1), f32)
    ready()
    for k in range(8):
        copies[k].wait()
        cols = slice(k * 512, (k + 1) * 512)
        x = x_ref[0:256, cols].astype(f32)
        squares = squares + jnp.sum(x * x, axis=1, keepdims=True)
        scaled = (x * x_ref[256:272, cols][0:1].astype(f32)).astype(bf16)
        for ref, j in ((gate, 0), (up, 1)):
            value = dot(scaled, held[k, j])
            ref[...] = value if k == 0 else ref[...] + value
    inv_rms = lax.rsqrt(squares / 4096 + norm_eps)
    g = gate[...] * inv_rms
    u = up[...] * inv_rms
    gate[...] = g
    up[...] = u
    hidden[...] = (g * jax.nn.sigmoid(g) * u).astype(bf16)
    core_out[:, 0:1024] = x_core[...]
    core_out[:, 1024:1792] = hidden[...]
    inv[...] = jnp.broadcast_to(inv_rms, (256, 128))


def forward(x_full, x_core, w3):
    shapes = [((256, 768), f32), ((256, 768), f32), ((256, 768), bf16), ((256, 128), f32), ((256, 1792), bf16)]
    scratch = [pltpu.VMEM((8, 2, 512, 768), bf16), pltpu.SemaphoreType.DMA((8,))]
    return call(forward_body, "forward", shapes, scratch, 18, 2 * 256 * 4096 * 1536, 16 * MiB,
                (x_full, x_core, w3), hbm=(2,), scalars=0, direct=(0,))


def backward_body(ready, spot, both, below, above, low, high, w, gate, up_val, inv, pair, products, mine, core_out, buf, acc,
                  held, sems):
    copies = fetch(w, held, sems, 2, 1, lambda k: k)
    put(buf, spot, [
        (0, 0, 0, both, 0, 256), (1, 0, 0, both, 256, 256), (0, 3, 0, below, 0, 256), (1, 3, 0, below, 256, 256),
        (0, 1, 0, above, 0, 256), (1, 1, 0, above, 256, 256), (0, 2, 0, low, 0, 128), (1, 2, 0, low, 128, 128),
        (0, 2, 128, high, 0, 128), (1, 2, 128, high, 128, 128),
    ])
    core = spot[9]
    for i in range(8):
        for ref, c in ((mine, core), (core_out, 1 - core)):
            ref[:, i * 256:(i + 1) * 256] = buf[:, lane(i * 512 + c * 256, 256, 256)]
    for k in range(8):
        copies[k].wait()
        value = dot(buf[:, k * 512:(k + 1) * 512], held[k, 0])
        acc[...] = value if k == 0 else acc[...] + value
    ready()
    d_hidden = acc[...] * inv[:, 0:1]
    g, u = gate[...], up_val[...]
    sigma = jax.nn.sigmoid(g)
    d_gate = (d_hidden * u * sigma * (1.0 + g * (1.0 - sigma))).astype(bf16)
    d_up = (d_hidden * g * sigma).astype(bf16)
    pair[:, 0:768] = d_gate
    pair[:, 768:1536] = d_up
    core_out[:, 2048:2816] = d_gate
    core_out[:, 2816:3584] = d_up
    total = jnp.sum(d_gate.astype(f32) * g + d_up.astype(f32) * u, axis=1, keepdims=True)
    products[...] = jnp.broadcast_to(total, (256, 128)).astype(bf16)


def backward(spot, pieces, w3, gate, up, inv):
    shapes = [((256, 1536), bf16), ((256, 128), bf16), ((256, 2048), bf16), ((256, 3584), bf16)]
    scratch = [pltpu.VMEM((256, 4096), bf16), pltpu.VMEM((256, 768), f32), pltpu.VMEM((8, 1, 512, 768), bf16),
               pltpu.SemaphoreType.DMA((8,))]
    return call(backward_body, "backward", shapes, scratch, 16, 2 * 256 * 4096 * 768, 8 * MiB, (spot, *pieces, w3, gate, up, inv),
                hbm=(6,), direct=range(1, 6))


def store(outs, k, value):
    half, i = k // 4, k % 4
    if i < 2:
        rows = value.shape[0]
        outs[half][i * rows:(i + 1) * rows, :] = value
    else:
        outs[2 * i - 2 + half][...] = value


def halving_shapes(rows, cols):
    return [((2 * rows, cols), bf16)] * 2 + [((rows, cols), bf16)] * 4


def outer_body(a_from, b_from, rows, cols, ready, order, *refs):
    n = len(a_from)
    a_refs, b_refs, outs = refs[:n], refs[n:2 * n], refs[2 * n:]
    ready()
    for k in range(8):
        total = None
        for a, a0, b, b0 in zip(a_refs, a_from, b_refs, b_from):
            b0 = k // 4 * cols + b0
            value = dot_tn(a[:, lane(order[k] * rows + a0, rows, 256)], b[:, b0:b0 + cols])
            total = value if total is None else total + value
        store(outs, k, total.astype(bf16))


def outer(name, order, a_list, b_list, rows, cols):
    body = functools.partial(outer_body, [f for _, f in a_list], [f for _, f in b_list], rows, cols)
    flops = 2 * 256 * len(a_list) * rows * 8 * cols
    return call(body, name, halving_shapes(rows, cols), [], 16, flops, 8 * MiB,
                (order, *[a for a, _ in a_list], *[b for b, _ in b_list]))


def branch_rows_body(ready, order, hidden, w, *refs):
    outs, held, sems = refs[:6], refs[6], refs[7]
    copies = fetch(w, held, sems, 2, 1, lambda k: k // 4 * 4 + order[k])
    ready()
    for k in range(8):
        copies[k].wait()
        store(outs, k, dot_nt(hidden[...], held[k, 0]).astype(bf16))


def branch_rows(order, hidden, w3):
    scratch = [pltpu.VMEM((8, 1, 512, 768), bf16), pltpu.SemaphoreType.DMA((8,))]
    return call(branch_rows_body, "branch_rows", halving_shapes(256, 512), scratch, 10, 2 * 256 * 768 * 4096, 8 * MiB,
                (order, hidden, w3), hbm=(2,))


def pair_rows_body(ready, order, pair, products, w, *refs):
    outs, held, sems = refs[:6], refs[6], refs[7]
    copies = fetch(w, held, sems, 0, 2, lambda k: k // 4 * 4 + order[k])
    ready()
    for k in range(8):
        copies[k].wait()
        value = dot_nt(pair[:, 0:768], held[k, 0]) + dot_nt(pair[:, 768:1536], held[k, 1])
        store(outs, k, jnp.concatenate([value.astype(bf16), products[...]], axis=1))


def pair_rows(order, pair, products, w3):
    scratch = [pltpu.VMEM((8, 2, 512, 768), bf16), pltpu.SemaphoreType.DMA((8,))]
    return call(pair_rows_body, "pair_rows", halving_shapes(256, 640), scratch, 16, 2 * 256 * 1536 * 4096, 16 * MiB,
                (order, pair, products, w3), hbm=(3,))


def second_step(terms, got, axis, done=()):
    rows = terms[2].shape[0]
    two, six, *got = lax.optimization_barrier((terms[2], terms[3], *got, *done))[:4]
    out = [(t.astype(f32) + g[rows:].astype(f32)).astype(bf16) for t, g in zip((two, six), got)]
    return out, [send(o, axis + move) for o, move in zip(out, ("^3", "^1"))]


def halve(terms, axis, done=()):
    got = [send(value, axis + move) for value, move in zip(terms[0:2], ("^1", "^3"))]
    return (got, *second_step(terms, got, axis, done))


def finish(terms, got, last, done=()):
    low, high = lax.optimization_barrier((terms[4], terms[5], *done))[:2]
    rows = terms[4].shape[0]
    return [t.astype(f32) + g[:rows].astype(f32) + e.astype(f32) for t, g, e in zip((low, high), got, last)]


def gather_both(own, cot):
    below, above, other = send(own, "y+"), send(own, "y-"), send(own, "z+2")
    up = send(rows_cat(below[:128], other), "y+")
    down = send(rows_cat(above[128:], other), "y-")
    cot_other = send(after(cot, other), "z+2")
    other_far = send(after(rows_cat(up[:128], down[:144]), cot_other), "z+2")
    both = after(rows_cat(cot, cot_other), up, down)
    cot_below, cot_above = send(both, "y+"), send(both, "y-")
    low = send(rows_cat(cot_below[:128], cot_below[256:384]), "y+")
    high = send(rows_cat(cot_above[128:256], cot_above[384:]), "y-")
    return (own, below, above, other, up, down, other_far), (both, cot_below, cot_above, low, high)


def local(inputs, gain, weights, d_out):
    width = weights.shape[0]
    t, s = lax.axis_index("tensor"), lax.axis_index("seq")
    z_hi, y = t // 4, t % 4
    x, z_lo, core = s // 4, s // 2 % 2, s % 2
    w3 = pltpu.with_memory_space_constraint(jnp.transpose(weights, (1, 0, 2)), pltpu.HBM)
    spot = jnp.stack(
        [(z_hi + dz) % 2 * 4 + (y + dy) % 4 for dz in (0, 1) for dy in range(4)] + [z_lo, core]
    ).astype(jnp.int32)

    def order(at):
        return jnp.stack([at ^ 1, at ^ 2, at ^ 3, at, at ^ 3, at ^ 2, at ^ 1, at]).astype(jnp.int32)

    own = rows_cat(inputs, jnp.broadcast_to(gain.reshape(1, 512), (16, 512)))
    x_pieces, cot_pieces = gather_both(own, d_out)
    x_full, gains, x_keep, x_core, x_same, x_cross = assemble(spot, x_pieces)
    x_same, x_cross = send(x_same, "z^3"), send(x_cross, "z^1")
    gate, up_val, hidden, inv, core_one = forward(after(x_full, *cot_pieces[1:3]), x_core, w3)
    core_one = send(core_one, "c")
    cot_pieces = (after(cot_pieces[0], x_same, x_cross), *cot_pieces[1:])
    d_pair, products, cot_mine, core_two = backward(spot, cot_pieces, w3, gate, up_val, inv)
    core_two = send(core_two, "c")
    branch_terms = branch_rows(order(y), after(hidden, d_pair), w3)
    pair_z = send(d_pair, "z^1")
    down_terms = outer("down_terms", order(x), [(after(cot_mine, branch_terms[0]), 0), (core_two, 0)], [(hidden, 0), (core_one, 1024)], 512, 384)
    branch_got = [send(value, move) for value, move in zip(branch_terms[0:2], ("y^1", "y^3"))]
    d_terms = pair_rows(order(y), after(d_pair, down_terms[0]), products, w3)
    down_got, _, down_last = halve(down_terms, "x")
    d_terms = lax.optimization_barrier((*d_terms, *branch_got))[:6]
    d_got = [send(value, move) for value, move in zip(d_terms[0:2], ("y^1", "y^3"))]
    core_three = send(jnp.concatenate([x_cross, after(pair_z, d_terms[0], *down_got)], axis=1), "c")
    pair_terms = outer(
        "pair_terms", order(x), [(x_keep, 0), (x_same, 0), (core_one, 0), (core_three, 0)],
        [(d_pair, 0), (pair_z, 0), (core_two, 2048), (core_three, 1024)], 256, 768,
    )
    down_last = lax.optimization_barrier((*down_last, pair_terms[0]))[:2]
    pair_terms = lax.optimization_barrier((*pair_terms, *down_last))[:6]
    down = finish(down_terms, down_got, down_last, (pair_terms[0],))
    d_w_down = jnp.concatenate(down, axis=1)
    lower = z_lo == 0
    theirs = jnp.where(lower, d_w_down[256:], d_w_down[:256]).astype(bf16)
    down_z = send(theirs, "z^1")
    pair_got, pair_out, pair_last = halve(pair_terms, "x", (down_z,))
    d_w_gate, d_w_up = finish(pair_terms, pair_got, pair_last)
    d_w_down = jnp.where(lower, d_w_down[:256], d_w_down[256:]) + down_z.astype(f32)

    _, d_last = second_step(d_terms, d_got, "y", (pair_terms[0],))
    d_low, d_high = finish(d_terms, d_got, d_last)
    _, branch_last = second_step(branch_terms, branch_got, "y", (pair_terms[0], *d_last))
    low, high = finish(branch_terms, branch_got, branch_last)
    upper = z_hi == 1
    mine = jnp.where(upper, d_high, d_low)
    theirs = send(after(jnp.where(upper, d_low, d_high).astype(bf16), *pair_got), "z+2")
    mine = after(mine, *pair_got) + theirs.astype(f32)
    theirs = send(after(jnp.where(upper, low, high).astype(bf16), theirs), "z+2")
    branch = (jnp.where(upper, high, low) + theirs.astype(f32)).astype(bf16)
    d_normed, products = mine[:, :512], mine[:, 512:513] / width

    x_own = inputs.astype(f32)
    d_input = (d_normed * gain.astype(f32) - inv[:, :1] * products * x_own).astype(bf16)
    d_gain = jnp.sum(d_normed * x_own, axis=0, keepdims=True)
    for move in ("c", "z^1"):
        d_gain = d_gain + send(d_gain, move)
    d_gain = after(d_gain, *pair_last)
    beside, across, opposite = send(d_gain, "x^1"), send(d_gain, "x^3"), send(d_gain, "x+2")
    d_gain = (d_gain + beside) + (across + opposite)

    gain_rows = lax.dynamic_slice(gains, (0, s * 256), (1, 256)).astype(f32).reshape(256, 1)
    d_weights = jnp.stack(
        [(d_w_gate * gain_rows).astype(bf16), (d_w_up * gain_rows).astype(bf16), d_w_down.astype(bf16)], axis=1
    )
    return (branch, d_input, d_gain.reshape(512), d_weights)


def solution(mesh):
    in_specs = (P("seq", "tensor"), P("tensor"), P(None, None, "tensor"), P("seq", "tensor"))
    out_specs = (P("seq", "tensor"), P("seq", "tensor"), P("tensor"), P("seq", None, "tensor"))
    return jax.shard_map(local, mesh=mesh, in_specs=in_specs, out_specs=out_specs, check_vma=False)
```

```python
import functools
import jax
import jax.numpy as jnp
from jax import lax
from jax.experimental import pallas as pl
from jax.experimental.pallas import tpu as pltpu
from jax.sharding import PartitionSpec as P

norm_eps = 1e-05
AXES = ("tensor", "seq")
f32 = jnp.float32
bf16 = jnp.bfloat16
MiB = 1 << 20


def flat(x, y, z, c):
    x, y, z = x % 4, y % 4, z % 4
    return ((z // 2) * 4 + y) * 16 + (x * 2 + z % 2) * 2 + c


def pairs(move):
    places = [(x, y, z, c) for x in range(4) for y in range(4) for z in range(4) for c in range(2)]
    return [(flat(*place), flat(*move(*place))) for place in places]


moves = {
    "x^1": lambda x, y, z, c: (x ^ 1, y, z, c),
    "x^3": lambda x, y, z, c: (x ^ 3, y, z, c),
    "x+2": lambda x, y, z, c: (x + 2, y, z, c),
    "y+": lambda x, y, z, c: (x, y + 1, z, c),
    "y-": lambda x, y, z, c: (x, y - 1, z, c),
    "y^1": lambda x, y, z, c: (x, y ^ 1, z, c),
    "y^3": lambda x, y, z, c: (x, y ^ 3, z, c),
    "z+2": lambda x, y, z, c: (x, y, z + 2, c),
    "z^1": lambda x, y, z, c: (x, y, z ^ 1, c),
    "z^3": lambda x, y, z, c: (x, y, z ^ 3, c),
    "z^3c": lambda x, y, z, c: (x, y, z ^ 3, 1 - c),
    "c": lambda x, y, z, c: (x, y, z, 1 - c),
}


def send(value, move):
    return lax.ppermute(value, AXES, pairs(moves[move]))


def after(value, *done):
    return lax.optimization_barrier((value, *done))[0]


def rows_cat(*parts):
    return jnp.concatenate(parts, axis=0)


def dot(a, b):
    return jnp.dot(a, b, preferred_element_type=f32)


def dot_nt(a, b):
    return lax.dot_general(a, b, (((1,), (1,)), ((), ())), preferred_element_type=f32)


def dot_tn(a, b):
    return lax.dot_general(a, b, (((0,), (0,)), ((), ())), preferred_element_type=f32)


def call(body, name, shapes, scratch, limit, flops, size, args, hbm=(), scalars=1, direct=()):
    loads = [i for i in range(scalars, len(args)) if i not in hbm and i not in direct]
    spaces = [pltpu.SMEM] * scalars + [
        pltpu.HBM if i in hbm else pltpu.VMEM if i in direct else pl.ANY for i in range(scalars, len(args))
    ]

    def whole(*refs):
        ins, rest = list(refs[:len(args)]), refs[len(args):]
        outs, rest = rest[:len(shapes)], rest[len(shapes):]
        own, rest = rest[:len(scratch)], rest[len(scratch):]
        copies = []
        for n, i in enumerate(loads):
            copies.append(pltpu.make_async_copy(ins[i], rest[n], rest[-1].at[n]))
            copies[-1].start()
            ins[i] = rest[n]

        def ready():
            for copy in copies:
                copy.wait()

        body(ready, *ins, *outs, *own)

    held = [pltpu.VMEM(args[i].shape, args[i].dtype) for i in loads] + [pltpu.SemaphoreType.DMA((max(len(loads), 1),))]
    return pl.pallas_call(
        whole,
        in_specs=[pl.BlockSpec(memory_space=space) for space in spaces],
        out_specs=[pl.BlockSpec(memory_space=pltpu.VMEM) for _ in shapes],
        out_shape=[jax.ShapeDtypeStruct(shape, dtype) for shape, dtype in shapes],
        scratch_shapes=list(scratch) + held,
        compiler_params=pltpu.CompilerParams(vmem_limit_bytes=limit * MiB),
        cost_estimate=pl.CostEstimate(flops=flops, bytes_accessed=size, transcendentals=0),
        name=name,
    )(*args)


def lane(at, size, unit):
    return pl.ds(pl.multiple_of(at, unit), size)


def put(buf, spot, pieces):
    for dz, dy, row, ref, first, rows in pieces:
        buf[row:row + rows, lane(spot[dz * 4 + dy] * 512, 512, 512)] = ref[first:first + rows, :]


def fetch(w, held, sems, first, count, block_of):
    copies = []
    for k in range(8):
        rows = pl.ds(pl.multiple_of(block_of(k) * 512, 512), 512)
        copies.append(pltpu.make_async_copy(w.at[pl.ds(first, count), rows, :], held.at[k], sems.at[k]))
        copies[-1].start()
    return copies


def assemble_body(ready, spot, own, below, above, other, up2, down2, other_far, full, gains, keep, core_out, z_out,
                  cross_out):
    put(full, spot, [
        (0, 0, 0, own, 0, 272), (0, 3, 0, below, 0, 272), (0, 1, 0, above, 0, 272), (1, 0, 0, other, 0, 272),
        (0, 2, 0, up2, 0, 128), (1, 3, 0, up2, 128, 272), (0, 2, 128, down2, 0, 144), (1, 1, 0, down2, 144, 272),
        (1, 2, 0, other_far, 0, 272),
    ])
    gains[...] = full[256:272, :]
    z_lo, core = spot[8], spot[9]
    for i in range(4):
        for ref, zl, c in ((keep, z_lo, core), (core_out, z_lo, 1 - core), (z_out, 1 - z_lo, core),
                           (cross_out, 1 - z_lo, 1 - core)):
            ref[:, i * 256:(i + 1) * 256] = full[0:256, lane((2 * i + zl) * 512 + c * 256, 256, 256)]


def assemble(spot, pieces):
    shapes = [((272, 4096), bf16), ((16, 4096), bf16)] + [((256, 1024), bf16)] * 4
    return call(assemble_body, "assemble", shapes, [], 4, 0, 8 * MiB, (spot, *pieces), direct=range(1, 8))


def forward_body(ready, x_ref, x_core, w, gate, up, hidden, inv, core_out, held, sems):
    copies = fetch(w, held, sems, 0, 2, lambda k: k)
    squares = jnp.zeros((256, 1), f32)
    ready()
    for k in range(8):
        copies[k].wait()
        cols = slice(k * 512, (k + 1) * 512)
        x = x_ref[0:256, cols].astype(f32)
        squares = squares + jnp.sum(x * x, axis=1, keepdims=True)
        scaled = (x * x_ref[256:272, cols][0:1].astype(f32)).astype(bf16)
        for ref, j in ((gate, 0), (up, 1)):
            value = dot(scaled, held[k, j])
            ref[...] = value if k == 0 else ref[...] + value
    inv_rms = lax.rsqrt(squares / 4096 + norm_eps)
    g = gate[...] * inv_rms
    u = up[...] * inv_rms
    gate[...] = g
    up[...] = u
    hidden[...] = (g * jax.nn.sigmoid(g) * u).astype(bf16)
    core_out[:, 0:1024] = x_core[...]
    core_out[:, 1024:1792] = hidden[...]
    inv[...] = jnp.broadcast_to(inv_rms, (256, 128))


def forward(x_full, x_core, w3):
    shapes = [((256, 768), f32), ((256, 768), f32), ((256, 768), bf16), ((256, 128), f32), ((256, 1792), bf16)]
    scratch = [pltpu.VMEM((8, 2, 512, 768), bf16), pltpu.SemaphoreType.DMA((8,))]
    return call(forward_body, "forward", shapes, scratch, 18, 2 * 256 * 4096 * 1536, 16 * MiB,
                (x_full, x_core, w3), hbm=(2,), scalars=0, direct=(0,))


def backward_body(ready, spot, both, below, above, low, high, w, gate, up_val, inv, pair, products, mine, core_out, buf, acc,
                  held, sems):
    copies = fetch(w, held, sems, 2, 1, lambda k: k)
    put(buf, spot, [
        (0, 0, 0, both, 0, 256), (1, 0, 0, both, 256, 256), (0, 3, 0, below, 0, 256), (1, 3, 0, below, 256, 256),
        (0, 1, 0, above, 0, 256), (1, 1, 0, above, 256, 256), (0, 2, 0, low, 0, 128), (1, 2, 0, low, 128, 128),
        (0, 2, 128, high, 0, 128), (1, 2, 128, high, 128, 128),
    ])
    core = spot[9]
    for i in range(8):
        for ref, c in ((mine, core), (core_out, 1 - core)):
            ref[:, i * 256:(i + 1) * 256] = buf[:, lane(i * 512 + c * 256, 256, 256)]
    for k in range(8):
        copies[k].wait()
        value = dot(buf[:, k * 512:(k + 1) * 512], held[k, 0])
        acc[...] = value if k == 0 else acc[...] + value
    ready()
    d_hidden = acc[...] * inv[:, 0:1]
    g, u = gate[...], up_val[...]
    sigma = jax.nn.sigmoid(g)
    d_gate = (d_hidden * u * sigma * (1.0 + g * (1.0 - sigma))).astype(bf16)
    d_up = (d_hidden * g * sigma).astype(bf16)
    pair[:, 0:768] = d_gate
    pair[:, 768:1536] = d_up
    core_out[:, 2048:2816] = d_gate
    core_out[:, 2816:3584] = d_up
    total = jnp.sum(d_gate.astype(f32) * g + d_up.astype(f32) * u, axis=1, keepdims=True)
    products[...] = jnp.broadcast_to(total, (256, 128)).astype(bf16)


def backward(spot, pieces, w3, gate, up, inv):
    shapes = [((256, 1536), bf16), ((256, 128), bf16), ((256, 2048), bf16), ((256, 3584), bf16)]
    scratch = [pltpu.VMEM((256, 4096), bf16), pltpu.VMEM((256, 768), f32), pltpu.VMEM((8, 1, 512, 768), bf16),
               pltpu.SemaphoreType.DMA((8,))]
    return call(backward_body, "backward", shapes, scratch, 16, 2 * 256 * 4096 * 768, 8 * MiB, (spot, *pieces, w3, gate, up, inv),
                hbm=(6,), direct=range(1, 6))


def store(outs, k, value):
    half, i = k // 4, k % 4
    if i < 2:
        rows = value.shape[0]
        outs[half][i * rows:(i + 1) * rows, :] = value
    else:
        outs[2 * i - 2 + half][...] = value


def halving_shapes(rows, cols):
    return [((2 * rows, cols), bf16)] * 2 + [((rows, cols), bf16)] * 4


def outer_body(a_from, b_from, rows, cols, ready, order, *refs):
    n = len(a_from)
    a_refs, b_refs, outs = refs[:n], refs[n:2 * n], refs[2 * n:]
    ready()
    for k in range(8):
        total = None
        for a, a0, b, b0 in zip(a_refs, a_from, b_refs, b_from):
            b0 = k // 4 * cols + b0
            value = dot_tn(a[:, lane(order[k] * rows + a0, rows, 256)], b[:, b0:b0 + cols])
            total = value if total is None else total + value
        store(outs, k, total.astype(bf16))


def outer(name, order, a_list, b_list, rows, cols):
    body = functools.partial(outer_body, [f for _, f in a_list], [f for _, f in b_list], rows, cols)
    flops = 2 * 256 * len(a_list) * rows * 8 * cols
    return call(body, name, halving_shapes(rows, cols), [], 16, flops, 8 * MiB,
                (order, *[a for a, _ in a_list], *[b for b, _ in b_list]))


def branch_rows_body(ready, order, hidden, w, *refs):
    outs, held, sems = refs[:6], refs[6], refs[7]
    copies = fetch(w, held, sems, 2, 1, lambda k: k // 4 * 4 + order[k])
    ready()
    for k in range(8):
        copies[k].wait()
        store(outs, k, dot_nt(hidden[...], held[k, 0]).astype(bf16))


def branch_rows(order, hidden, w3):
    scratch = [pltpu.VMEM((8, 1, 512, 768), bf16), pltpu.SemaphoreType.DMA((8,))]
    return call(branch_rows_body, "branch_rows", halving_shapes(256, 512), scratch, 10, 2 * 256 * 768 * 4096, 8 * MiB,
                (order, hidden, w3), hbm=(2,))


def pair_rows_body(ready, order, pair, products, w, *refs):
    outs, held, sems = refs[:6], refs[6], refs[7]
    copies = fetch(w, held, sems, 0, 2, lambda k: k // 4 * 4 + order[k])
    ready()
    for k in range(8):
        copies[k].wait()
        value = dot_nt(pair[:, 0:768], held[k, 0]) + dot_nt(pair[:, 768:1536], held[k, 1])
        store(outs, k, jnp.concatenate([value.astype(bf16), products[...]], axis=1))


def pair_rows(order, pair, products, w3):
    scratch = [pltpu.VMEM((8, 2, 512, 768), bf16), pltpu.SemaphoreType.DMA((8,))]
    return call(pair_rows_body, "pair_rows", halving_shapes(256, 640), scratch, 16, 2 * 256 * 1536 * 4096, 16 * MiB,
                (order, pair, products, w3), hbm=(3,))


def second_step(terms, got, axis, done=()):
    rows = terms[2].shape[0]
    two, six, *got = lax.optimization_barrier((terms[2], terms[3], *got, *done))[:4]
    out = [(t.astype(f32) + g[rows:].astype(f32)).astype(bf16) for t, g in zip((two, six), got)]
    return out, [send(o, axis + move) for o, move in zip(out, ("^3", "^1"))]


def halve(terms, axis, done=()):
    got = [send(value, axis + move) for value, move in zip(terms[0:2], ("^1", "^3"))]
    return (got, *second_step(terms, got, axis, done))


def finish(terms, got, last, done=()):
    low, high = lax.optimization_barrier((terms[4], terms[5], *done))[:2]
    rows = terms[4].shape[0]
    return [t.astype(f32) + g[:rows].astype(f32) + e.astype(f32) for t, g, e in zip((low, high), got, last)]


def gather_both(own, cot):
    below, above, other = send(own, "y+"), send(own, "y-"), send(own, "z+2")
    up = send(rows_cat(below[:128], other), "y+")
    down = send(rows_cat(above[128:], other), "y-")
    cot_other = send(after(cot, other), "z+2")
    other_far = send(after(rows_cat(up[:128], down[:144]), cot_other), "z+2")
    both = after(rows_cat(cot, cot_other), up, down)
    cot_below, cot_above = send(both, "y+"), send(both, "y-")
    low = send(rows_cat(cot_below[:128], cot_below[256:384]), "y+")
    high = send(rows_cat(cot_above[128:256], cot_above[384:]), "y-")
    return (own, below, above, other, up, down, other_far), (both, cot_below, cot_above, low, high)


def local(inputs, gain, weights, d_out):
    width = weights.shape[0]
    t, s = lax.axis_index("tensor"), lax.axis_index("seq")
    z_hi, y = t // 4, t % 4
    x, z_lo, core = s // 4, s // 2 % 2, s % 2
    w3 = pltpu.with_memory_space_constraint(jnp.transpose(weights, (1, 0, 2)), pltpu.HBM)
    spot = jnp.stack(
        [(z_hi + dz) % 2 * 4 + (y + dy) % 4 for dz in (0, 1) for dy in range(4)] + [z_lo, core]
    ).astype(jnp.int32)

    def order(at):
        return jnp.stack([at ^ 1, at ^ 2, at ^ 3, at, at ^ 3, at ^ 2, at ^ 1, at]).astype(jnp.int32)

    own = rows_cat(inputs, jnp.broadcast_to(gain.reshape(1, 512), (16, 512)))
    x_pieces, cot_pieces = gather_both(own, d_out)
    x_full, gains, x_keep, x_core, x_same, x_cross = assemble(spot, x_pieces)
    x_same, x_cross = send(x_same, "z^3"), send(x_cross, "z^1")
    gate, up_val, hidden, inv, core_one = forward(after(x_full, *cot_pieces[1:3]), x_core, w3)
    core_one = send(core_one, "c")
    cot_pieces = (after(cot_pieces[0], x_same, x_cross), *cot_pieces[1:])
    d_pair, products, cot_mine, core_two = backward(spot, cot_pieces, w3, gate, up_val, inv)
    core_two = send(core_two, "c")
    pair_z = send(d_pair, "z^1")
    down_terms = outer("down_terms", order(x), [(cot_mine, 0), (core_two, 0)], [(hidden, 0), (core_one, 1024)], 512, 384)
    branch_terms = branch_rows(order(y), after(hidden, down_terms[0]), w3)
    branch_got = [send(value, move) for value, move in zip(branch_terms[0:2], ("y^1", "y^3"))]
    d_terms = pair_rows(order(y), after(d_pair, branch_terms[0]), products, w3)
    down_got, _, down_last = halve(down_terms, "x")
    d_terms = lax.optimization_barrier((*d_terms, *branch_got))[:6]
    d_got = [send(value, move) for value, move in zip(d_terms[0:2], ("y^1", "y^3"))]
    core_three = send(jnp.concatenate([x_cross, after(pair_z, d_terms[0], *down_got)], axis=1), "c")
    pair_terms = outer(
        "pair_terms", order(x), [(x_keep, 0), (x_same, 0), (core_one, 0), (core_three, 0)],
        [(d_pair, 0), (pair_z, 0), (core_two, 2048), (core_three, 1024)], 256, 768,
    )
    down_last = lax.optimization_barrier((*down_last, pair_terms[0]))[:2]
    pair_terms = lax.optimization_barrier((*pair_terms, *down_last))[:6]
    down = finish(down_terms, down_got, down_last, (pair_terms[0],))
    d_w_down = jnp.concatenate(down, axis=1)
    lower = z_lo == 0
    theirs = jnp.where(lower, d_w_down[256:], d_w_down[:256]).astype(bf16)
    down_z = send(theirs, "z^1")
    pair_got, pair_out, pair_last = halve(pair_terms, "x", (down_z,))
    d_w_gate, d_w_up = finish(pair_terms, pair_got, pair_last)
    d_w_down = jnp.where(lower, d_w_down[:256], d_w_down[256:]) + down_z.astype(f32)

    _, d_last = second_step(d_terms, d_got, "y", (pair_terms[0],))
    d_low, d_high = finish(d_terms, d_got, d_last)
    _, branch_last = second_step(branch_terms, branch_got, "y", (pair_terms[0], *d_last))
    low, high = finish(branch_terms, branch_got, branch_last)
    upper = z_hi == 1
    mine = jnp.where(upper, d_high, d_low)
    theirs = send(after(jnp.where(upper, d_low, d_high).astype(bf16), *pair_got), "z+2")
    mine = after(mine, *pair_got) + theirs.astype(f32)
    theirs = send(after(jnp.where(upper, low, high).astype(bf16), theirs), "z+2")
    branch = (jnp.where(upper, high, low) + theirs.astype(f32)).astype(bf16)
    d_normed, products = mine[:, :512], mine[:, 512:513] / width

    x_own = inputs.astype(f32)
    d_input = (d_normed * gain.astype(f32) - inv[:, :1] * products * x_own).astype(bf16)
    d_gain = jnp.sum(d_normed * x_own, axis=0, keepdims=True)
    for move in ("c", "z^1"):
        d_gain = d_gain + send(d_gain, move)
    d_gain = after(d_gain, *pair_last)
    beside, across, opposite = send(d_gain, "x^1"), send(d_gain, "x^3"), send(d_gain, "x+2")
    d_gain = (d_gain + beside) + (across + opposite)

    gain_rows = lax.dynamic_slice(gains, (0, s * 256), (1, 256)).astype(f32).reshape(256, 1)
    d_weights = jnp.stack(
        [(d_w_gate * gain_rows).astype(bf16), (d_w_up * gain_rows).astype(bf16), d_w_down.astype(bf16)], axis=1
    )
    return (branch, d_input, d_gain.reshape(512), d_weights)


def solution(mesh):
    in_specs = (P("seq", "tensor"), P("tensor"), P(None, None, "tensor"), P("seq", "tensor"))
    out_specs = (P("seq", "tensor"), P("seq", "tensor"), P("tensor"), P("seq", None, "tensor"))
    return jax.shard_map(local, mesh=mesh, in_specs=in_specs, out_specs=out_specs, check_vma=False)
```
